512 devices in a mesh: video: 4 (over z_lo), frame: 32 (over x, y), chan: 4 (over z_hi, core).
Axes of the slice: x: 4, y: 8, z: 8 (z_hi: 2, z_lo: 4; z = z_hi * 4 + z_lo), core: 2. Of those that a mesh axis runs over, the one named last changes fastest.
Arguments:
- latents: bfloat16 [128, 320, 3072], P(('video', 'frame'), 'chan'), parts along dimension 0, may hold values from -96 to 96
- time_weight1: bfloat16 [3, 320, 320], replicated, may hold values from -0.1875 to 0.1875
- norm_gain1: float32 [320], P('chan'), may hold values from 0.1 to 1.9
- norm_shift1: float32 [320], P('chan'), may hold values from -3 to 3
- down_weight: bfloat16 [9, 320, 320], P(None, 'chan'), may hold values from -0.109375 to 0.109375
- norm_gain2: float32 [320], replicated, may hold values from 0.1 to 1.9
- norm_shift2: float32 [320], replicated, may hold values from -3 to 3
- conv_weight2: bfloat16 [9, 320, 640], P(None, None, 'chan'), may hold values from -0.109375 to 0.109375
- skip_weight2: bfloat16 [320, 640], P(None, 'chan'), may hold values from -0.3125 to 0.3125
- time_bias2: float32 [640], P('chan'), may hold values from -4 to 4
- time_weight2: bfloat16 [3, 640, 640], replicated, may hold values from -0.125 to 0.125
- norm_gain3: float32 [640], P('chan'), may hold values from 0.1 to 1.9
- norm_shift3: float32 [640], P('chan'), may hold values from -3 to 3
Outputs:
- block_out: bfloat16 [128, 640, 768], P(('video', 'frame'), 'chan'), parts along dimension 0
The draws below stay inside these ranges and needn't reach their ends.
There are 4 independent parts, one for each index of `video`. The reference program is written for one: setup_inputs(seed, part) draws one part's arguments, and reference() takes and returns one part's arrays. A program takes and returns all parts, laid end to end along the dimension named above; an argument that names none is the same for every part. Nothing has to cross between parts.
All inputs are finite; a program needn't handle non-finite values.
Results may differ from the reference program's by a relative error of at most 0.013.
Values may be sent and summed in bfloat16 or wider, within the bound.
A program may use at most 128 MiB of HBM per device.

```python
import math
import jax
import jax.numpy as jnp
from jax import lax

C1 = 320
C2 = 640
GROUPS = 32
W1 = 128
H1 = 24
FRAMES = 32
H2 = 12
W2 = 64
P1 = 3072


def draw_latents(key, part):
    key = jax.random.fold_in(key, 17)
    key_noise, key_chan, key_cell, key_band, key_shift, key_frame = jax.random.split(key, 6)
    steps_frac = jnp.arange(FRAMES, dtype=jnp.float32) / max(FRAMES - 1, 1)
    noise = jnp.clip(jax.random.normal(key_noise, (FRAMES, C1, P1), jnp.float32), -4.0, 4.0)
    rising = jnp.exp(math.log(3.0) * steps_frac)
    frame_pos = jnp.arange(FRAMES)
    inner_frame = (frame_pos > 0) & (frame_pos < FRAMES - 1)
    frame_factor = jnp.exp(jax.random.uniform(key_frame, (FRAMES,), jnp.float32, math.log(0.6), math.log(1.6)))
    amplitude = rising * jnp.where(inner_frame, frame_factor, 1.0)
    chan_scale = jnp.exp(jax.random.uniform(key_chan, (C1,), jnp.float32, math.log(0.7), math.log(1.4)))
    cell_scale = jnp.exp(jax.random.uniform(key_cell, (P1,), jnp.float32, math.log(0.7), math.log(1.4)))
    band_index = jnp.arange(P1) // W1 * 6 // H1
    band_scale = jnp.exp(jax.random.uniform(key_band, (6,), jnp.float32, math.log(0.5), math.log(2.0)))
    band_shift = jnp.clip(0.5 * jax.random.normal(key_shift, (C1, 6), jnp.float32), -1.2, 1.2)
    scale_cells = cell_scale * band_scale[band_index]
    shift_cells = band_shift[:, band_index]
    values = (noise * scale_cells[None, None, :] + shift_cells[None, :, :]) * amplitude[:, None, None] * chan_scale[None, :, None]
    return values.astype(jnp.bfloat16)


def levels(key, shape, shards, low, top_value):
    gain, own = 1.0, jax.random.fold_in(key, 6)
    for position, parts in shards:
        heights = jnp.exp(jax.random.uniform(jax.random.fold_in(own, position), (parts,), jnp.float32, low / len(shards), top_value / len(shards)))
        gain = gain * jnp.repeat(heights, shape[position] // parts).reshape([-1 if axis == position else 1 for axis in range(len(shape))])
    return gain


def bell_draw(rng, dims, scale, most, cuts=(), held_as=jnp.bfloat16):
    values = scale * jax.random.normal(rng, dims, jnp.float32)
    if cuts:
        values = values * levels(rng, dims, cuts, -0.22, 0.18)
    return jnp.clip(values, -most, most).astype(held_as)


def setup_inputs(seed: int = 0, part: int = 0) -> dict:
    key_of = jax.random.split(jax.random.key(seed), 14)
    own_keys = jax.random.split(jax.random.fold_in(key_of[13], part), 14)
    latents = draw_latents(jax.random.fold_in(jax.random.fold_in(key_of[13], part), 71), part)
    time_weight1 = bell_draw(key_of[1], (3, C1, C1), (3 * C1) ** -0.5, 0.1875)
    norm_gain1 = jnp.clip(1.0 + 0.18 * jax.random.normal(key_of[2], (C1,), jnp.float32), 0.1, 1.9)
    norm_shift1 = bell_draw(key_of[3], (C1,), 0.5, 3.0, ((0, 4),), jnp.float32)
    down_weight = bell_draw(key_of[4], (9, C1, C1), (9 * C1) ** -0.5, 0.109375, ((1, 4),))
    norm_gain2 = jnp.clip(1.0 + 0.18 * jax.random.normal(key_of[5], (C1,), jnp.float32), 0.1, 1.9)
    norm_shift2 = bell_draw(key_of[6], (C1,), 0.5, 3.0, (), jnp.float32)
    conv_weight2 = bell_draw(key_of[7], (9, C1, C2), (9 * C1) ** -0.5, 0.109375, ((2, 4),))
    skip_weight2 = bell_draw(key_of[8], (C1, C2), C1 ** -0.5, 0.3125, ((1, 4),))
    time_bias2 = bell_draw(key_of[9], (C2,), 1.0, 4.0, ((0, 4),), jnp.float32)
    time_weight2 = bell_draw(key_of[10], (3, C2, C2), (3 * C2) ** -0.5, 0.125)
    norm_gain3 = jnp.clip(1.0 + 0.18 * jax.random.normal(key_of[11], (C2,), jnp.float32), 0.1, 1.9)
    norm_shift3 = bell_draw(key_of[12], (C2,), 0.5, 3.0, ((0, 4),), jnp.float32)
    return {"latents": latents, "time_weight1": time_weight1, "norm_gain1": norm_gain1, "norm_shift1": norm_shift1, "down_weight": down_weight, "norm_gain2": norm_gain2, "norm_shift2": norm_shift2, "conv_weight2": conv_weight2, "skip_weight2": skip_weight2, "time_bias2": time_bias2, "time_weight2": time_weight2, "norm_gain3": norm_gain3, "norm_shift3": norm_shift3}


epsilon = 1e-06

def norm_time(values, gain_vec, shift_vec):
    frames, channels, positions = values.shape
    grouped = values.reshape(frames, GROUPS, channels // GROUPS, positions)
    mean_val = lax.optimization_barrier(jnp.mean(grouped, axis=(0, 2, 3), keepdims=True))
    mean_sq = lax.optimization_barrier(jnp.mean(grouped * grouped, axis=(0, 2, 3), keepdims=True))
    scaled = (grouped - mean_val) * lax.rsqrt(mean_sq - mean_val * mean_val + epsilon)
    scaled = scaled.reshape(frames, channels, positions) * gain_vec[None, :, None] + shift_vec[None, :, None]
    return jax.nn.silu(scaled).astype(jnp.bfloat16)

def norm_space(values, gain_vec, shift_vec):
    frames, channels, positions = values.shape
    grouped = values.reshape(frames, GROUPS, channels // GROUPS, positions)
    mean_val = lax.optimization_barrier(jnp.mean(grouped, axis=(2, 3), keepdims=True))
    mean_sq = lax.optimization_barrier(jnp.mean(grouped * grouped, axis=(2, 3), keepdims=True))
    scaled = (grouped - mean_val) * lax.rsqrt(mean_sq - mean_val * mean_val + epsilon)
    scaled = scaled.reshape(frames, channels, positions) * gain_vec[None, :, None] + shift_vec[None, :, None]
    return jax.nn.silu(scaled).astype(jnp.bfloat16)

def conv_time(hidden, weight):
    frames = hidden.shape[0]
    padded = jnp.pad(hidden.astype(jnp.float32), ((1, 1), (0, 0), (0, 0)))
    widened = weight.astype(jnp.float32)
    summed = jnp.zeros((frames, weight.shape[2], hidden.shape[2]), jnp.float32)
    for tap_index in range(3):
        summed = summed + jnp.einsum('fcp,co->fop', padded[tap_index:tap_index + frames], widened[tap_index])
    return summed

def conv_grid(values, weight, height, breadth, stride):
    frames, channels, positions = values.shape
    grid_view = values.astype(jnp.float32).reshape(frames, channels, height, breadth)
    padded = jnp.pad(grid_view, ((0, 0), (0, 0), (1, 1), (1, 1)))
    out_rows = height // stride
    out_cols = breadth // stride
    widened = weight.astype(jnp.float32)
    summed = jnp.zeros((frames, weight.shape[2], out_rows * out_cols), jnp.float32)
    for row_off in range(3):
        for col_off in range(3):
            window = padded[:, :, row_off:row_off + stride * out_rows:stride, col_off:col_off + stride * out_cols:stride]
            window = window.reshape(frames, channels, out_rows * out_cols)
            summed = summed + jnp.einsum('fcp,co->fop', window, widened[3 * row_off + col_off])
    return summed

def reference(latents, time_weight1, norm_gain1, norm_shift1, down_weight, norm_gain2, norm_shift2, conv_weight2, skip_weight2, time_bias2, time_weight2, norm_gain3, norm_shift3):
    hidden_one = norm_time(latents.astype(jnp.float32), norm_gain1, norm_shift1)
    mixed_one = lax.optimization_barrier(conv_time(hidden_one, time_weight1).astype(jnp.bfloat16))
    block_one = (latents.astype(jnp.float32) + mixed_one.astype(jnp.float32)).astype(jnp.bfloat16)
    reduced = lax.optimization_barrier(conv_grid(block_one, down_weight, H1, W1, 2).astype(jnp.bfloat16))
    normed = norm_space(reduced.astype(jnp.float32), norm_gain2, norm_shift2)
    spatial = conv_grid(normed, conv_weight2, H2, W2, 1)
    spatial = spatial + jnp.einsum('fcp,co->fop', reduced.astype(jnp.float32), skip_weight2.astype(jnp.float32))
    spatial = (spatial + time_bias2[None, :, None]).astype(jnp.bfloat16)
    spatial = lax.optimization_barrier(spatial)
    hidden_two = norm_time(spatial.astype(jnp.float32), norm_gain3, norm_shift3)
    mixed_two = lax.optimization_barrier(conv_time(hidden_two, time_weight2).astype(jnp.bfloat16))
    return (spatial.astype(jnp.float32) + mixed_two.astype(jnp.float32)).astype(jnp.bfloat16)
```

```python
import functools

import jax
import jax.numpy as jnp
from jax import lax
from jax.experimental import pallas as pl
from jax.experimental.pallas import tpu as pltpu
from jax.sharding import PartitionSpec as P

MESH = pl.DeviceIdType.MESH
BF = jnp.bfloat16
F32 = jnp.float32
C1 = 320
C2 = 640
GROUPS = 32
W1 = 128
H1 = 24
H2 = 12
W2 = 64
NX = 4
EPS = 1e-6

Q1 = C1 // 4
Q2 = C2 // 4
HALF1 = H1 * W1 // 2
WIN1 = HALF1 + W1
HALF2 = H2 * W2 // 2
POS2 = H2 * W2
DPAD = 768
DPART = DPAD // NX
CHUNKS = ((0, 128), (128, 512), (640, 512), (1152, 512))

SCRATCH = {
    "lat_v": ((Q1, H1 * W1), BF),
    "tw1_v": ((3 * C1, C1), BF),
    "tw2_v": ((3 * C2, C2), BF),
    "cw2_v": ((9 * C1, Q2), BF),
    "sw2_v": ((C1, Q2), BF),
    "raw1": ((3, 2, Q1, WIN1), BF),
    "hid1": ((2, 3, 2, Q1, WIN1), BF),
    "tmp1": ((C1, 6 * Q1), BF),
    "w1t": ((2, 2 * Q1, 6 * Q1), BF),
    "blk": ((2 * Q1, WIN1), BF),
    "dwt": ((2, DPAD, C1), BF),
    "taps1": ((2, 9 * Q1, HALF2), BF),
    "part": ((C1, HALF2), F32),
    "part_rx": ((C1 // 2, HALF2), F32),
    "red": ((2, 2, C1 // 2, HALF2), BF),
    "nrm": ((C1, POS2 + 256), BF),
    "taps2": ((10 * C1, POS2), BF),
    "w2t": ((Q2, 10 * C1), BF),
    "spat": ((Q2, POS2), BF),
    "raw2": ((3, 2, Q2, HALF2), BF),
    "hid2": ((2, 3, 2, Q2, HALF2), BF),
    "tmp2": ((C2, 6 * Q2), BF),
    "w4t": ((2, 2 * Q2, 6 * Q2), BF),
    "fin": ((2, Q2, HALF2), BF),
    "fin_rx": ((Q2, HALF2), BF),
    "par": ((2, 8, 256), F32),
    "par2": ((8, 384), F32),
    "st_tx": ((6, 1, 128), F32),
    "st_rx": ((32, 1, 128), F32),
}
N_SEM = 96


def dot(a, b):
    return lax.dot_general(a, b, (((1,), (0,)), ((), ())), preferred_element_type=F32)


def silu(u):
    return u / (1.0 + jnp.exp(-u))


def to_columns(rows):
    return jnp.concatenate([rows] * (128 // rows.shape[0]), axis=0).T


def one_hots(chan, size):
    lane = lax.broadcasted_iota(jnp.int32, (chan.shape[0], 128), 1) * size
    off = GROUPS * size
    first = (lane <= chan) & (chan < lane + size)
    second = (lane - off <= chan) & (chan < lane - off + size)
    return first, second


def group_row(sums, squares, chan, size):
    first, second = one_hots(chan, size)
    spread = jnp.where(first, sums, 0.0) + jnp.where(second, squares, 0.0)
    return jnp.sum(spread, axis=0, keepdims=True)


def scale_columns(row, count, chan, size, gain, shift):
    first, second = one_hots(chan, size)
    mean = jnp.sum(jnp.where(first, row, 0.0), axis=1, keepdims=True) / count
    square = jnp.sum(jnp.where(second, row, 0.0), axis=1, keepdims=True) / count
    scale = lax.rsqrt(square - mean * mean + EPS) * gain
    return scale, shift - mean * scale


def kernel(frames, *refs):
    (lat, tw1, g1, s1, dw, g2, s2, cw2, sw2, tb, tw2, g3, s3, out) = refs[:14]
    names = list(SCRATCH)
    r = dict(zip(names, refs[14 : 14 + len(names)]))
    send_sem, recv_sem, local_sem = refs[14 + len(names) :]
    ny = frames // NX
    f = lax.axis_index("frame")
    c = lax.axis_index("chan")
    x, y = f // ny, lax.rem(f, ny)
    zh, k = c // 2, lax.rem(c, 2)
    oz, ok = 1 - zh, 1 - k
    zp = {"chan": lax.rem(c + 2, 4)}
    kp = {"chan": c + 1 - 2 * k}
    after = {"frame": lax.rem(f + 1, frames)}
    before = {"frame": lax.rem(f + frames - 1, frames)}
    chan_peers = [{"chan": lax.rem(c + d, 4)} for d in range(1, 4)]
    x_peers = [{"frame": lax.rem(x + d, NX) * ny + y} for d in range(1, NX)]
    y_peers = [{"frame": x * ny + lax.rem(y + d, ny)} for d in range(1, ny)]

    loads = {}
    for number, (name, ref, dst) in enumerate(
        (
            ("lat", lat, r["lat_v"]),
            ("dw", dw, r["dwt"].at[zh, pl.ds(0, 9 * Q1)]),
            ("tw1", tw1, r["tw1_v"]),
            ("cw2", cw2, r["cw2_v"]),
            ("sw2", sw2, r["sw2_v"]),
            ("tw2", tw2, r["tw2_v"]),
        )
    ):
        loads[name] = pltpu.make_async_copy(ref, dst, local_sem.at[number])
        loads[name].start()

    barrier = pltpu.get_barrier_semaphore()
    greeted = chan_peers + x_peers + y_peers + [after, before]
    for peer in greeted:
        pl.semaphore_signal(barrier, inc=1, device_id=peer, device_id_type=MESH)

    counter = [0]
    sent = []

    def send(src, dst, peer):
        number = counter[0]
        counter[0] += 1
        copy = pltpu.make_async_remote_copy(
            src_ref=src,
            dst_ref=dst,
            send_sem=send_sem.at[number],
            recv_sem=recv_sem.at[number],
            device_id=peer,
            device_id_type=MESH,
        )
        copy.start()
        sent.append(copy)
        return copy

    def lanes(start, size):
        return pl.ds(pl.multiple_of(start, 128), size)

    st_tx, st_rx = r["st_tx"], r["st_rx"]
    stat_slot = [0, 0]

    def stat_send(row, peers):
        tx, rx = stat_slot
        stat_slot[0] += 1
        stat_slot[1] += len(peers)
        st_tx[tx] = row
        return [send(st_tx.at[tx], st_rx.at[rx + i], p) for i, p in enumerate(peers)], tx, rx

    def stat_wait(state):
        copies, tx, rx = state
        total = st_tx[tx]
        for i, copy in enumerate(copies):
            copy.wait_recv()
            total = total + st_rx[rx + i]
        return total

    raw1, raw2 = r["raw1"], r["raw2"]
    lat_v = r["lat_v"]

    par = r["par"]
    par[zh, 0:1, 0:Q1] = g1[...]
    par[zh, 1:2, 0:Q1] = s1[...]
    par[zh, 2:3, 0:Q2] = g3[...]
    par[zh, 3:4, 0:Q2] = s3[...]
    par[zh, 4:5, 0:Q2] = tb[...]
    r["par2"][0:1, 0:C1] = g2[...]
    r["par2"][1:2, 0:C1] = s2[...]
    loads["lat"].wait()
    raw1[1, zh, :, 0:W1] = lat_v[:, HALF1 - W1 : HALF1]
    raw1[1, zh, :, W1:WIN1] = lat_v[:, lanes(zh * HALF1, HALF1)]
    pl.semaphore_wait(barrier, len(greeted))

    z_copies = []
    for start, size in CHUNKS:
        if start == 0:
            src = lat_v.at[:, pl.ds(HALF1 - W1, W1)]
        else:
            src = lat_v.at[:, lanes(oz * HALF1 + start - W1, size)]
        z_copies.append(send(src, raw1.at[1, zh, :, pl.ds(start, size)], zp))
    y_own = [
        send(raw1.at[1, zh], raw1.at[0, zh], after),
        send(raw1.at[1, zh], raw1.at[2, zh], before),
    ]
    par_copy = send(par.at[zh], par.at[zh], zp)

    wide = lat_v[...].astype(F32)
    row_iota = lax.broadcasted_iota(jnp.int32, (Q1, 1), 0)
    row1 = group_row(
        jnp.sum(wide, axis=1, keepdims=True),
        jnp.sum(wide * wide, axis=1, keepdims=True),
        row_iota + c * Q1,
        C1 // GROUPS,
    )
    state = stat_send(row1, chan_peers)

    dwt = r["dwt"]
    loads["dw"].wait()
    dwt[zh, 9 * Q1 : DPAD, :] = jnp.zeros((DPAD - 9 * Q1, C1), BF)
    own_part = pl.ds(pl.multiple_of(x * DPART, DPART), DPART)
    dw_z = send(dwt.at[zh, own_part], dwt.at[zh, own_part], zp)

    loads["tw1"].wait()
    tmp1, w1t = r["tmp1"], r["w1t"]
    for slot, core in ((0, k), (1, ok)):
        rows = [
            r["tw1_v"][pl.ds(pl.multiple_of(t * C1 + z * 2 * Q1 + core * Q1, 16), Q1), :]
            for t in range(3)
            for z in range(2)
        ]
        tmp1[...] = jnp.concatenate(rows, axis=0).T
        for z in range(2):
            w1t[slot, z * Q1 : (z + 1) * Q1, :] = tmp1[
                pl.ds(pl.multiple_of(z * 2 * Q1 + k * Q1, 16), Q1), :
            ]

    state = stat_send(stat_wait(state), x_peers)

    y_fwd = []

    def forward(index):
        start, size = CHUNKS[index]
        z_copies[index].wait_recv()
        here = raw1.at[1, oz, :, pl.ds(start, size)]
        y_fwd.append(send(here, raw1.at[0, oz, :, pl.ds(start, size)], after))
        y_fwd.append(send(here, raw1.at[2, oz, :, pl.ds(start, size)], before))

    forward(0)
    state = stat_send(stat_wait(state), y_peers)
    forward(1)
    w2t = r["w2t"]
    loads["cw2"].wait()
    loads["sw2"].wait()
    for t in range(9):
        w2t[:, t * C1 : (t + 1) * C1] = r["cw2_v"][t * C1 : (t + 1) * C1, :].T
    w2t[:, 9 * C1 : 10 * C1] = r["sw2_v"][...].T
    forward(2)
    tmp2, w4t = r["tmp2"], r["w4t"]
    loads["tw2"].wait()

    def prepare(slot, core):
        rows = [
            r["tw2_v"][pl.ds(pl.multiple_of(t * C2 + z * 2 * Q2 + core * Q2, 16), Q2), :]
            for t in range(3)
            for z in range(2)
        ]
        tmp2[...] = jnp.concatenate(rows, axis=0).T
        for z in range(2):
            w4t[slot, z * Q2 : (z + 1) * Q2, :] = tmp2[
                pl.ds(pl.multiple_of(z * 2 * Q2 + k * Q2, 16), Q2), :
            ]

    prepare(0, k)
    forward(3)
    prepare(1, ok)
    dw_z.wait_recv()
    other_part = dwt.at[oz, own_part]
    dw_x = [send(other_part, other_part, p) for p in x_peers]

    par_copy.wait_recv()
    cols = [to_columns(par[z]) for z in range(2)]
    total = stat_wait(state)
    row_iota = lax.broadcasted_iota(jnp.int32, (Q1, 1), 0)
    affine1 = [
        scale_columns(
            total,
            float(C1 // GROUPS * H1 * W1 * frames),
            row_iota + (2 * z + k) * Q1,
            C1 // GROUPS,
            cols[z][0:Q1, 0:1],
            cols[z][0:Q1, 1:2],
        )
        for z in range(2)
    ]
    hid1 = r["hid1"]
    alive = {0: f > 0, 2: f < frames - 1}

    def pick(pair, z):
        return [jnp.where(z == 0, pair[0][i], pair[1][i]) for i in range(2)]

    def hidden(raw, hid, tap, z, affine):
        scale, shift = pick(affine, z)
        value = silu(raw[tap, z].astype(F32) * scale + shift)
        if tap != 1:
            value = jnp.where(alive[tap], value, 0.0)
        hid[0, tap, z] = value.astype(BF)
        return send(hid.at[0, tap, z], hid.at[1, tap, z], kp)

    k_copies = [hidden(raw1, hid1, 1, zh, affine1)]
    for tap, copy in ((0, y_own[0]), (2, y_own[1])):
        copy.wait_recv()
        k_copies.append(hidden(raw1, hid1, tap, zh, affine1))
    k_copies.append(hidden(raw1, hid1, 1, oz, affine1))
    for tap in (0, 2):
        for copy in y_fwd[tap // 2 :: 2]:
            copy.wait_recv()
        k_copies.append(hidden(raw1, hid1, tap, oz, affine1))
    for copy in k_copies:
        copy.wait_recv()

    blk = r["blk"]
    for start, size in CHUNKS:
        span = slice(start, start + size)
        mixed = sum(
            dot(w1t[slot], hid1[slot, :, :, :, span].reshape(6 * Q1, size)) for slot in range(2)
        ).astype(BF)
        value = raw1[1, :, :, span].reshape(2 * Q1, size).astype(F32) + mixed.astype(F32)
        if start == 0:
            value = jnp.where(zh == 0, 0.0, value)
        blk[:, span] = value.astype(BF)

    src = lax.broadcasted_iota(jnp.int32, (256, 128), 0)
    dst = lax.broadcasted_iota(jnp.int32, (256, 128), 1)
    same = (src >= 128) == (dst >= 64)
    src_col = src - jnp.where(src >= 128, 128, 0)
    dst_col = dst - jnp.where(dst >= 64, 64, 0)
    taps1 = r["taps1"]
    picks = jnp.concatenate(
        [
            jnp.where(same & (src_col == 2 * dst_col + dx - 1), 1.0, 0.0).astype(BF)
            for dx in range(3)
        ],
        axis=1,
    )
    for dy in range(3):
        for j in range(HALF2 // 128):
            top = (4 * j + dy) * W1
            pair = jnp.concatenate(
                [blk[:, top : top + W1], blk[:, top + 2 * W1 : top + 3 * W1]], axis=1
            )
            got = dot(pair, picks).astype(BF)
            for dx in range(3):
                t = 3 * dy + dx
                for z in range(2):
                    taps1[z, t * Q1 : (t + 1) * Q1, j * 128 : (j + 1) * 128] = got[
                        z * Q1 : (z + 1) * Q1, dx * 128 : (dx + 1) * 128
                    ]
    for copy in dw_x:
        copy.wait_recv()
    part = r["part"]
    part[...] = sum(
        lax.dot_general(
            dwt[z, 0 : 9 * Q1, :],
            taps1[z],
            (((0,), (0,)), ((), ())),
            preferred_element_type=F32,
        )
        for z in range(2)
    )
    half = C1 // 2
    part_copy = send(
        part.at[pl.ds(pl.multiple_of(ok * half, 16), half)], r["part_rx"], kp
    )
    part_copy.wait_recv()
    red = r["red"]
    mine = part[pl.ds(pl.multiple_of(k * half, 16), half), :]
    red[k, zh] = (mine + r["part_rx"][...]).astype(BF)
    red_z = send(red.at[k, zh], red.at[k, zh], zp)
    red_k = send(red.at[k, zh], red.at[k, zh], kp)
    red_z.wait_recv()
    red_k2 = send(red.at[k, oz], red.at[k, oz], kp)
    red_k.wait_recv()
    red_k2.wait_recv()

    nrm, taps2 = r["nrm"], r["taps2"]
    nrm[:, 0:128] = jnp.zeros((C1, 128), BF)
    nrm[:, 128 + POS2 :] = jnp.zeros((C1, 128), BF)
    cols2 = to_columns(r["par2"][...])
    half_iota = lax.broadcasted_iota(jnp.int32, (half, 1), 0)
    for core in range(2):
        pieces = [red[core, z] for z in range(2)]
        wide = jnp.concatenate(pieces, axis=1).astype(F32)
        chan = half_iota + core * half
        row2 = group_row(
            jnp.sum(wide, axis=1, keepdims=True),
            jnp.sum(wide * wide, axis=1, keepdims=True),
            chan,
            C1 // GROUPS,
        )
        span = slice(core * half, (core + 1) * half)
        scale, shift = scale_columns(
            row2, float(C1 // GROUPS * POS2), chan, C1 // GROUPS, cols2[span, 0:1], cols2[span, 1:2]
        )
        nrm[span, 128 : 128 + POS2] = silu(wide * scale + shift).astype(BF)
        for z in range(2):
            taps2[9 * C1 + core * half : 9 * C1 + (core + 1) * half, z * HALF2 : (z + 1) * HALF2] = (
                pieces[z]
            )

    src = lax.broadcasted_iota(jnp.int32, (256, 256), 0)
    dst = lax.broadcasted_iota(jnp.int32, (256, 256), 1)
    second = dst >= 128
    lane = dst - jnp.where(second, 128, 0)
    upper = lane >= 64
    col = lane - jnp.where(upper, 64, 0)
    base = jnp.where(second, 128, 64) + jnp.where(upper, 64, 0)
    for dx in range(3):
        want = col + (dx - 1)
        keep = (want >= 0) & (want < W2) & (src == base + want)
        pick2 = jnp.where(keep, 1.0, 0.0).astype(BF)
        for j in range(POS2 // 128 + 1):
            got = dot(nrm[:, j * 128 : j * 128 + 256], pick2).astype(BF)
            if j < POS2 // 128:
                at = slice(j * 128, (j + 1) * 128)
                taps2[dx * C1 : (dx + 1) * C1, at] = got[:, 0:128]
                taps2[(3 + dx) * C1 : (4 + dx) * C1, at] = got[:, 128:256]
            if j > 0:
                at = slice((j - 1) * 128, j * 128)
                taps2[(6 + dx) * C1 : (7 + dx) * C1, at] = got[:, 0:128]
    spat = r["spat"]
    bias = jnp.where(zh == 0, cols[0][0:Q2, 4:5], cols[1][0:Q2, 4:5])
    for j in range(POS2 // 256):
        at = slice(j * 256, (j + 1) * 256)
        spat[:, at] = (dot(w2t[...], taps2[:, at]) + bias).astype(BF)

    raw2[1, zh] = spat[:, lanes(zh * HALF2, HALF2)]
    z2 = send(spat.at[:, lanes(oz * HALF2, HALF2)], raw2.at[1, zh], zp)
    y2_own = [
        send(raw2.at[1, zh], raw2.at[0, zh], after),
        send(raw2.at[1, zh], raw2.at[2, zh], before),
    ]
    wide = spat[...].astype(F32)
    row_iota = lax.broadcasted_iota(jnp.int32, (Q2, 1), 0)
    row3 = group_row(
        jnp.sum(wide, axis=1, keepdims=True),
        jnp.sum(wide * wide, axis=1, keepdims=True),
        row_iota + c * Q2,
        C2 // GROUPS,
    )
    state = stat_send(row3, chan_peers)
    state = stat_send(stat_wait(state), x_peers)
    z2.wait_recv()
    y2_fwd = [
        send(raw2.at[1, oz], raw2.at[0, oz], after),
        send(raw2.at[1, oz], raw2.at[2, oz], before),
    ]
    state = stat_send(stat_wait(state), y_peers)
    total = stat_wait(state)
    affine3 = [
        scale_columns(
            total,
            float(C2 // GROUPS * POS2 * frames),
            row_iota + (2 * z + k) * Q2,
            C2 // GROUPS,
            cols[z][0:Q2, 2:3],
            cols[z][0:Q2, 3:4],
        )
        for z in range(2)
    ]
    hid2 = r["hid2"]
    k2_copies = [hidden(raw2, hid2, 1, zh, affine3), hidden(raw2, hid2, 1, oz, affine3)]
    for z, copies in ((zh, y2_own), (oz, y2_fwd)):
        for tap in (0, 2):
            copies[tap // 2].wait_recv()
            k2_copies.append(hidden(raw2, hid2, tap, z, affine3))
    for copy in k2_copies:
        copy.wait_recv()
    fin = r["fin"]
    mixed = sum(
        dot(w4t[slot], hid2[slot].reshape(6 * Q2, HALF2)) for slot in range(2)
    ).astype(BF)
    value = raw2[1].reshape(2 * Q2, HALF2).astype(F32) + mixed.astype(F32)
    fin[...] = value.astype(BF).reshape(2, Q2, HALF2)
    last = send(fin.at[oz], r["fin_rx"], zp)
    out[:, lanes(zh * HALF2, HALF2)] = fin[zh]
    last.wait_recv()
    out[:, lanes(oz * HALF2, HALF2)] = r["fin_rx"][...]
    for copy in sent:
        copy.wait_send()


def per_device(frames, lat, tw1, g1, s1, dw, g2, s2, cw2, sw2, tb, tw2, g3, s3):
    vmem = pl.BlockSpec(memory_space=pltpu.VMEM)
    far = pl.BlockSpec(memory_space=pl.ANY)
    row = lambda v: v.reshape(1, v.shape[0])
    result = pl.pallas_call(
        functools.partial(kernel, frames),
        out_shape=jax.ShapeDtypeStruct((Q2, POS2), BF),
        in_specs=[far, far, vmem, vmem, far, vmem, vmem, far, far, vmem, far, vmem, vmem],
        out_specs=vmem,
        scratch_shapes=[pltpu.VMEM(shape, dtype) for shape, dtype in SCRATCH.values()]
        + [
            pltpu.SemaphoreType.DMA((N_SEM,)),
            pltpu.SemaphoreType.DMA((N_SEM,)),
            pltpu.SemaphoreType.DMA((8,)),
        ],
        compiler_params=pltpu.CompilerParams(
            collective_id=0, has_side_effects=True, vmem_limit_bytes=56 * 2**20
        ),
        name="video_block",
    )(
        lat.reshape(Q1, H1 * W1),
        tw1.reshape(3 * C1, C1),
        row(g1),
        row(s1),
        dw.reshape(9 * Q1, C1),
        row(g2),
        row(s2),
        cw2.reshape(9 * C1, Q2),
        sw2,
        row(tb),
        tw2.reshape(3 * C2, C2),
        row(g3),
        row(s3),
    )
    return result.reshape(1, Q2, POS2)


def solution(mesh):
    return jax.shard_map(
        functools.partial(per_device, mesh.shape["frame"]),
        mesh=mesh,
        in_specs=(
            P(("video", "frame"), "chan", None),
            P(),
            P("chan"),
            P("chan"),
            P(None, "chan", None),
            P(),
            P(),
            P(None, None, "chan"),
            P(None, "chan"),
            P("chan"),
            P(),
            P("chan"),
            P("chan"),
        ),
        out_specs=P(("video", "frame"), "chan", None),
        check_vma=False,
    )
```

```python
import functools

import jax
import jax.numpy as jnp
from jax import lax
from jax.experimental import pallas as pl
from jax.experimental.pallas import tpu as pltpu
from jax.sharding import PartitionSpec as P

MESH = pl.DeviceIdType.MESH
BF = jnp.bfloat16
F32 = jnp.float32
C1 = 320
C2 = 640
GROUPS = 32
W1 = 128
H1 = 24
H2 = 12
W2 = 64
NX = 4
EPS = 1e-6

Q1 = C1 // 4
Q2 = C2 // 4
HALF1 = H1 * W1 // 2
WIN1 = HALF1 + W1
HALF2 = H2 * W2 // 2
POS2 = H2 * W2
DPAD = 768
DPART = DPAD // NX
TILES = HALF2 // 128
CHUNKS = ((0, 640), (640, 512), (1152, 512))

SCRATCH = {
    "lat_v": ((Q1, H1 * W1), BF),
    "tw1_v": ((3 * C1, C1), BF),
    "tw2_v": ((3 * C2, C2), BF),
    "cw2_v": ((9 * Q2, C1), BF),
    "sw2_v": ((Q2, C1), BF),
    "zsrc": ((Q1, WIN1), BF),
    "raw1": ((3, 2, Q1, WIN1), BF),
    "hid1": ((2, 3, 2, Q1, WIN1), BF),
    "tmp1": ((C1, 6 * Q1), BF),
    "w1t": ((2, 2 * Q1, 6 * Q1), BF),
    "blk": ((2 * Q1, WIN1), BF),
    "dwt": ((2, DPAD, C1), BF),
    "taps1": ((2, 9 * Q1, HALF2), BF),
    "part": ((C1, HALF2), F32),
    "part_rx": ((C1 // 2, HALF2), F32),
    "red": ((2, 2, C1 // 2, HALF2), BF),
    "nrm": ((C1, POS2 + 256), BF),
    "taps2": ((10 * C1, POS2), BF),
    "w2t": ((Q2, 10 * C1), BF),
    "spat": ((Q2, POS2), BF),
    "raw2": ((3, 2, Q2, HALF2), BF),
    "hid2": ((2, 3, 2, Q2, HALF2), BF),
    "tmp2": ((C2, 6 * Q2), BF),
    "w4t": ((2, 2, Q2, 6 * Q2), BF),
    "pick1": ((256, 384), BF),
    "pick2": ((3, 256, 256), BF),
    "fin": ((Q2, HALF2), BF),
    "fin_rx": ((Q2, HALF2), BF),
    "par": ((2, 8, 256), F32),
    "par2": ((8, 384), F32),
    "st_tx": ((6, 1, 128), F32),
    "st_rx": ((32, 1, 128), F32),
}
N_SEM = 128


def dot(a, b):
    return lax.dot_general(a, b, (((1,), (0,)), ((), ())), preferred_element_type=F32)


def silu_of_half(w):
    return w + w * jnp.tanh(w)


def to_columns(rows):
    return jnp.concatenate([rows] * (128 // rows.shape[0]), axis=0).T


def one_hots(chan, size):
    lane = lax.broadcasted_iota(jnp.int32, (chan.shape[0], 128), 1) * size
    off = GROUPS * size
    first = (lane <= chan) & (chan < lane + size)
    second = (lane - off <= chan) & (chan < lane - off + size)
    return first, second


def group_row(sums, squares, chan, size):
    first, second = one_hots(chan, size)
    spread = jnp.where(first, sums, 0.0) + jnp.where(second, squares, 0.0)
    return jnp.sum(spread, axis=0, keepdims=True)


def scale_columns(row, count, chan, size, gain, shift):
    first, second = one_hots(chan, size)
    mean = jnp.sum(jnp.where(first, row, 0.0), axis=1, keepdims=True) / count
    square = jnp.sum(jnp.where(second, row, 0.0), axis=1, keepdims=True) / count
    scale = lax.rsqrt(square - mean * mean + EPS) * gain
    return 0.5 * scale, 0.5 * (shift - mean * scale)


class Done:
    def wait_recv(self):
        pass


def kernel(frames, *refs):
    (lat, tw1, g1, s1, dw, g2, s2, cw2, sw2, tb, tw2, g3, s3, out) = refs[:14]
    names = list(SCRATCH)
    r = dict(zip(names, refs[14 : 14 + len(names)]))
    send_sem, recv_sem, local_sem = refs[14 + len(names) :]
    ny = frames // NX
    f = lax.axis_index("frame")
    c = lax.axis_index("chan")
    x, y = f // ny, lax.rem(f, ny)
    zh, k = c // 2, lax.rem(c, 2)
    oz, ok = 1 - zh, 1 - k
    zp = {"chan": lax.rem(c + 2, 4)}
    kp = {"chan": c + 1 - 2 * k}
    after = {"frame": lax.rem(f + 1, frames)}
    before = {"frame": lax.rem(f + frames - 1, frames)}
    chan_peers = [{"chan": lax.rem(c + d, 4)} for d in range(1, 4)]
    x_peers = [{"frame": lax.rem(x + d, NX) * ny + y} for d in range(1, NX)]
    y_peers = [{"frame": x * ny + lax.rem(y + d, ny)} for d in range(1, ny)]

    loads = {}
    for number, (name, ref, dst) in enumerate(
        (
            ("lat", lat, r["lat_v"]),
            ("dw", dw, r["dwt"].at[zh, pl.ds(0, 9 * Q1)]),
            ("tw1", tw1, r["tw1_v"]),
            ("cw2", cw2, r["cw2_v"]),
            ("sw2", sw2, r["sw2_v"]),
            ("tw2", tw2, r["tw2_v"]),
        )
    ):
        loads[name] = pltpu.make_async_copy(ref, dst, local_sem.at[number])
        loads[name].start()

    barrier = pltpu.get_barrier_semaphore()
    greeted = chan_peers + x_peers + y_peers + [after, before]
    for peer in greeted:
        pl.semaphore_signal(barrier, inc=1, device_id=peer, device_id_type=MESH)

    counter = [0]
    sent = []

    def send(src, dst, peer):
        number = counter[0]
        counter[0] += 1
        copy = pltpu.make_async_remote_copy(
            src_ref=src,
            dst_ref=dst,
            send_sem=send_sem.at[number],
            recv_sem=recv_sem.at[number],
            device_id=peer,
            device_id_type=MESH,
        )
        copy.start()
        sent.append(copy)
        return copy

    def lanes(start, size):
        return pl.ds(pl.multiple_of(start, 128), size)

    st_tx, st_rx = r["st_tx"], r["st_rx"]
    stat_slot = [0, 0]

    def stat_send(row, peers):
        tx, rx = stat_slot
        stat_slot[0] += 1
        stat_slot[1] += len(peers)
        st_tx[tx] = row
        return [send(st_tx.at[tx], st_rx.at[rx + i], p) for i, p in enumerate(peers)], tx, rx

    def stat_wait(state):
        copies, tx, rx = state
        total = st_tx[tx]
        for i, copy in enumerate(copies):
            copy.wait_recv()
            total = total + st_rx[rx + i]
        return total

    raw1, raw2 = r["raw1"], r["raw2"]
    lat_v = r["lat_v"]

    par = r["par"]
    par[zh, 0:1, 0:Q1] = g1[...]
    par[zh, 1:2, 0:Q1] = s1[...]
    par[zh, 2:3, 0:Q2] = g3[...]
    par[zh, 3:4, 0:Q2] = s3[...]
    par[zh, 4:5, 0:Q2] = tb[...]
    r["par2"][0:1, 0:C1] = g2[...].reshape(1, C1)
    r["par2"][1:2, 0:C1] = s2[...].reshape(1, C1)
    loads["lat"].wait()
    zsrc = r["zsrc"]
    raw1[1, zh, :, 0:W1] = lat_v[:, HALF1 - W1 : HALF1]
    raw1[1, zh, :, W1:WIN1] = lat_v[:, lanes(zh * HALF1, HALF1)]
    zsrc[:, 0:W1] = lat_v[:, HALF1 - W1 : HALF1]
    zsrc[:, W1:WIN1] = lat_v[:, lanes(oz * HALF1, HALF1)]
    wide = lat_v[...].astype(F32)
    q1_iota = lax.broadcasted_iota(jnp.int32, (Q1, 1), 0)
    row1 = group_row(
        jnp.sum(wide, axis=1, keepdims=True),
        jnp.sum(wide * wide, axis=1, keepdims=True),
        q1_iota + c * Q1,
        C1 // GROUPS,
    )
    dwt = r["dwt"]
    loads["dw"].wait()
    dwt[zh, 9 * Q1 : DPAD, :] = jnp.zeros((DPAD - 9 * Q1, C1), BF)
    pl.semaphore_wait(barrier, len(greeted))

    state = stat_send(row1, chan_peers)
    pieces = ny // 2
    piece = DPART // pieces
    own_piece = pl.ds(pl.multiple_of(x * DPART + (y // 2) * piece, 16), piece)
    own_part = pl.ds(pl.multiple_of(x * DPART, 16), DPART)
    dw_z = send(dwt.at[zh, own_piece], dwt.at[zh, own_piece], zp)

    z_copies = [
        send(zsrc.at[:, pl.ds(a, n)], raw1.at[1, zh, :, pl.ds(a, n)], zp) for a, n in CHUNKS
    ]

    def to_frames(raw, z, a, n):
        here = raw.at[1, z, :, pl.ds(a, n)]
        return [
            send(here, raw.at[0, z, :, pl.ds(a, n)], after),
            send(here, raw.at[2, z, :, pl.ds(a, n)], before),
        ]

    y_own = [to_frames(raw1, zh, a, n) for a, n in CHUNKS]
    par_copy = send(par.at[zh], par.at[zh], zp)

    def prepare(weight, held, store, width, count, slot, core):
        rows = [
            weight[pl.ds(pl.multiple_of(t * width + z * 2 * count + core * count, 16), count), :]
            for t in range(3)
            for z in range(2)
        ]
        held[...] = jnp.concatenate(rows, axis=0).T
        for z in range(2):
            store(slot, z, held[pl.ds(pl.multiple_of(z * 2 * count + k * count, 16), count), :])

    w1t, w4t, w2t = r["w1t"], r["w4t"], r["w2t"]

    def store1(slot, z, value):
        w1t[slot, z * Q1 : (z + 1) * Q1, :] = value

    def store4(slot, z, value):
        w4t[slot, z] = value

    loads["tw1"].wait()
    for slot, core in ((0, k), (1, ok)):
        prepare(r["tw1_v"], r["tmp1"], store1, C1, Q1, slot, core)

    src = lax.broadcasted_iota(jnp.int32, (256, 128), 0)
    dst = lax.broadcasted_iota(jnp.int32, (256, 128), 1)
    same = (src >= 128) == (dst >= 64)
    src_col = src - jnp.where(src >= 128, 128, 0)
    dst_col = dst - jnp.where(dst >= 64, 64, 0)
    for dx in range(3):
        r["pick1"][:, dx * 128 : (dx + 1) * 128] = jnp.where(
            same & (src_col == 2 * dst_col + dx - 1), 1.0, 0.0
        ).astype(BF)

    state = stat_send(stat_wait(state), x_peers)
    dw_z.wait_recv()
    here = dwt.at[oz, own_piece]
    dw_y = [
        send(here, here, {"frame": x * ny + lax.rem(y + 2 * d, ny)}) for d in range(1, pieces)
    ]

    src = lax.broadcasted_iota(jnp.int32, (256, 256), 0)
    dst = lax.broadcasted_iota(jnp.int32, (256, 256), 1)
    second = dst >= 128
    lane = dst - jnp.where(second, 128, 0)
    upper = lane >= 64
    col = lane - jnp.where(upper, 64, 0)
    base = jnp.where(second, 128, 64) + jnp.where(upper, 64, 0)
    for dx in range(3):
        want = col + (dx - 1)
        keep = (want >= 0) & (want < W2) & (src == base + want)
        r["pick2"][dx] = jnp.where(keep, 1.0, 0.0).astype(BF)
    loads["cw2"].wait()
    loads["sw2"].wait()
    for t in range(9):
        w2t[:, t * C1 : (t + 1) * C1] = r["cw2_v"][t * Q2 : (t + 1) * Q2, :]
    w2t[:, 9 * C1 : 10 * C1] = r["sw2_v"][...]
    state = stat_send(stat_wait(state), y_peers)
    y_fwd = []

    def forward(i):
        z_copies[i].wait_recv()
        y_fwd.append(to_frames(raw1, oz, *CHUNKS[i]))

    forward(0)
    loads["tw2"].wait()
    for slot, core in ((0, k), (1, ok)):
        prepare(r["tw2_v"], r["tmp2"], store4, C2, Q2, slot, core)
    par_copy.wait_recv()
    cols = [to_columns(par[z]) for z in range(2)]
    cols2 = to_columns(r["par2"][...])
    bias = jnp.where(zh == 0, cols[0][0:Q2, 4:5], cols[1][0:Q2, 4:5])
    total = stat_wait(state)
    affine1 = [
        scale_columns(
            total,
            float(C1 // GROUPS * H1 * W1 * frames),
            q1_iota + (2 * z + k) * Q1,
            C1 // GROUPS,
            cols[z][0:Q1, 0:1],
            cols[z][0:Q1, 1:2],
        )
        for z in range(2)
    ]
    for copy in dw_y:
        copy.wait_recv()
    other_part = dwt.at[oz, own_part]
    dw_x = [send(other_part, other_part, p) for p in x_peers]
    forward(1)
    hid1 = r["hid1"]
    alive = {0: f > 0, 2: f < frames - 1}

    def pick(pair, z):
        return [jnp.where(z == 0, pair[0][i], pair[1][i]) for i in range(2)]

    def hidden(raw, hid, z, affine, a, n, waits):
        span = slice(a, a + n)
        scale, shift = pick(affine, z)
        for tap in (1, 0, 2):
            if tap != 1:
                waits[tap // 2].wait_recv()
            value = silu_of_half(raw[tap, z, :, span].astype(F32) * scale + shift)
            if tap != 1:
                value = jnp.where(alive[tap], value, 0.0)
            hid[0, tap, z, :, span] = value.astype(BF)
        return send(hid.at[0, :, z, :, pl.ds(a, n)], hid.at[1, :, z, :, pl.ds(a, n)], kp)

    blk, taps1 = r["blk"], r["taps1"]
    part, part_rx, red = r["part"], r["part_rx"], r["red"]
    half = C1 // 2
    k1, part_k, red_z, red_k = {}, {}, {}, {}

    def hid_own(i):
        k1[i] = [hidden(raw1, hid1, zh, affine1, *CHUNKS[i], y_own[i])]

    def hid_other(i):
        k1[i].append(hidden(raw1, hid1, oz, affine1, *CHUNKS[i], y_fwd[i]))

    def first_conv(i):
        a, n = CHUNKS[i]
        span = slice(a, a + n)
        for copy in k1[i]:
            copy.wait_recv()
        mixed = sum(
            dot(w1t[slot], hid1[slot, :, :, :, span].reshape(6 * Q1, n)) for slot in range(2)
        ).astype(BF)
        value = raw1[1, :, :, span].reshape(2 * Q1, n).astype(F32) + mixed.astype(F32)
        if i == 0:
            blk[:, 0:W1] = jnp.where(zh == 0, 0.0, value[:, 0:W1]).astype(BF)
            blk[:, W1:n] = value[:, W1:].astype(BF)
        else:
            blk[:, span] = value.astype(BF)
        at = slice(i * 128, (i + 1) * 128)
        for dy in range(3):
            top = (4 * i + dy) * W1
            pair = jnp.concatenate(
                [blk[:, top : top + W1], blk[:, top + 2 * W1 : top + 3 * W1]], axis=1
            )
            got = dot(pair, r["pick1"][...]).astype(BF)
            for dx in range(3):
                t = 3 * dy + dx
                for z in range(2):
                    taps1[z, t * Q1 : (t + 1) * Q1, at] = got[
                        z * Q1 : (z + 1) * Q1, dx * 128 : (dx + 1) * 128
                    ]

    def down(i):
        at = slice(i * 128, (i + 1) * 128)
        part[:, at] = sum(
            lax.dot_general(
                dwt[z, 0 : 9 * Q1, :],
                taps1[z, :, at],
                (((0,), (0,)), ((), ())),
                preferred_element_type=F32,
            )
            for z in range(2)
        )
        part_k[i] = send(
            part.at[pl.ds(pl.multiple_of(ok * half, 16), half), pl.ds(i * 128, 128)],
            part_rx.at[:, pl.ds(i * 128, 128)],
            kp,
        )

    def reduced(i):
        at = slice(i * 128, (i + 1) * 128)
        part_k[i].wait_recv()
        mine = part[pl.ds(pl.multiple_of(k * half, 16), half), at]
        red[k, zh, :, at] = (mine + part_rx[:, at]).astype(BF)
        here = red.at[k, zh, :, pl.ds(i * 128, 128)]
        red_z[i] = send(here, here, zp)
        red_k[i] = [send(here, here, kp)]

    def pass_reduced(i):
        red_z[i].wait_recv()
        here = red.at[k, oz, :, pl.ds(i * 128, 128)]
        red_k[i].append(send(here, here, kp))

    hid_own(0)
    hid_other(0)
    hid_own(1)
    hid_other(1)
    first_conv(0)
    forward(2)
    first_conv(1)
    hid_own(2)
    for copy in dw_x:
        copy.wait_recv()
    down(0)
    down(1)
    hid_other(2)
    reduced(0)
    reduced(1)
    first_conv(2)
    down(2)
    reduced(2)
    for i in range(3):
        pass_reduced(i)
    for i in range(3):
        for copy in red_k[i]:
            copy.wait_recv()

    nrm, taps2 = r["nrm"], r["taps2"]
    nrm[:, 0:128] = jnp.zeros((C1, 128), BF)
    nrm[:, 128 + POS2 :] = jnp.zeros((C1, 128), BF)
    half_iota = lax.broadcasted_iota(jnp.int32, (half, 1), 0)
    for core in range(2):
        sides = [red[core, z] for z in range(2)]
        wide = jnp.concatenate(sides, axis=1).astype(F32)
        chan = half_iota + core * half
        row2 = group_row(
            jnp.sum(wide, axis=1, keepdims=True),
            jnp.sum(wide * wide, axis=1, keepdims=True),
            chan,
            C1 // GROUPS,
        )
        span = slice(core * half, (core + 1) * half)
        scale, shift = scale_columns(
            row2, float(C1 // GROUPS * POS2), chan, C1 // GROUPS, cols2[span, 0:1], cols2[span, 1:2]
        )
        nrm[span, 128 : 128 + POS2] = silu_of_half(wide * scale + shift).astype(BF)
        for z in range(2):
            taps2[9 * C1 + core * half : 9 * C1 + (core + 1) * half, z * HALF2 : (z + 1) * HALF2] = (
                sides[z]
            )

    for dx in range(3):
        for j in range(POS2 // 128 + 1):
            got = dot(nrm[:, j * 128 : j * 128 + 256], r["pick2"][dx]).astype(BF)
            if j < POS2 // 128:
                at = slice(j * 128, (j + 1) * 128)
                taps2[dx * C1 : (dx + 1) * C1, at] = got[:, 0:128]
                taps2[(3 + dx) * C1 : (4 + dx) * C1, at] = got[:, 128:256]
            if j > 0:
                at = slice((j - 1) * 128, j * 128)
                taps2[(6 + dx) * C1 : (7 + dx) * C1, at] = got[:, 0:128]

    spat = r["spat"]
    z2 = []
    for i in range(TILES):
        at = lanes(oz * HALF2 + i * 128, 128)
        spat[:, at] = (dot(w2t[...], taps2[:, at]) + bias).astype(BF)
        z2.append(send(spat.at[:, at], raw2.at[1, zh, :, pl.ds(i * 128, 128)], zp))
    at = lanes(zh * HALF2, HALF2)
    mine = (dot(w2t[...], taps2[:, at]) + bias).astype(BF)
    spat[:, at] = mine
    raw2[1, zh] = mine
    y2_own = to_frames(raw2, zh, 0, HALF2)
    wide = spat[...].astype(F32)
    q2_iota = lax.broadcasted_iota(jnp.int32, (Q2, 1), 0)
    row3 = group_row(
        jnp.sum(wide, axis=1, keepdims=True),
        jnp.sum(wide * wide, axis=1, keepdims=True),
        q2_iota + c * Q2,
        C2 // GROUPS,
    )
    state = stat_send(row3, x_peers)
    y2_fwd = []

    def forward2(i):
        z2[i].wait_recv()
        y2_fwd.append(to_frames(raw2, oz, i * 128, 128))

    state = stat_send(stat_wait(state), y_peers)
    forward2(0)
    state = stat_send(stat_wait(state), chan_peers)
    forward2(1)
    forward2(2)
    total = stat_wait(state)
    affine3 = [
        scale_columns(
            total,
            float(C2 // GROUPS * POS2 * frames),
            q2_iota + (2 * z + k) * Q2,
            C2 // GROUPS,
            cols[z][0:Q2, 2:3],
            cols[z][0:Q2, 3:4],
        )
        for z in range(2)
    ]
    hid2 = r["hid2"]
    k2 = []
    for i in range(TILES):
        k2.append([hidden(raw2, hid2, zh, affine3, i * 128, 128, y2_own if i == 0 else [Done()] * 2)])
        k2[i].append(hidden(raw2, hid2, oz, affine3, i * 128, 128, y2_fwd[i]))

    fin, fin_rx = r["fin"], r["fin_rx"]

    def second_conv(z, at, n):
        mixed = sum(
            dot(w4t[slot, z], hid2[slot, :, :, :, at].reshape(6 * Q2, n)) for slot in range(2)
        ).astype(BF)
        return (raw2[1, z, :, at].astype(F32) + mixed.astype(F32)).astype(BF)

    last = []
    for i in range(TILES):
        for copy in k2[i]:
            copy.wait_recv()
        at = slice(i * 128, (i + 1) * 128)
        fin[:, at] = second_conv(oz, at, 128)
        last.append(send(fin.at[:, pl.ds(i * 128, 128)], fin_rx.at[:, pl.ds(i * 128, 128)], zp))
    out[:, lanes(zh * HALF2, HALF2)] = second_conv(zh, slice(0, HALF2), HALF2)
    for copy in last:
        copy.wait_recv()
    out[:, lanes(oz * HALF2, HALF2)] = fin_rx[...]
    for copy in sent:
        copy.wait_send()


def per_device(frames, lat, tw1, g1, s1, dw, g2, s2, cw2, sw2, tb, tw2, g3, s3):
    vmem = pl.BlockSpec(memory_space=pltpu.VMEM)
    far = pl.BlockSpec(memory_space=pl.ANY)
    row = lambda v: v.reshape(1, v.shape[0])
    result = pl.pallas_call(
        functools.partial(kernel, frames),
        out_shape=jax.ShapeDtypeStruct((Q2, POS2), BF),
        in_specs=[far, far, vmem, vmem, far, vmem, vmem, far, far, vmem, far, vmem, vmem],
        out_specs=vmem,
        scratch_shapes=[pltpu.VMEM(shape, dtype) for shape, dtype in SCRATCH.values()]
        + [
            pltpu.SemaphoreType.DMA((N_SEM,)),
            pltpu.SemaphoreType.DMA((N_SEM,)),
            pltpu.SemaphoreType.DMA((8,)),
        ],
        compiler_params=pltpu.CompilerParams(
            collective_id=0, has_side_effects=True, vmem_limit_bytes=56 * 2**20
        ),
        name="video_block",
    )(
        lat.reshape(Q1, H1 * W1),
        tw1.reshape(3 * C1, C1),
        row(g1),
        row(s1),
        dw.reshape(9 * Q1, C1),
        g2,
        s2,
        cw2.transpose(0, 2, 1).reshape(9 * Q2, C1),
        sw2.T,
        row(tb),
        tw2.reshape(3 * C2, C2),
        row(g3),
        row(s3),
    )
    return result.reshape(1, Q2, POS2)


def solution(mesh):
    return jax.shard_map(
        functools.partial(per_device, mesh.shape["frame"]),
        mesh=mesh,
        in_specs=(
            P(("video", "frame"), "chan", None),
            P(),
            P("chan"),
            P("chan"),
            P(None, "chan", None),
            P(),
            P(),
            P(None, None, "chan"),
            P(None, "chan"),
            P("chan"),
            P(),
            P("chan"),
            P("chan"),
        ),
        out_specs=P(("video", "frame"), "chan", None),
        check_vma=False,
    )
```

```python
import functools

import jax
import jax.numpy as jnp
from jax import lax
from jax.experimental import pallas as pl
from jax.experimental.pallas import tpu as pltpu
from jax.sharding import PartitionSpec as P

MESH = pl.DeviceIdType.MESH
BF = jnp.bfloat16
F32 = jnp.float32
C1 = 320
C2 = 640
GROUPS = 32
W1 = 128
H1 = 24
H2 = 12
W2 = 64
NX = 4
EPS = 1e-6

Q1 = C1 // 4
Q2 = C2 // 4
HALF1 = H1 * W1 // 2
WIN1 = HALF1 + W1
HALF2 = H2 * W2 // 2
POS2 = H2 * W2
DPAD = 768
DPART = DPAD // NX
TILES = HALF2 // 128
CHUNKS = ((0, 640), (640, 512), (1152, 512))

SCRATCH = {
    "lat_v": ((Q1, H1 * W1), BF),
    "tw1_v": ((3 * C1, C1), BF),
    "tw2_v": ((3 * C2, C2), BF),
    "cw2_v": ((9 * Q2, C1), BF),
    "sw2_v": ((Q2, C1), BF),
    "zsrc": ((Q1, WIN1), BF),
    "raw1": ((3, 2, Q1, WIN1), BF),
    "hid1": ((2, 3, 2, Q1, WIN1), BF),
    "tmp1": ((C1, 6 * Q1), BF),
    "w1t": ((2, 2 * Q1, 6 * Q1), BF),
    "blk": ((2 * Q1, WIN1), BF),
    "dwt": ((2, DPAD, C1), BF),
    "taps1": ((2, 9 * Q1, HALF2), BF),
    "part": ((C1, HALF2), F32),
    "part_rx": ((C1 // 2, HALF2), F32),
    "red": ((2, 2, C1 // 2, HALF2), BF),
    "nrm": ((C1, POS2 + 256), BF),
    "taps2": ((10 * C1, HALF2), BF),
    "taps2o": ((10 * C1, HALF2), BF),
    "w2t": ((Q2, 10 * C1), BF),
    "spat_o": ((Q2, HALF2), BF),
    "raw2": ((2, 3, 2, Q2, HALF2), BF),
    "hid2": ((2, 3, 2, Q2, HALF2), BF),
    "tmp2": ((C2, 6 * Q2), BF),
    "w4t": ((2, 2, Q2, 6 * Q2), BF),
    "pick1": ((256, 384), BF),
    "pick2": ((3, 256, 256), BF),
    "fin": ((2, Q2, HALF2), BF),
    "par": ((2, 2, 8, 256), F32),
    "par2": ((8, 384), F32),
    "g1_v": ((1, Q1), F32),
    "s1_v": ((1, Q1), F32),
    "g2_v": ((C1,), F32),
    "s2_v": ((C1,), F32),
    "g3_v": ((1, Q2), F32),
    "s3_v": ((1, Q2), F32),
    "tb_v": ((1, Q2), F32),
    "st_tx": ((6, 1, 128), F32),
    "st_rx": ((32, 1, 128), F32),
}
N_SEM = 128


def dot(a, b):
    return lax.dot_general(a, b, (((1,), (0,)), ((), ())), preferred_element_type=F32)


def silu_of_half(w):
    return w + w * jnp.tanh(w)


def to_columns(rows):
    return jnp.concatenate([rows] * (128 // rows.shape[0]), axis=0).T


def one_hots(chan, size):
    lane = lax.broadcasted_iota(jnp.int32, (chan.shape[0], 128), 1) * size
    off = GROUPS * size
    first = (lane <= chan) & (chan < lane + size)
    second = (lane - off <= chan) & (chan < lane - off + size)
    return first, second


def group_row(sums, squares, chan, size):
    first, second = one_hots(chan, size)
    spread = jnp.where(first, sums, 0.0) + jnp.where(second, squares, 0.0)
    return jnp.sum(spread, axis=0, keepdims=True)


def scale_columns(row, count, chan, size, gain, shift):
    first, second = one_hots(chan, size)
    mean = jnp.sum(jnp.where(first, row, 0.0), axis=1, keepdims=True) / count
    square = jnp.sum(jnp.where(second, row, 0.0), axis=1, keepdims=True) / count
    scale = lax.rsqrt(square - mean * mean + EPS) * gain
    return 0.5 * scale, 0.5 * (shift - mean * scale)


def kernel(frames, *refs):
    (lat, tw1, g1, s1, dw, g2, s2, cw2, sw2, tb, tw2, g3, s3, out) = refs[:14]
    names = list(SCRATCH)
    r = dict(zip(names, refs[14 : 14 + len(names)]))
    send_sem, recv_sem, local_sem = refs[14 + len(names) :]
    ny = frames // NX
    f = lax.axis_index("frame")
    c = lax.axis_index("chan")
    x, y = f // ny, lax.rem(f, ny)
    zh, k = c // 2, lax.rem(c, 2)
    oz, ok = 1 - zh, 1 - k
    zp = {"chan": lax.rem(c + 2, 4)}
    kp = {"chan": c + 1 - 2 * k}
    after = {"frame": lax.rem(f + 1, frames)}
    before = {"frame": lax.rem(f + frames - 1, frames)}
    chan_peers = [{"chan": lax.rem(c + d, 4)} for d in range(1, 4)]
    x_peers = [{"frame": lax.rem(x + d, NX) * ny + y} for d in range(1, NX)]
    y_peers = [{"frame": x * ny + lax.rem(y + d, ny)} for d in range(1, ny)]

    barrier = pltpu.get_barrier_semaphore()
    greeted = chan_peers + x_peers + y_peers + [after, before]
    for peer in greeted:
        pl.semaphore_signal(barrier, inc=1, device_id=peer, device_id_type=MESH)

    loads = {}
    for number, (name, ref, dst) in enumerate(
        (
            ("lat", lat, r["lat_v"]),
            ("dw", dw, r["dwt"].at[zh, pl.ds(0, 9 * Q1)]),
            ("g1", g1, r["g1_v"]),
            ("s1", s1, r["s1_v"]),
            ("g2", g2, r["g2_v"]),
            ("s2", s2, r["s2_v"]),
            ("g3", g3, r["g3_v"]),
            ("s3", s3, r["s3_v"]),
            ("tb", tb, r["tb_v"]),
            ("tw1", tw1, r["tw1_v"]),
            ("cw2", cw2, r["cw2_v"]),
            ("sw2", sw2, r["sw2_v"]),
            ("tw2", tw2, r["tw2_v"]),
        )
    ):
        loads[name] = pltpu.make_async_copy(ref, dst, local_sem.at[number])
        loads[name].start()

    counter = [0]
    sent = []

    def send(src, dst, peer):
        number = counter[0]
        counter[0] += 1
        copy = pltpu.make_async_remote_copy(
            src_ref=src,
            dst_ref=dst,
            send_sem=send_sem.at[number],
            recv_sem=recv_sem.at[number],
            device_id=peer,
            device_id_type=MESH,
        )
        copy.start()
        sent.append(copy)
        return copy

    def lanes(start, size):
        return pl.ds(pl.multiple_of(start, 128), size)

    st_tx, st_rx = r["st_tx"], r["st_rx"]
    stat_slot = [0, 0]

    def stat_send(row, peers):
        tx, rx = stat_slot
        stat_slot[0] += 1
        stat_slot[1] += len(peers)
        st_tx[tx] = row
        return [send(st_tx.at[tx], st_rx.at[rx + i], p) for i, p in enumerate(peers)], tx, rx

    def stat_wait(state):
        copies, tx, rx = state
        total = st_tx[tx]
        for i, copy in enumerate(copies):
            copy.wait_recv()
            total = total + st_rx[rx + i]
        return total

    raw1, raw2 = r["raw1"], r["raw2"]
    lat_v = r["lat_v"]

    par = r["par"]
    loads["lat"].wait()
    zsrc = r["zsrc"]
    raw1[1, zh, :, 0:W1] = lat_v[:, HALF1 - W1 : HALF1]
    raw1[1, zh, :, W1:WIN1] = lat_v[:, lanes(zh * HALF1, HALF1)]
    zsrc[:, 0:W1] = lat_v[:, HALF1 - W1 : HALF1]
    zsrc[:, W1:WIN1] = lat_v[:, lanes(oz * HALF1, HALF1)]
    wide = lat_v[...].astype(F32)
    q1_iota = lax.broadcasted_iota(jnp.int32, (Q1, 1), 0)
    row1 = group_row(
        jnp.sum(wide, axis=1, keepdims=True),
        jnp.sum(wide * wide, axis=1, keepdims=True),
        q1_iota + c * Q1,
        C1 // GROUPS,
    )
    dwt = r["dwt"]
    for name in ("dw", "g1", "s1", "g2", "s2", "g3", "s3", "tb"):
        loads[name].wait()
    par[0, zh, 0:1, 0:Q1] = r["g1_v"][...]
    par[0, zh, 1:2, 0:Q1] = r["s1_v"][...]
    par[0, zh, 2:3, 0:Q2] = r["g3_v"][...]
    par[0, zh, 3:4, 0:Q2] = r["s3_v"][...]
    par[0, zh, 4:5, 0:Q2] = r["tb_v"][...]
    r["par2"][0:1, 0:C1] = r["g2_v"][...].reshape(1, C1)
    r["par2"][1:2, 0:C1] = r["s2_v"][...].reshape(1, C1)
    dwt[zh, 9 * Q1 : DPAD, :] = jnp.zeros((DPAD - 9 * Q1, C1), BF)
    pl.semaphore_wait(barrier, len(greeted))

    state = stat_send(row1, chan_peers)
    pieces = ny // 2
    piece = DPART // pieces
    own_piece = pl.ds(pl.multiple_of(x * DPART + (y // 2) * piece, 16), piece)
    dw_z = send(dwt.at[zh, own_piece], dwt.at[zh, own_piece], zp)

    z_copies = [
        send(zsrc.at[:, pl.ds(a, n)], raw1.at[1, zh, :, pl.ds(a, n)], zp) for a, n in CHUNKS
    ]

    def to_frames(raw, z, a, n):
        here = raw.at[1, z, :, pl.ds(a, n)]
        return [
            send(here, raw.at[0, z, :, pl.ds(a, n)], after),
            send(here, raw.at[2, z, :, pl.ds(a, n)], before),
        ]

    y_own = [to_frames(raw1, zh, a, n) for a, n in CHUNKS]
    par_copy = send(par.at[0, zh], par.at[0, zh], zp)

    def prepare(weight, held, store, width, count, slot, core):
        rows = [
            weight[pl.ds(pl.multiple_of(t * width + z * 2 * count + core * count, 16), count), :]
            for t in range(3)
            for z in range(2)
        ]
        held[...] = jnp.concatenate(rows, axis=0).T
        for z in range(2):
            store(slot, z, held[pl.ds(pl.multiple_of(z * 2 * count + k * count, 16), count), :])

    w1t, w4t, w2t = r["w1t"], r["w4t"], r["w2t"]

    def store1(slot, z, value):
        w1t[slot, z * Q1 : (z + 1) * Q1, :] = value

    def store4(slot, z, value):
        w4t[slot, z] = value

    loads["tw1"].wait()
    for slot, core in ((0, k), (1, ok)):
        prepare(r["tw1_v"], r["tmp1"], store1, C1, Q1, slot, core)

    src = lax.broadcasted_iota(jnp.int32, (256, 128), 0)
    dst = lax.broadcasted_iota(jnp.int32, (256, 128), 1)
    same = (src >= 128) == (dst >= 64)
    src_col = src - jnp.where(src >= 128, 128, 0)
    dst_col = dst - jnp.where(dst >= 64, 64, 0)
    for dx in range(3):
        r["pick1"][:, dx * 128 : (dx + 1) * 128] = jnp.where(
            same & (src_col == 2 * dst_col + dx - 1), 1.0, 0.0
        ).astype(BF)

    state = stat_send(stat_wait(state), x_peers)
    dw_z.wait_recv()
    here = dwt.at[oz, own_piece]
    dw_y = [
        send(here, here, {"frame": x * ny + lax.rem(y + 2 * d, ny)}) for d in range(1, pieces)
    ]
    dw_x = [send(here, here, p) for p in x_peers]

    src = lax.broadcasted_iota(jnp.int32, (256, 256), 0)
    dst = lax.broadcasted_iota(jnp.int32, (256, 256), 1)
    second = dst >= 128
    lane = dst - jnp.where(second, 128, 0)
    upper = lane >= 64
    col = lane - jnp.where(upper, 64, 0)
    base = jnp.where(second, 128, 64) + jnp.where(upper, 64, 0)
    for dx in range(3):
        want = col + (dx - 1)
        keep = (want >= 0) & (want < W2) & (src == base + want)
        r["pick2"][dx] = jnp.where(keep, 1.0, 0.0).astype(BF)
    loads["cw2"].wait()
    loads["sw2"].wait()
    for t in range(9):
        w2t[:, t * C1 : (t + 1) * C1] = r["cw2_v"][t * Q2 : (t + 1) * Q2, :]
    w2t[:, 9 * C1 : 10 * C1] = r["sw2_v"][...]
    y_fwd = []

    def forward(i):
        z_copies[i].wait_recv()
        y_fwd.append(to_frames(raw1, oz, *CHUNKS[i]))

    forward(0)
    state = stat_send(stat_wait(state), y_peers)
    for d in range(1, pieces):
        dw_y[d - 1].wait_recv()
        start = x * DPART + lax.rem(y // 2 + pieces - d, pieces) * piece
        there = dwt.at[oz, pl.ds(pl.multiple_of(start, 16), piece)]
        dw_x += [send(there, there, p) for p in x_peers]
    forward(1)
    loads["tw2"].wait()
    for slot, core in ((0, k), (1, ok)):
        prepare(r["tw2_v"], r["tmp2"], store4, C2, Q2, slot, core)
    par_copy.wait_recv()
    par_k = send(par.at[0], par.at[1], kp)
    cols = [to_columns(par[0, z]) for z in range(2)]
    cols2 = to_columns(r["par2"][...])
    bias = jnp.where(zh == 0, cols[0][0:Q2, 4:5], cols[1][0:Q2, 4:5])
    total = stat_wait(state)
    affine1 = [
        scale_columns(
            total,
            float(C1 // GROUPS * H1 * W1 * frames),
            q1_iota + (2 * z + k) * Q1,
            C1 // GROUPS,
            cols[z][0:Q1, 0:1],
            cols[z][0:Q1, 1:2],
        )
        for z in range(2)
    ]
    hid1 = r["hid1"]
    alive = {0: f > 0, 2: f < frames - 1}

    def pick(pair, z):
        return [jnp.where(z == 0, pair[0][i], pair[1][i]) for i in range(2)]

    def hidden(raw, hid, z, affine, a, n, waits):
        span = slice(a, a + n)
        scale, shift = pick(affine, z)
        for tap in (1, 0, 2):
            if tap != 1:
                waits[tap // 2].wait_recv()
            value = silu_of_half(raw[tap, z, :, span].astype(F32) * scale + shift)
            if tap != 1:
                value = jnp.where(alive[tap], value, 0.0)
            hid[0, tap, z, :, span] = value.astype(BF)
        return send(hid.at[0, :, z, :, pl.ds(a, n)], hid.at[1, :, z, :, pl.ds(a, n)], kp)

    blk, taps1 = r["blk"], r["taps1"]
    part, part_rx, red = r["part"], r["part_rx"], r["red"]
    half = C1 // 2
    k1, part_k, red_z, red_k = {}, {}, {}, {}

    def hid_own(i):
        k1[i] = [hidden(raw1, hid1, zh, affine1, *CHUNKS[i], y_own[i])]

    def hid_other(i):
        k1[i].append(hidden(raw1, hid1, oz, affine1, *CHUNKS[i], y_fwd[i]))

    def first_conv(i):
        a, n = CHUNKS[i]
        span = slice(a, a + n)
        for copy in k1[i]:
            copy.wait_recv()
        mixed = sum(
            dot(w1t[slot], hid1[slot, :, :, :, span].reshape(6 * Q1, n)) for slot in range(2)
        ).astype(BF)
        value = raw1[1, :, :, span].reshape(2 * Q1, n).astype(F32) + mixed.astype(F32)
        if i == 0:
            blk[:, 0:W1] = jnp.where(zh == 0, 0.0, value[:, 0:W1]).astype(BF)
            blk[:, W1:n] = value[:, W1:].astype(BF)
        else:
            blk[:, span] = value.astype(BF)
        at = slice(i * 128, (i + 1) * 128)
        for dy in range(3):
            top = (4 * i + dy) * W1
            pair = jnp.concatenate(
                [blk[:, top : top + W1], blk[:, top + 2 * W1 : top + 3 * W1]], axis=1
            )
            got = dot(pair, r["pick1"][...]).astype(BF)
            for dx in range(3):
                t = 3 * dy + dx
                for z in range(2):
                    taps1[z, t * Q1 : (t + 1) * Q1, at] = got[
                        z * Q1 : (z + 1) * Q1, dx * 128 : (dx + 1) * 128
                    ]

    def down(i):
        at = slice(i * 128, (i + 1) * 128)
        part[:, at] = sum(
            lax.dot_general(
                dwt[z, 0 : 9 * Q1, :],
                taps1[z, :, at],
                (((0,), (0,)), ((), ())),
                preferred_element_type=F32,
            )
            for z in range(2)
        )
        part_k[i] = send(
            part.at[pl.ds(pl.multiple_of(ok * half, 16), half), pl.ds(i * 128, 128)],
            part_rx.at[:, pl.ds(i * 128, 128)],
            kp,
        )

    def reduced(i):
        at = slice(i * 128, (i + 1) * 128)
        part_k[i].wait_recv()
        mine = part[pl.ds(pl.multiple_of(k * half, 16), half), at]
        red[k, zh, :, at] = (mine + part_rx[:, at]).astype(BF)
        here = red.at[k, zh, :, pl.ds(i * 128, 128)]
        red_z[i] = send(here, here, zp)
        red_k[i] = [send(here, here, kp)]

    def pass_reduced(i):
        red_z[i].wait_recv()
        here = red.at[k, oz, :, pl.ds(i * 128, 128)]
        red_k[i].append(send(here, here, kp))

    hid_own(0)
    hid_other(0)
    hid_own(1)
    forward(2)
    first_conv(0)
    hid_other(1)
    hid_own(2)
    first_conv(1)
    for copy in dw_x:
        copy.wait_recv()
    down(0)
    down(1)
    hid_other(2)
    reduced(0)
    reduced(1)
    first_conv(2)
    down(2)
    reduced(2)
    for i in range(3):
        pass_reduced(i)
    for i in range(3):
        for copy in red_k[i]:
            copy.wait_recv()

    nrm = r["nrm"]
    nrm[:, 0:128] = jnp.zeros((C1, 128), BF)
    nrm[:, 128 + POS2 :] = jnp.zeros((C1, 128), BF)
    half_iota = lax.broadcasted_iota(jnp.int32, (half, 1), 0)
    for core in range(2):
        sides = [red[core, z] for z in range(2)]
        wide = jnp.concatenate(sides, axis=1).astype(F32)
        chan = half_iota + core * half
        row2 = group_row(
            jnp.sum(wide, axis=1, keepdims=True),
            jnp.sum(wide * wide, axis=1, keepdims=True),
            chan,
            C1 // GROUPS,
        )
        span = slice(core * half, (core + 1) * half)
        scale, shift = scale_columns(
            row2, float(C1 // GROUPS * POS2), chan, C1 // GROUPS, cols2[span, 0:1], cols2[span, 1:2]
        )
        nrm[span, 128 : 128 + POS2] = silu_of_half(wide * scale + shift).astype(BF)

    def second(side, taps):
        for dx in range(3):
            for j in range(TILES + 1):
                window = nrm[:, lanes(side * HALF2 + j * 128, 256)]
                got = dot(window, r["pick2"][dx]).astype(BF)
                if j < TILES:
                    at = slice(j * 128, (j + 1) * 128)
                    taps[dx * C1 : (dx + 1) * C1, at] = got[:, 0:128]
                    taps[(3 + dx) * C1 : (4 + dx) * C1, at] = got[:, 128:256]
                if j > 0:
                    at = slice((j - 1) * 128, j * 128)
                    taps[(6 + dx) * C1 : (7 + dx) * C1, at] = got[:, 0:128]
        for core in range(2):
            taps[9 * C1 + core * half : 9 * C1 + (core + 1) * half, :] = red[core, side]

    spat_o = r["spat_o"]
    second(oz, r["taps2o"])
    z2 = []
    for i in range(TILES):
        at = slice(i * 128, (i + 1) * 128)
        spat_o[:, at] = (dot(w2t[...], r["taps2o"][:, at]) + bias).astype(BF)
        here = pl.ds(i * 128, 128)
        z2.append(send(spat_o.at[:, here], raw2.at[0, 1, zh, :, here], zp))
    second(zh, r["taps2"])
    raw2[0, 1, zh] = (dot(w2t[...], r["taps2"][...]) + bias).astype(BF)
    own = raw2.at[0]
    y2_own = to_frames(own, zh, 0, HALF2)
    raw_k = [send(raw2.at[0, 1, zh], raw2.at[1, 1, zh], kp)]
    wide = jnp.concatenate([raw2[0, 1, zh], spat_o[...]], axis=1).astype(F32)
    q2_iota = lax.broadcasted_iota(jnp.int32, (Q2, 1), 0)
    row3 = group_row(
        jnp.sum(wide, axis=1, keepdims=True),
        jnp.sum(wide * wide, axis=1, keepdims=True),
        q2_iota + c * Q2,
        C2 // GROUPS,
    )
    state = stat_send(row3, x_peers)
    par_k.wait_recv()
    cols3 = [cols, [to_columns(par[1, z]) for z in range(2)]]
    y2_fwd = []

    def share(tap, z, a, n):
        here = pl.ds(a, n)
        raw_k.append(send(raw2.at[0, tap, z, :, here], raw2.at[1, tap, z, :, here], kp))

    def forward2(i):
        z2[i].wait_recv()
        y2_fwd.append(to_frames(own, oz, i * 128, 128))
        share(1, oz, i * 128, 128)

    state = stat_send(stat_wait(state), y_peers)
    for tap in (0, 2):
        y2_own[tap // 2].wait_recv()
        share(tap, zh, 0, HALF2)
    forward2(0)
    state = stat_send(stat_wait(state), chan_peers)
    forward2(1)
    forward2(2)
    for i in range(TILES):
        for tap in (0, 2):
            y2_fwd[i][tap // 2].wait_recv()
            share(tap, oz, i * 128, 128)
    total = stat_wait(state)
    hid2 = r["hid2"]
    for slot, core in ((0, k), (1, ok)):
        if slot == 1:
            for copy in raw_k:
                copy.wait_recv()
        for z in range(2):
            scale, shift = scale_columns(
                total,
                float(C2 // GROUPS * POS2 * frames),
                q2_iota + (2 * z + core) * Q2,
                C2 // GROUPS,
                cols3[slot][z][0:Q2, 2:3],
                cols3[slot][z][0:Q2, 3:4],
            )
            for tap in range(3):
                value = silu_of_half(raw2[slot, tap, z].astype(F32) * scale + shift)
                if tap != 1:
                    value = jnp.where(alive[tap], value, 0.0)
                hid2[slot, tap, z] = value.astype(BF)

    fin = r["fin"]

    def second_conv(z, at, n):
        mixed = sum(
            dot(w4t[slot, z], hid2[slot, :, :, :, at].reshape(6 * Q2, n)) for slot in range(2)
        ).astype(BF)
        return (raw2[0, 1, z, :, at].astype(F32) + mixed.astype(F32)).astype(BF)

    last = []
    for i in range(TILES):
        at = slice(i * 128, (i + 1) * 128)
        fin[0, :, at] = second_conv(oz, at, 128)
        there = out.at[:, lanes(zh * HALF2 + i * 128, 128)]
        last.append(send(fin.at[0, :, pl.ds(i * 128, 128)], there, zp))
    fin[1] = second_conv(zh, slice(0, HALF2), HALF2)
    kept = pltpu.make_async_copy(fin.at[1], out.at[:, lanes(zh * HALF2, HALF2)], local_sem.at[15])
    kept.start()
    for copy in last:
        copy.wait_recv()
    kept.wait()
    for copy in sent:
        copy.wait_send()


def per_device(frames, lat, tw1, g1, s1, dw, g2, s2, cw2, sw2, tb, tw2, g3, s3):
    far = pl.BlockSpec(memory_space=pl.ANY)
    row = lambda v: v.reshape(1, v.shape[0])
    result = pl.pallas_call(
        functools.partial(kernel, frames),
        out_shape=jax.ShapeDtypeStruct((Q2, POS2), BF),
        in_specs=[far] * 13,
        out_specs=far,
        scratch_shapes=[pltpu.VMEM(shape, dtype) for shape, dtype in SCRATCH.values()]
        + [
            pltpu.SemaphoreType.DMA((N_SEM,)),
            pltpu.SemaphoreType.DMA((N_SEM,)),
            pltpu.SemaphoreType.DMA((16,)),
        ],
        compiler_params=pltpu.CompilerParams(
            collective_id=0, has_side_effects=True, vmem_limit_bytes=56 * 2**20
        ),
        name="video_block",
    )(
        lat.reshape(Q1, H1 * W1),
        tw1.reshape(3 * C1, C1),
        row(g1),
        row(s1),
        dw.reshape(9 * Q1, C1),
        g2,
        s2,
        cw2.transpose(0, 2, 1).reshape(9 * Q2, C1),
        sw2.T,
        row(tb),
        tw2.reshape(3 * C2, C2),
        row(g3),
        row(s3),
    )
    return result.reshape(1, Q2, POS2)


def solution(mesh):
    return jax.shard_map(
        functools.partial(per_device, mesh.shape["frame"]),
        mesh=mesh,
        in_specs=(
            P(("video", "frame"), "chan", None),
            P(),
            P("chan"),
            P("chan"),
            P(None, "chan", None),
            P(),
            P(),
            P(None, None, "chan"),
            P(None, "chan"),
            P("chan"),
            P(),
            P("chan"),
            P("chan"),
        ),
        out_specs=P(("video", "frame"), "chan", None),
        check_vma=False,
    )
```

```python
import functools

import jax
import jax.numpy as jnp
from jax import lax
from jax.experimental import pallas as pl
from jax.experimental.pallas import tpu as pltpu
from jax.sharding import PartitionSpec as P

MESH = pl.DeviceIdType.MESH
BF = jnp.bfloat16
F32 = jnp.float32
C1 = 320
C2 = 640
GROUPS = 32
W1 = 128
H1 = 24
H2 = 12
W2 = 64
NX = 4
EPS = 1e-6

Q1 = C1 // 4
Q2 = C2 // 4
HALF1 = H1 * W1 // 2
WIN1 = HALF1 + W1
HALF2 = H2 * W2 // 2
POS2 = H2 * W2
DPAD = 768
DPART = DPAD // NX
TILES = HALF2 // 128
KTILES = 10 * C1 // 128
CROWS = 4096
CPART = CROWS // NX
CHUNKS = ((0, 640), (640, 512), (1152, 512))

SCRATCH = {
    "lat_v": ((Q1, H1 * W1), BF),
    "tw1_v": ((3 * C1, C1), BF),
    "tw2_v": ((3 * C2, C2), BF),
    "cw2_v": ((9 * Q2, C1), BF),
    "sw2_v": ((Q2, C1), BF),
    "zsrc": ((Q1, WIN1), BF),
    "raw1": ((3, 2, Q1, WIN1), BF),
    "hid1": ((2, 3, 2, Q1, WIN1), BF),
    "tmp1": ((C1, 6 * Q1), BF),
    "w1t": ((2, 2 * Q1, 6 * Q1), BF),
    "blk": ((2 * Q1, WIN1), BF),
    "dwt": ((2, DPAD, C1), BF),
    "taps1": ((2, 9 * Q1, HALF2), BF),
    "part": ((C1, HALF2), F32),
    "part_rx": ((C1 // 2, HALF2), F32),
    "red": ((2, C1 // 2, HALF2), BF),
    "halo": ((2, C1 // 2, 128), BF),
    "nrm": ((C1, HALF2 + 256), BF),
    "taps2": ((10 * C1, HALF2), BF),
    "w2t": ((Q2, 10 * C1), BF),
    "cwt": ((2, CROWS, 128), BF),
    "raw2": ((2, 3, 2, Q2, HALF2), BF),
    "hid2": ((2, 3, 2, Q2, HALF2), BF),
    "tmp2": ((C2, 6 * Q2), BF),
    "w4t": ((2, 2, Q2, 6 * Q2), BF),
    "pick1": ((256, 384), BF),
    "pick2": ((3, 256, 256), BF),
    "fin": ((2, Q2, HALF2), BF),
    "par": ((2, 2, 8, 256), F32),
    "par2": ((8, 384), F32),
    "g1_v": ((1, Q1), F32),
    "s1_v": ((1, Q1), F32),
    "g2_v": ((C1,), F32),
    "s2_v": ((C1,), F32),
    "g3_v": ((1, Q2), F32),
    "s3_v": ((1, Q2), F32),
    "tb_v": ((1, Q2), F32),
    "st_tx": ((8, 1, 128), F32),
    "st_rx": ((40, 1, 128), F32),
}
N_SEM = 128


def dot(a, b):
    return lax.dot_general(a, b, (((1,), (0,)), ((), ())), preferred_element_type=F32)


def silu_of_half(w):
    return w + w * jnp.tanh(w)


def to_columns(rows):
    return jnp.concatenate([rows] * (128 // rows.shape[0]), axis=0).T


def one_hots(chan, size):
    lane = lax.broadcasted_iota(jnp.int32, (chan.shape[0], 128), 1) * size
    off = GROUPS * size
    first = (lane <= chan) & (chan < lane + size)
    second = (lane - off <= chan) & (chan < lane - off + size)
    return first, second


def group_row(sums, squares, chan, size):
    first, second = one_hots(chan, size)
    spread = jnp.where(first, sums, 0.0) + jnp.where(second, squares, 0.0)
    return jnp.sum(spread, axis=0, keepdims=True)


def scale_columns(row, count, chan, size, gain, shift):
    first, second = one_hots(chan, size)
    mean = jnp.sum(jnp.where(first, row, 0.0), axis=1, keepdims=True) / count
    square = jnp.sum(jnp.where(second, row, 0.0), axis=1, keepdims=True) / count
    scale = lax.rsqrt(square - mean * mean + EPS) * gain
    return 0.5 * scale, 0.5 * (shift - mean * scale)


def kernel(frames, *refs):
    (lat, tw1, g1, s1, dw, g2, s2, cw2, sw2, tb, tw2, g3, s3, out) = refs[:14]
    names = list(SCRATCH)
    r = dict(zip(names, refs[14 : 14 + len(names)]))
    send_sem, recv_sem, local_sem = refs[14 + len(names) :]
    ny = frames // NX
    f = lax.axis_index("frame")
    c = lax.axis_index("chan")
    x, y = f // ny, lax.rem(f, ny)
    zh, k = c // 2, lax.rem(c, 2)
    oz, ok = 1 - zh, 1 - k
    zp = {"chan": lax.rem(c + 2, 4)}
    kp = {"chan": c + 1 - 2 * k}
    after = {"frame": lax.rem(f + 1, frames)}
    before = {"frame": lax.rem(f + frames - 1, frames)}
    chan_peers = [{"chan": lax.rem(c + d, 4)} for d in range(1, 4)]
    x_peers = [{"frame": lax.rem(x + d, NX) * ny + y} for d in range(1, NX)]
    y_peers = [{"frame": x * ny + lax.rem(y + d, ny)} for d in range(1, ny)]

    xz_peers = [
        {"frame": lax.rem(x + d, NX) * ny + y, "chan": lax.rem(c + e, 4)}
        for d in range(NX)
        for e in (0, 2)
        if d or e
    ]
    diagonal = {"chan": lax.rem(c + 2, 4) + 1 - 2 * k}

    barrier = pltpu.get_barrier_semaphore()
    greeted = xz_peers + y_peers + [kp, diagonal, after, before]
    for peer in greeted:
        pl.semaphore_signal(barrier, inc=1, device_id=peer, device_id_type=MESH)

    loads = {}
    for number, (name, ref, dst) in enumerate(
        (
            ("lat", lat, r["lat_v"]),
            ("dw", dw, r["dwt"].at[zh, pl.ds(0, 9 * Q1)]),
            ("g1", g1, r["g1_v"]),
            ("s1", s1, r["s1_v"]),
            ("g2", g2, r["g2_v"]),
            ("s2", s2, r["s2_v"]),
            ("g3", g3, r["g3_v"]),
            ("s3", s3, r["s3_v"]),
            ("tb", tb, r["tb_v"]),
            ("tw1", tw1, r["tw1_v"]),
            ("cw2", cw2, r["cw2_v"]),
            ("sw2", sw2, r["sw2_v"]),
            ("tw2", tw2, r["tw2_v"]),
        )
    ):
        loads[name] = pltpu.make_async_copy(ref, dst, local_sem.at[number])
        loads[name].start()

    counter = [0]
    sent = []

    def send(src, dst, peer):
        number = counter[0]
        counter[0] += 1
        copy = pltpu.make_async_remote_copy(
            src_ref=src,
            dst_ref=dst,
            send_sem=send_sem.at[number],
            recv_sem=recv_sem.at[number],
            device_id=peer,
            device_id_type=MESH,
        )
        copy.start()
        sent.append(copy)
        return copy

    def lanes(start, size):
        return pl.ds(pl.multiple_of(start, 128), size)

    st_tx, st_rx = r["st_tx"], r["st_rx"]
    stat_slot = [0, 0]

    def stat_send(row, peers):
        tx, rx = stat_slot
        stat_slot[0] += 1
        stat_slot[1] += len(peers)
        st_tx[tx] = row
        return [send(st_tx.at[tx], st_rx.at[rx + i], p) for i, p in enumerate(peers)], tx, rx

    def stat_wait(state):
        copies, tx, rx = state
        total = st_tx[tx]
        for i, copy in enumerate(copies):
            copy.wait_recv()
            total = total + st_rx[rx + i]
        return total

    raw1, raw2 = r["raw1"], r["raw2"]
    lat_v = r["lat_v"]

    par = r["par"]
    loads["lat"].wait()
    zsrc = r["zsrc"]
    raw1[1, zh, :, 0:W1] = lat_v[:, HALF1 - W1 : HALF1]
    raw1[1, zh, :, W1:WIN1] = lat_v[:, lanes(zh * HALF1, HALF1)]
    zsrc[:, 0:W1] = lat_v[:, HALF1 - W1 : HALF1]
    zsrc[:, W1:WIN1] = lat_v[:, lanes(oz * HALF1, HALF1)]
    wide = lat_v[...].astype(F32)
    q1_iota = lax.broadcasted_iota(jnp.int32, (Q1, 1), 0)
    row1 = group_row(
        jnp.sum(wide, axis=1, keepdims=True),
        jnp.sum(wide * wide, axis=1, keepdims=True),
        q1_iota + c * Q1,
        C1 // GROUPS,
    )
    dwt = r["dwt"]
    for name in ("dw", "g1", "s1", "g2", "s2", "g3", "s3", "tb"):
        loads[name].wait()
    par[0, zh, 0:1, 0:Q1] = r["g1_v"][...]
    par[0, zh, 1:2, 0:Q1] = r["s1_v"][...]
    par[0, zh, 2:3, 0:Q2] = r["g3_v"][...]
    par[0, zh, 3:4, 0:Q2] = r["s3_v"][...]
    par[0, zh, 4:5, 0:Q2] = r["tb_v"][...]
    r["par2"][0:1, 0:C1] = r["g2_v"][...].reshape(1, C1)
    r["par2"][1:2, 0:C1] = r["s2_v"][...].reshape(1, C1)
    dwt[zh, 9 * Q1 : DPAD, :] = jnp.zeros((DPAD - 9 * Q1, C1), BF)
    pl.semaphore_wait(barrier, len(greeted))

    state = stat_send(row1, xz_peers)
    pieces = ny // 2
    piece = DPART // pieces
    own_piece = pl.ds(pl.multiple_of(x * DPART + (y // 2) * piece, 16), piece)
    dw_z = send(dwt.at[zh, own_piece], dwt.at[zh, own_piece], zp)

    z_copies = [
        send(zsrc.at[:, pl.ds(a, n)], raw1.at[1, zh, :, pl.ds(a, n)], zp) for a, n in CHUNKS
    ]

    def to_frames(raw, z, a, n):
        here = raw.at[1, z, :, pl.ds(a, n)]
        return [
            send(here, raw.at[0, z, :, pl.ds(a, n)], after),
            send(here, raw.at[2, z, :, pl.ds(a, n)], before),
        ]

    y_own = [to_frames(raw1, zh, a, n) for a, n in CHUNKS]
    par_copy = send(par.at[0, zh], par.at[0, zh], zp)

    def prepare(weight, held, store, width, count, slot, core):
        rows = [
            weight[pl.ds(pl.multiple_of(t * width + z * 2 * count + core * count, 16), count), :]
            for t in range(3)
            for z in range(2)
        ]
        held[...] = jnp.concatenate(rows, axis=0).T
        for z in range(2):
            store(slot, z, held[pl.ds(pl.multiple_of(z * 2 * count + k * count, 16), count), :])

    w1t, w4t, w2t = r["w1t"], r["w4t"], r["w2t"]

    def store1(slot, z, value):
        w1t[slot, z * Q1 : (z + 1) * Q1, :] = value

    def store4(slot, z, value):
        w4t[slot, z] = value

    loads["tw1"].wait()
    for slot, core in ((0, k), (1, ok)):
        prepare(r["tw1_v"], r["tmp1"], store1, C1, Q1, slot, core)

    src = lax.broadcasted_iota(jnp.int32, (256, 128), 0)
    dst = lax.broadcasted_iota(jnp.int32, (256, 128), 1)
    same = (src >= 128) == (dst >= 64)
    src_col = src - jnp.where(src >= 128, 128, 0)
    dst_col = dst - jnp.where(dst >= 64, 64, 0)
    for dx in range(3):
        r["pick1"][:, dx * 128 : (dx + 1) * 128] = jnp.where(
            same & (src_col == 2 * dst_col + dx - 1), 1.0, 0.0
        ).astype(BF)

    loads["cw2"].wait()
    loads["sw2"].wait()
    cwt = r["cwt"]
    for t in range(9):
        w2t[:, t * C1 : (t + 1) * C1] = r["cw2_v"][t * Q2 : (t + 1) * Q2, :]
    w2t[:, 9 * C1 : 10 * C1] = r["sw2_v"][...]
    for j in range(KTILES):
        cwt[zh, j * Q2 : (j + 1) * Q2, :] = w2t[:, j * 128 : (j + 1) * 128]
    cwt[zh, KTILES * Q2 :, :] = jnp.zeros((CROWS - KTILES * Q2, 128), BF)
    cpiece = CPART // pieces

    def cw_rows(d):
        start = x * CPART + lax.rem(y // 2 + pieces - d, pieces) * cpiece
        return pl.ds(pl.multiple_of(start, 16), cpiece)

    cw_z = send(cwt.at[zh, cw_rows(0)], cwt.at[zh, cw_rows(0)], zp)
    dw_z.wait_recv()
    here = dwt.at[oz, own_piece]
    dw_y = [
        send(here, here, {"frame": x * ny + lax.rem(y + 2 * d, ny)}) for d in range(1, pieces)
    ]
    dw_x = [send(here, here, p) for p in x_peers]

    src = lax.broadcasted_iota(jnp.int32, (256, 256), 0)
    dst = lax.broadcasted_iota(jnp.int32, (256, 256), 1)
    second = dst >= 128
    lane = dst - jnp.where(second, 128, 0)
    upper = lane >= 64
    col = lane - jnp.where(upper, 64, 0)
    base = jnp.where(second, 128, 64) + jnp.where(upper, 64, 0)
    for dx in range(3):
        want = col + (dx - 1)
        keep = (want >= 0) & (want < W2) & (src == base + want)
        r["pick2"][dx] = jnp.where(keep, 1.0, 0.0).astype(BF)
    y_fwd = []

    def forward(i):
        z_copies[i].wait_recv()
        y_fwd.append(to_frames(raw1, oz, *CHUNKS[i]))

    forward(0)
    state = stat_send(stat_wait(state), y_peers)
    for d in range(1, pieces):
        dw_y[d - 1].wait_recv()
        start = x * DPART + lax.rem(y // 2 + pieces - d, pieces) * piece
        there = dwt.at[oz, pl.ds(pl.multiple_of(start, 16), piece)]
        dw_x += [send(there, there, p) for p in x_peers]
    forward(1)
    loads["tw2"].wait()
    for slot, core in ((0, k), (1, ok)):
        prepare(r["tw2_v"], r["tmp2"], store4, C2, Q2, slot, core)
    par_copy.wait_recv()
    par_k = send(par.at[0], par.at[1], kp)
    state = stat_send(stat_wait(state), [kp])
    cols = [to_columns(par[0, z]) for z in range(2)]
    cols2 = to_columns(r["par2"][...])
    total = stat_wait(state)
    affine1 = [
        scale_columns(
            total,
            float(C1 // GROUPS * H1 * W1 * frames),
            q1_iota + (2 * z + k) * Q1,
            C1 // GROUPS,
            cols[z][0:Q1, 0:1],
            cols[z][0:Q1, 1:2],
        )
        for z in range(2)
    ]
    hid1 = r["hid1"]
    alive = {0: f > 0, 2: f < frames - 1}

    def pick(pair, z):
        return [jnp.where(z == 0, pair[0][i], pair[1][i]) for i in range(2)]

    def hidden(raw, hid, z, affine, a, n, waits):
        span = slice(a, a + n)
        scale, shift = pick(affine, z)
        for tap in (1, 0, 2):
            if tap != 1:
                waits[tap // 2].wait_recv()
            value = silu_of_half(raw[tap, z, :, span].astype(F32) * scale + shift)
            if tap != 1:
                value = jnp.where(alive[tap], value, 0.0)
            hid[0, tap, z, :, span] = value.astype(BF)
        return send(hid.at[0, :, z, :, pl.ds(a, n)], hid.at[1, :, z, :, pl.ds(a, n)], kp)

    blk, taps1 = r["blk"], r["taps1"]
    part, part_rx, red = r["part"], r["part_rx"], r["red"]
    half = C1 // 2
    k1, part_k, red_k = {}, {}, {}

    def hid_own(i):
        k1[i] = [hidden(raw1, hid1, zh, affine1, *CHUNKS[i], y_own[i])]

    def hid_other(i):
        k1[i].append(hidden(raw1, hid1, oz, affine1, *CHUNKS[i], y_fwd[i]))

    def first_conv(i):
        a, n = CHUNKS[i]
        span = slice(a, a + n)
        for copy in k1[i]:
            copy.wait_recv()
        mixed = sum(
            dot(w1t[slot], hid1[slot, :, :, :, span].reshape(6 * Q1, n)) for slot in range(2)
        ).astype(BF)
        value = raw1[1, :, :, span].reshape(2 * Q1, n).astype(F32) + mixed.astype(F32)
        if i == 0:
            blk[:, 0:W1] = jnp.where(zh == 0, 0.0, value[:, 0:W1]).astype(BF)
            blk[:, W1:n] = value[:, W1:].astype(BF)
        else:
            blk[:, span] = value.astype(BF)
        at = slice(i * 128, (i + 1) * 128)
        for dy in range(3):
            top = (4 * i + dy) * W1
            pair = jnp.concatenate(
                [blk[:, top : top + W1], blk[:, top + 2 * W1 : top + 3 * W1]], axis=1
            )
            got = dot(pair, r["pick1"][...]).astype(BF)
            for dx in range(3):
                t = 3 * dy + dx
                for z in range(2):
                    taps1[z, t * Q1 : (t + 1) * Q1, at] = got[
                        z * Q1 : (z + 1) * Q1, dx * 128 : (dx + 1) * 128
                    ]

    def down(i):
        at = slice(i * 128, (i + 1) * 128)
        part[:, at] = sum(
            lax.dot_general(
                dwt[z, 0 : 9 * Q1, :],
                taps1[z, :, at],
                (((0,), (0,)), ((), ())),
                preferred_element_type=F32,
            )
            for z in range(2)
        )
        part_k[i] = send(
            part.at[pl.ds(pl.multiple_of(ok * half, 16), half), pl.ds(i * 128, 128)],
            part_rx.at[:, pl.ds(i * 128, 128)],
            kp,
        )

    def reduced(i):
        at = slice(i * 128, (i + 1) * 128)
        part_k[i].wait_recv()
        mine = part[pl.ds(pl.multiple_of(k * half, 16), half), at]
        red[k, :, at] = (mine + part_rx[:, at]).astype(BF)
        here = red.at[k, :, pl.ds(i * 128, 128)]
        red_k[i] = send(here, here, kp)

    hid_own(0)
    hid_other(0)
    hid_own(1)
    forward(2)
    cw_z.wait_recv()
    here = cwt.at[oz, cw_rows(0)]
    cw_y = [
        send(here, here, {"frame": x * ny + lax.rem(y + 2 * d, ny)}) for d in range(1, pieces)
    ]
    cw_x = [send(here, here, p) for p in x_peers]
    first_conv(0)
    hid_other(1)
    hid_own(2)
    first_conv(1)
    for copy in dw_x:
        copy.wait_recv()
    down(0)
    down(1)
    hid_other(2)
    reduced(0)
    reduced(1)
    first_conv(2)
    down(2)
    reduced(2)

    half_iota = lax.broadcasted_iota(jnp.int32, (half, 1), 0)
    wide = red[k].astype(F32)
    row2 = group_row(
        jnp.sum(wide, axis=1, keepdims=True),
        jnp.sum(wide * wide, axis=1, keepdims=True),
        half_iota + k * half,
        C1 // GROUPS,
    )
    state = stat_send(row2, chan_peers)
    edge = red.at[k, :, lanes(oz * (HALF2 - 128), 128)]
    halo = r["halo"]
    edges = [send(edge, halo.at[k], p) for p in (zp, diagonal)]
    for d in range(1, pieces):
        cw_y[d - 1].wait_recv()
        there = cwt.at[oz, cw_rows(d)]
        cw_x += [send(there, there, p) for p in x_peers]
    for i in range(TILES):
        red_k[i].wait_recv()
    total2 = stat_wait(state)
    for copy in edges:
        copy.wait_recv()
    nrm, taps2 = r["nrm"], r["taps2"]
    for core in range(2):
        span = slice(core * half, (core + 1) * half)
        scale, shift = scale_columns(
            total2,
            float(C1 // GROUPS * POS2),
            half_iota + core * half,
            C1 // GROUPS,
            cols2[span, 0:1],
            cols2[span, 1:2],
        )
        nrm[span, 128 : 128 + HALF2] = silu_of_half(red[core].astype(F32) * scale + shift).astype(BF)
        outer = silu_of_half(halo[core].astype(F32) * scale + shift)
        nrm[span, 0:128] = jnp.where(zh == 1, outer, 0.0).astype(BF)
        nrm[span, 128 + HALF2 :] = jnp.where(zh == 0, outer, 0.0).astype(BF)
        taps2[9 * C1 + core * half : 9 * C1 + (core + 1) * half, :] = red[core]

    for dx in range(3):
        for j in range(TILES + 1):
            got = dot(nrm[:, j * 128 : j * 128 + 256], r["pick2"][dx]).astype(BF)
            if j < TILES:
                at = slice(j * 128, (j + 1) * 128)
                taps2[dx * C1 : (dx + 1) * C1, at] = got[:, 0:128]
                taps2[(3 + dx) * C1 : (4 + dx) * C1, at] = got[:, 128:256]
            if j > 0:
                at = slice((j - 1) * 128, j * 128)
                taps2[(6 + dx) * C1 : (7 + dx) * C1, at] = got[:, 0:128]
    for copy in cw_x:
        copy.wait_recv()
    own = raw2.at[0]
    y2 = []
    for z in range(2):
        weight = jnp.concatenate(
            [cwt[z, j * Q2 : (j + 1) * Q2, :] for j in range(KTILES)], axis=1
        )
        raw2[0, 1, z] = (dot(weight, taps2[...]) + cols[z][0:Q2, 4:5]).astype(BF)
        y2.append(to_frames(own, z, 0, HALF2))
    raw_k = [send(raw2.at[0, 1], raw2.at[1, 1], kp)]
    q2_iota = lax.broadcasted_iota(jnp.int32, (Q2, 1), 0)
    row3 = jnp.zeros((1, 128), F32)
    for z in range(2):
        wide = raw2[0, 1, z].astype(F32)
        row3 = row3 + group_row(
            jnp.sum(wide, axis=1, keepdims=True),
            jnp.sum(wide * wide, axis=1, keepdims=True),
            q2_iota + (2 * z + k) * Q2,
            C2 // GROUPS,
        )
    state = stat_send(row3, xz_peers)
    par_k.wait_recv()
    cols3 = [cols, [to_columns(par[1, z]) for z in range(2)]]
    state = stat_send(stat_wait(state), y_peers)
    for z in range(2):
        for tap in (0, 2):
            y2[z][tap // 2].wait_recv()
            raw_k.append(send(raw2.at[0, tap, z], raw2.at[1, tap, z], kp))
    state = stat_send(stat_wait(state), [kp])
    total = stat_wait(state)
    hid2 = r["hid2"]
    for slot, core in ((0, k), (1, ok)):
        if slot == 1:
            for copy in raw_k:
                copy.wait_recv()
        for z in range(2):
            scale, shift = scale_columns(
                total,
                float(C2 // GROUPS * POS2 * frames),
                q2_iota + (2 * z + core) * Q2,
                C2 // GROUPS,
                cols3[slot][z][0:Q2, 2:3],
                cols3[slot][z][0:Q2, 3:4],
            )
            for tap in range(3):
                value = silu_of_half(raw2[slot, tap, z].astype(F32) * scale + shift)
                if tap != 1:
                    value = jnp.where(alive[tap], value, 0.0)
                hid2[slot, tap, z] = value.astype(BF)

    fin = r["fin"]

    def second_conv(z, at, n):
        mixed = sum(
            dot(w4t[slot, z], hid2[slot, :, :, :, at].reshape(6 * Q2, n)) for slot in range(2)
        ).astype(BF)
        return (raw2[0, 1, z, :, at].astype(F32) + mixed.astype(F32)).astype(BF)

    last = []
    for i in range(TILES):
        at = slice(i * 128, (i + 1) * 128)
        fin[0, :, at] = second_conv(oz, at, 128)
        there = out.at[:, lanes(zh * HALF2 + i * 128, 128)]
        last.append(send(fin.at[0, :, pl.ds(i * 128, 128)], there, zp))
    fin[1] = second_conv(zh, slice(0, HALF2), HALF2)
    kept = pltpu.make_async_copy(fin.at[1], out.at[:, lanes(zh * HALF2, HALF2)], local_sem.at[15])
    kept.start()
    for copy in last:
        copy.wait_recv()
    kept.wait()
    for copy in sent:
        copy.wait_send()


def per_device(frames, lat, tw1, g1, s1, dw, g2, s2, cw2, sw2, tb, tw2, g3, s3):
    far = pl.BlockSpec(memory_space=pl.ANY)
    row = lambda v: v.reshape(1, v.shape[0])
    result = pl.pallas_call(
        functools.partial(kernel, frames),
        out_shape=jax.ShapeDtypeStruct((Q2, POS2), BF),
        in_specs=[far] * 13,
        out_specs=far,
        scratch_shapes=[pltpu.VMEM(shape, dtype) for shape, dtype in SCRATCH.values()]
        + [
            pltpu.SemaphoreType.DMA((N_SEM,)),
            pltpu.SemaphoreType.DMA((N_SEM,)),
            pltpu.SemaphoreType.DMA((16,)),
        ],
        compiler_params=pltpu.CompilerParams(
            collective_id=0, has_side_effects=True, vmem_limit_bytes=56 * 2**20
        ),
        name="video_block",
    )(
        lat.reshape(Q1, H1 * W1),
        tw1.reshape(3 * C1, C1),
        row(g1),
        row(s1),
        dw.reshape(9 * Q1, C1),
        g2,
        s2,
        cw2.transpose(0, 2, 1).reshape(9 * Q2, C1),
        sw2.T,
        row(tb),
        tw2.reshape(3 * C2, C2),
        row(g3),
        row(s3),
    )
    return result.reshape(1, Q2, POS2)


def solution(mesh):
    return jax.shard_map(
        functools.partial(per_device, mesh.shape["frame"]),
        mesh=mesh,
        in_specs=(
            P(("video", "frame"), "chan", None),
            P(),
            P("chan"),
            P("chan"),
            P(None, "chan", None),
            P(),
            P(),
            P(None, None, "chan"),
            P(None, "chan"),
            P("chan"),
            P(),
            P("chan"),
            P("chan"),
        ),
        out_specs=P(("video", "frame"), "chan", None),
        check_vma=False,
    )
```

```python
import functools

import jax
import jax.numpy as jnp
from jax import lax
from jax.experimental import pallas as pl
from jax.experimental.pallas import tpu as pltpu
from jax.sharding import PartitionSpec as P

MESH = pl.DeviceIdType.MESH
BF = jnp.bfloat16
F32 = jnp.float32
C1 = 320
C2 = 640
GROUPS = 32
W1 = 128
H1 = 24
H2 = 12
W2 = 64
NX = 4
EPS = 1e-6

Q1 = C1 // 4
Q2 = C2 // 4
HALF1 = H1 * W1 // 2
WIN1 = HALF1 + W1
HALF2 = H2 * W2 // 2
POS2 = H2 * W2
DPAD = 768
DPART = DPAD // NX
TILES = HALF2 // 128
CHUNKS = ((0, 640), (640, 512), (1152, 512))

SCRATCH = {
    "lat_v": ((Q1, H1 * W1), BF),
    "tw1_v": ((3 * C1, C1), BF),
    "tw2_v": ((3 * C2, C2), BF),
    "cw2_v": ((9 * Q2, C1), BF),
    "sw2_v": ((Q2, C1), BF),
    "zsrc": ((Q1, WIN1), BF),
    "raw1": ((3, 2, Q1, WIN1), BF),
    "hid1": ((2, 3, 2, Q1, WIN1), BF),
    "tmp1": ((C1, 6 * Q1), BF),
    "w1t": ((2, 2 * Q1, 6 * Q1), BF),
    "blk": ((2 * Q1, WIN1), BF),
    "dwt": ((2, DPAD, C1), BF),
    "taps1": ((2, 9 * Q1, HALF2), BF),
    "part": ((C1, HALF2), F32),
    "part_rx": ((C1 // 2, HALF2), F32),
    "red": ((2, 2, C1 // 2, HALF2), BF),
    "nrm": ((C1, POS2 + 256), BF),
    "taps2": ((10 * C1, HALF2), BF),
    "taps2o": ((10 * C1, HALF2), BF),
    "w2t": ((Q2, 10 * C1), BF),
    "spat_o": ((Q2, HALF2), BF),
    "raw2": ((2, 3, 2, Q2, HALF2), BF),
    "hid2": ((2, 3, 2, Q2, HALF2), BF),
    "tmp2": ((C2, 6 * Q2), BF),
    "w4t": ((2, 2, Q2, 6 * Q2), BF),
    "pick1": ((256, 384), BF),
    "pick2": ((3, 256, 256), BF),
    "fin": ((2, Q2, HALF2), BF),
    "par": ((2, 2, 8, 256), F32),
    "par2": ((8, 384), F32),
    "g1_v": ((1, Q1), F32),
    "s1_v": ((1, Q1), F32),
    "g2_v": ((C1,), F32),
    "s2_v": ((C1,), F32),
    "g3_v": ((1, Q2), F32),
    "s3_v": ((1, Q2), F32),
    "tb_v": ((1, Q2), F32),
    "st_tx": ((6, 1, 128), F32),
    "st_rx": ((32, 1, 128), F32),
}
N_SEM = 128


def dot(a, b):
    return lax.dot_general(a, b, (((1,), (0,)), ((), ())), preferred_element_type=F32)


def silu_of_half(w):
    return w + w * jnp.tanh(w)


def to_columns(rows):
    return jnp.concatenate([rows] * (128 // rows.shape[0]), axis=0).T


def one_hots(chan, size):
    lane = lax.broadcasted_iota(jnp.int32, (chan.shape[0], 128), 1) * size
    off = GROUPS * size
    first = (lane <= chan) & (chan < lane + size)
    second = (lane - off <= chan) & (chan < lane - off + size)
    return first, second


def group_row(sums, squares, chan, size):
    first, second = one_hots(chan, size)
    spread = jnp.where(first, sums, 0.0) + jnp.where(second, squares, 0.0)
    return jnp.sum(spread, axis=0, keepdims=True)


def scale_columns(row, count, chan, size, gain, shift):
    first, second = one_hots(chan, size)
    mean = jnp.sum(jnp.where(first, row, 0.0), axis=1, keepdims=True) / count
    square = jnp.sum(jnp.where(second, row, 0.0), axis=1, keepdims=True) / count
    scale = lax.rsqrt(square - mean * mean + EPS) * gain
    return 0.5 * scale, 0.5 * (shift - mean * scale)


def kernel(frames, *refs):
    (lat, tw1, g1, s1, dw, g2, s2, cw2, sw2, tb, tw2, g3, s3, out) = refs[:14]
    names = list(SCRATCH)
    r = dict(zip(names, refs[14 : 14 + len(names)]))
    send_sem, recv_sem, local_sem = refs[14 + len(names) :]
    ny = frames // NX
    f = lax.axis_index("frame")
    c = lax.axis_index("chan")
    x, y = f // ny, lax.rem(f, ny)
    zh, k = c // 2, lax.rem(c, 2)
    oz, ok = 1 - zh, 1 - k
    zp = {"chan": lax.rem(c + 2, 4)}
    kp = {"chan": c + 1 - 2 * k}
    after = {"frame": lax.rem(f + 1, frames)}
    before = {"frame": lax.rem(f + frames - 1, frames)}
    x_peers = [{"frame": lax.rem(x + d, NX) * ny + y} for d in range(1, NX)]
    y_peers = [{"frame": x * ny + lax.rem(y + d, ny)} for d in range(1, ny)]

    xz_peers = [
        {"frame": lax.rem(x + d, NX) * ny + y, "chan": lax.rem(c + e, 4)}
        for d in range(NX)
        for e in (0, 2)
        if d or e
    ]
    y_pair = {"frame": x * ny + y + 1 - 2 * lax.rem(y, 2)}

    barrier = pltpu.get_barrier_semaphore()
    greeted = xz_peers + y_peers + [kp, after, before]
    for peer in greeted:
        pl.semaphore_signal(barrier, inc=1, device_id=peer, device_id_type=MESH)

    loads = {}
    for number, (name, ref, dst) in enumerate(
        (
            ("lat", lat, r["lat_v"]),
            ("dw", dw, r["dwt"].at[zh, pl.ds(0, 9 * Q1)]),
            ("g1", g1, r["g1_v"]),
            ("s1", s1, r["s1_v"]),
            ("g2", g2, r["g2_v"]),
            ("s2", s2, r["s2_v"]),
            ("g3", g3, r["g3_v"]),
            ("s3", s3, r["s3_v"]),
            ("tb", tb, r["tb_v"]),
            ("tw1", tw1, r["tw1_v"]),
            ("cw2", cw2, r["cw2_v"]),
            ("sw2", sw2, r["sw2_v"]),
            ("tw2", tw2, r["tw2_v"]),
        )
    ):
        loads[name] = pltpu.make_async_copy(ref, dst, local_sem.at[number])
        loads[name].start()

    counter = [0]
    sent = []

    def send(src, dst, peer):
        number = counter[0]
        counter[0] += 1
        copy = pltpu.make_async_remote_copy(
            src_ref=src,
            dst_ref=dst,
            send_sem=send_sem.at[number],
            recv_sem=recv_sem.at[number],
            device_id=peer,
            device_id_type=MESH,
        )
        copy.start()
        sent.append(copy)
        return copy

    def lanes(start, size):
        return pl.ds(pl.multiple_of(start, 128), size)

    st_tx, st_rx = r["st_tx"], r["st_rx"]
    stat_slot = [0, 0]

    def stat_send(row, peers):
        tx, rx = stat_slot
        stat_slot[0] += 1
        stat_slot[1] += len(peers)
        st_tx[tx] = row
        return [send(st_tx.at[tx], st_rx.at[rx + i], p) for i, p in enumerate(peers)], tx, rx

    def stat_wait(state):
        copies, tx, rx = state
        total = st_tx[tx]
        for i, copy in enumerate(copies):
            copy.wait_recv()
            total = total + st_rx[rx + i]
        return total

    raw1, raw2 = r["raw1"], r["raw2"]
    lat_v = r["lat_v"]

    par = r["par"]
    loads["lat"].wait()
    zsrc = r["zsrc"]
    raw1[1, zh, :, 0:W1] = lat_v[:, HALF1 - W1 : HALF1]
    raw1[1, zh, :, W1:WIN1] = lat_v[:, lanes(zh * HALF1, HALF1)]
    zsrc[:, 0:W1] = lat_v[:, HALF1 - W1 : HALF1]
    zsrc[:, W1:WIN1] = lat_v[:, lanes(oz * HALF1, HALF1)]
    wide = lat_v[...].astype(F32)
    q1_iota = lax.broadcasted_iota(jnp.int32, (Q1, 1), 0)
    row1 = group_row(
        jnp.sum(wide, axis=1, keepdims=True),
        jnp.sum(wide * wide, axis=1, keepdims=True),
        q1_iota + c * Q1,
        C1 // GROUPS,
    )
    dwt = r["dwt"]
    for name in ("dw", "g1", "s1", "g2", "s2", "g3", "s3", "tb"):
        loads[name].wait()
    par[0, zh, 0:1, 0:Q1] = r["g1_v"][...]
    par[0, zh, 1:2, 0:Q1] = r["s1_v"][...]
    par[0, zh, 2:3, 0:Q2] = r["g3_v"][...]
    par[0, zh, 3:4, 0:Q2] = r["s3_v"][...]
    par[0, zh, 4:5, 0:Q2] = r["tb_v"][...]
    r["par2"][0:1, 0:C1] = r["g2_v"][...].reshape(1, C1)
    r["par2"][1:2, 0:C1] = r["s2_v"][...].reshape(1, C1)
    dwt[zh, 9 * Q1 : DPAD, :] = jnp.zeros((DPAD - 9 * Q1, C1), BF)
    pl.semaphore_wait(barrier, len(greeted))

    state = stat_send(row1, xz_peers)
    piece = DPART // 2
    own_piece = pl.ds(pl.multiple_of(x * DPART + lax.rem(y, 2) * piece, 16), piece)
    pair_piece = pl.ds(pl.multiple_of(x * DPART + lax.rem(y + 1, 2) * piece, 16), piece)
    dw_z = send(dwt.at[zh, own_piece], dwt.at[zh, own_piece], zp)

    z_copies = [
        send(zsrc.at[:, pl.ds(a, n)], raw1.at[1, zh, :, pl.ds(a, n)], zp) for a, n in CHUNKS
    ]

    def to_frames(raw, z, a, n):
        here = raw.at[1, z, :, pl.ds(a, n)]
        return [
            send(here, raw.at[0, z, :, pl.ds(a, n)], after),
            send(here, raw.at[2, z, :, pl.ds(a, n)], before),
        ]

    y_own = [to_frames(raw1, zh, a, n) for a, n in CHUNKS]
    par_copy = send(par.at[0, zh], par.at[0, zh], zp)

    def prepare(weight, held, store, width, count, slot, core):
        rows = [
            weight[pl.ds(pl.multiple_of(t * width + z * 2 * count + core * count, 16), count), :]
            for t in range(3)
            for z in range(2)
        ]
        held[...] = jnp.concatenate(rows, axis=0).T
        for z in range(2):
            store(slot, z, held[pl.ds(pl.multiple_of(z * 2 * count + k * count, 16), count), :])

    w1t, w4t, w2t = r["w1t"], r["w4t"], r["w2t"]

    def store1(slot, z, value):
        w1t[slot, z * Q1 : (z + 1) * Q1, :] = value

    def store4(slot, z, value):
        w4t[slot, z] = value

    loads["tw1"].wait()
    for slot, core in ((0, k), (1, ok)):
        prepare(r["tw1_v"], r["tmp1"], store1, C1, Q1, slot, core)

    src = lax.broadcasted_iota(jnp.int32, (256, 128), 0)
    dst = lax.broadcasted_iota(jnp.int32, (256, 128), 1)
    same = (src >= 128) == (dst >= 64)
    src_col = src - jnp.where(src >= 128, 128, 0)
    dst_col = dst - jnp.where(dst >= 64, 64, 0)
    for dx in range(3):
        r["pick1"][:, dx * 128 : (dx + 1) * 128] = jnp.where(
            same & (src_col == 2 * dst_col + dx - 1), 1.0, 0.0
        ).astype(BF)

    src = lax.broadcasted_iota(jnp.int32, (256, 256), 0)
    dst = lax.broadcasted_iota(jnp.int32, (256, 256), 1)
    second = dst >= 128
    lane = dst - jnp.where(second, 128, 0)
    upper = lane >= 64
    col = lane - jnp.where(upper, 64, 0)
    base = jnp.where(second, 128, 64) + jnp.where(upper, 64, 0)
    for dx in range(3):
        want = col + (dx - 1)
        keep = (want >= 0) & (want < W2) & (src == base + want)
        r["pick2"][dx] = jnp.where(keep, 1.0, 0.0).astype(BF)
    loads["cw2"].wait()
    loads["sw2"].wait()
    for t in range(9):
        w2t[:, t * C1 : (t + 1) * C1] = r["cw2_v"][t * Q2 : (t + 1) * Q2, :]
    w2t[:, 9 * C1 : 10 * C1] = r["sw2_v"][...]
    dw_z.wait_recv()
    here = dwt.at[oz, own_piece]
    dw_y = send(here, here, y_pair)
    dw_x = [send(here, here, p) for p in x_peers]
    state = stat_send(stat_wait(state), y_peers)
    y_fwd = []

    def forward(i):
        z_copies[i].wait_recv()
        y_fwd.append(to_frames(raw1, oz, *CHUNKS[i]))

    forward(0)
    dw_y.wait_recv()
    there = dwt.at[oz, pair_piece]
    dw_x += [send(there, there, p) for p in x_peers]
    forward(1)
    loads["tw2"].wait()
    for slot, core in ((0, k), (1, ok)):
        prepare(r["tw2_v"], r["tmp2"], store4, C2, Q2, slot, core)
    par_copy.wait_recv()
    par_k = send(par.at[0], par.at[1], kp)
    state = stat_send(stat_wait(state), [kp])
    cols = [to_columns(par[0, z]) for z in range(2)]
    cols2 = to_columns(r["par2"][...])
    bias = jnp.where(zh == 0, cols[0][0:Q2, 4:5], cols[1][0:Q2, 4:5])
    total = stat_wait(state)
    affine1 = [
        scale_columns(
            total,
            float(C1 // GROUPS * H1 * W1 * frames),
            q1_iota + (2 * z + k) * Q1,
            C1 // GROUPS,
            cols[z][0:Q1, 0:1],
            cols[z][0:Q1, 1:2],
        )
        for z in range(2)
    ]
    hid1 = r["hid1"]
    alive = {0: f > 0, 2: f < frames - 1}

    def pick(pair, z):
        return [jnp.where(z == 0, pair[0][i], pair[1][i]) for i in range(2)]

    def hidden(raw, hid, z, affine, a, n, waits):
        span = slice(a, a + n)
        scale, shift = pick(affine, z)
        for tap in (1, 0, 2):
            if tap != 1:
                waits[tap // 2].wait_recv()
            value = silu_of_half(raw[tap, z, :, span].astype(F32) * scale + shift)
            if tap != 1:
                value = jnp.where(alive[tap], value, 0.0)
            hid[0, tap, z, :, span] = value.astype(BF)
        return send(hid.at[0, :, z, :, pl.ds(a, n)], hid.at[1, :, z, :, pl.ds(a, n)], kp)

    blk, taps1 = r["blk"], r["taps1"]
    part, part_rx, red = r["part"], r["part_rx"], r["red"]
    half = C1 // 2
    k1, part_k, red_z, red_k = {}, {}, {}, {}

    def hid_own(i):
        k1[i] = [hidden(raw1, hid1, zh, affine1, *CHUNKS[i], y_own[i])]

    def hid_other(i):
        k1[i].append(hidden(raw1, hid1, oz, affine1, *CHUNKS[i], y_fwd[i]))

    def first_conv(i):
        a, n = CHUNKS[i]
        span = slice(a, a + n)
        for copy in k1[i]:
            copy.wait_recv()
        mixed = sum(
            dot(w1t[slot], hid1[slot, :, :, :, span].reshape(6 * Q1, n)) for slot in range(2)
        ).astype(BF)
        value = raw1[1, :, :, span].reshape(2 * Q1, n).astype(F32) + mixed.astype(F32)
        if i == 0:
            blk[:, 0:W1] = jnp.where(zh == 0, 0.0, value[:, 0:W1]).astype(BF)
            blk[:, W1:n] = value[:, W1:].astype(BF)
        else:
            blk[:, span] = value.astype(BF)
        at = slice(i * 128, (i + 1) * 128)
        for dy in range(3):
            top = (4 * i + dy) * W1
            pair = jnp.concatenate(
                [blk[:, top : top + W1], blk[:, top + 2 * W1 : top + 3 * W1]], axis=1
            )
            got = dot(pair, r["pick1"][...]).astype(BF)
            for dx in range(3):
                t = 3 * dy + dx
                for z in range(2):
                    taps1[z, t * Q1 : (t + 1) * Q1, at] = got[
                        z * Q1 : (z + 1) * Q1, dx * 128 : (dx + 1) * 128
                    ]

    def down(i):
        at = slice(i * 128, (i + 1) * 128)
        part[:, at] = sum(
            lax.dot_general(
                dwt[z, 0 : 9 * Q1, :],
                taps1[z, :, at],
                (((0,), (0,)), ((), ())),
                preferred_element_type=F32,
            )
            for z in range(2)
        )
        part_k[i] = send(
            part.at[pl.ds(pl.multiple_of(ok * half, 16), half), pl.ds(i * 128, 128)],
            part_rx.at[:, pl.ds(i * 128, 128)],
            kp,
        )

    def reduced(i):
        at = slice(i * 128, (i + 1) * 128)
        part_k[i].wait_recv()
        mine = part[pl.ds(pl.multiple_of(k * half, 16), half), at]
        red[k, zh, :, at] = (mine + part_rx[:, at]).astype(BF)
        here = red.at[k, zh, :, pl.ds(i * 128, 128)]
        red_z[i] = send(here, here, zp)
        red_k[i] = [send(here, here, kp)]

    def pass_reduced(i):
        red_z[i].wait_recv()
        here = red.at[k, oz, :, pl.ds(i * 128, 128)]
        red_k[i].append(send(here, here, kp))

    for i in range(3):
        hid_own(i)
    forward(2)
    hid_other(0)
    hid_other(1)
    first_conv(0)
    for copy in dw_x:
        copy.wait_recv()
    down(0)
    first_conv(1)
    down(1)
    reduced(0)
    hid_other(2)
    reduced(1)
    first_conv(2)
    down(2)
    reduced(2)
    for i in range(3):
        pass_reduced(i)
    for i in range(3):
        for copy in red_k[i]:
            copy.wait_recv()

    nrm = r["nrm"]
    nrm[:, 0:128] = jnp.zeros((C1, 128), BF)
    nrm[:, 128 + POS2 :] = jnp.zeros((C1, 128), BF)
    half_iota = lax.broadcasted_iota(jnp.int32, (half, 1), 0)
    for core in range(2):
        sides = [red[core, z] for z in range(2)]
        wide = jnp.concatenate(sides, axis=1).astype(F32)
        chan = half_iota + core * half
        row2 = group_row(
            jnp.sum(wide, axis=1, keepdims=True),
            jnp.sum(wide * wide, axis=1, keepdims=True),
            chan,
            C1 // GROUPS,
        )
        span = slice(core * half, (core + 1) * half)
        scale, shift = scale_columns(
            row2, float(C1 // GROUPS * POS2), chan, C1 // GROUPS, cols2[span, 0:1], cols2[span, 1:2]
        )
        nrm[span, 128 : 128 + POS2] = silu_of_half(wide * scale + shift).astype(BF)

    def second(side, taps):
        for dx in range(3):
            for j in range(TILES + 1):
                window = nrm[:, lanes(side * HALF2 + j * 128, 256)]
                got = dot(window, r["pick2"][dx]).astype(BF)
                if j < TILES:
                    at = slice(j * 128, (j + 1) * 128)
                    taps[dx * C1 : (dx + 1) * C1, at] = got[:, 0:128]
                    taps[(3 + dx) * C1 : (4 + dx) * C1, at] = got[:, 128:256]
                if j > 0:
                    at = slice((j - 1) * 128, j * 128)
                    taps[(6 + dx) * C1 : (7 + dx) * C1, at] = got[:, 0:128]
        for core in range(2):
            taps[9 * C1 + core * half : 9 * C1 + (core + 1) * half, :] = red[core, side]

    spat_o = r["spat_o"]
    second(oz, r["taps2o"])
    z2 = []
    for i in range(TILES):
        at = slice(i * 128, (i + 1) * 128)
        spat_o[:, at] = (dot(w2t[...], r["taps2o"][:, at]) + bias).astype(BF)
        here = pl.ds(i * 128, 128)
        z2.append(send(spat_o.at[:, here], raw2.at[0, 1, zh, :, here], zp))
    second(zh, r["taps2"])
    raw2[0, 1, zh] = (dot(w2t[...], r["taps2"][...]) + bias).astype(BF)
    own = raw2.at[0]
    y2_own = to_frames(own, zh, 0, HALF2)
    raw_k = [send(raw2.at[0, 1, zh], raw2.at[1, 1, zh], kp)]
    wide = jnp.concatenate([raw2[0, 1, zh], spat_o[...]], axis=1).astype(F32)
    q2_iota = lax.broadcasted_iota(jnp.int32, (Q2, 1), 0)
    row3 = group_row(
        jnp.sum(wide, axis=1, keepdims=True),
        jnp.sum(wide * wide, axis=1, keepdims=True),
        q2_iota + c * Q2,
        C2 // GROUPS,
    )
    state = stat_send(row3, xz_peers)
    par_k.wait_recv()
    cols3 = [cols, [to_columns(par[1, z]) for z in range(2)]]
    y2_fwd = []

    def share(tap, z, a, n):
        here = pl.ds(a, n)
        raw_k.append(send(raw2.at[0, tap, z, :, here], raw2.at[1, tap, z, :, here], kp))

    def forward2(i):
        z2[i].wait_recv()
        y2_fwd.append(to_frames(own, oz, i * 128, 128))
        share(1, oz, i * 128, 128)

    for tap in (0, 2):
        y2_own[tap // 2].wait_recv()
        share(tap, zh, 0, HALF2)
    state = stat_send(stat_wait(state), y_peers)
    for i in range(TILES):
        forward2(i)
    state = stat_send(stat_wait(state), [kp])
    for i in range(TILES):
        for tap in (0, 2):
            y2_fwd[i][tap // 2].wait_recv()
            share(tap, oz, i * 128, 128)
    total = stat_wait(state)
    hid2 = r["hid2"]
    for slot, core in ((0, k), (1, ok)):
        if slot == 1:
            for copy in raw_k:
                copy.wait_recv()
        for z in range(2):
            scale, shift = scale_columns(
                total,
                float(C2 // GROUPS * POS2 * frames),
                q2_iota + (2 * z + core) * Q2,
                C2 // GROUPS,
                cols3[slot][z][0:Q2, 2:3],
                cols3[slot][z][0:Q2, 3:4],
            )
            for tap in range(3):
                value = silu_of_half(raw2[slot, tap, z].astype(F32) * scale + shift)
                if tap != 1:
                    value = jnp.where(alive[tap], value, 0.0)
                hid2[slot, tap, z] = value.astype(BF)

    fin = r["fin"]

    def second_conv(z, at, n):
        mixed = sum(
            dot(w4t[slot, z], hid2[slot, :, :, :, at].reshape(6 * Q2, n)) for slot in range(2)
        ).astype(BF)
        return (raw2[0, 1, z, :, at].astype(F32) + mixed.astype(F32)).astype(BF)

    last = []
    for i in range(TILES):
        at = slice(i * 128, (i + 1) * 128)
        fin[0, :, at] = second_conv(oz, at, 128)
        there = out.at[:, lanes(zh * HALF2 + i * 128, 128)]
        last.append(send(fin.at[0, :, pl.ds(i * 128, 128)], there, zp))
    fin[1] = second_conv(zh, slice(0, HALF2), HALF2)
    kept = pltpu.make_async_copy(fin.at[1], out.at[:, lanes(zh * HALF2, HALF2)], local_sem.at[15])
    kept.start()
    for copy in last:
        copy.wait_recv()
    kept.wait()
    for copy in sent:
        copy.wait_send()


def per_device(frames, lat, tw1, g1, s1, dw, g2, s2, cw2, sw2, tb, tw2, g3, s3):
    far = pl.BlockSpec(memory_space=pl.ANY)
    row = lambda v: v.reshape(1, v.shape[0])
    result = pl.pallas_call(
        functools.partial(kernel, frames),
        out_shape=jax.ShapeDtypeStruct((Q2, POS2), BF),
        in_specs=[far] * 13,
        out_specs=far,
        scratch_shapes=[pltpu.VMEM(shape, dtype) for shape, dtype in SCRATCH.values()]
        + [
            pltpu.SemaphoreType.DMA((N_SEM,)),
            pltpu.SemaphoreType.DMA((N_SEM,)),
            pltpu.SemaphoreType.DMA((16,)),
        ],
        compiler_params=pltpu.CompilerParams(
            collective_id=0, has_side_effects=True, vmem_limit_bytes=56 * 2**20
        ),
        name="video_block",
    )(
        lat.reshape(Q1, H1 * W1),
        tw1.reshape(3 * C1, C1),
        row(g1),
        row(s1),
        dw.reshape(9 * Q1, C1),
        g2,
        s2,
        cw2.transpose(0, 2, 1).reshape(9 * Q2, C1),
        sw2.T,
        row(tb),
        tw2.reshape(3 * C2, C2),
        row(g3),
        row(s3),
    )
    return result.reshape(1, Q2, POS2)


def solution(mesh):
    return jax.shard_map(
        functools.partial(per_device, mesh.shape["frame"]),
        mesh=mesh,
        in_specs=(
            P(("video", "frame"), "chan", None),
            P(),
            P("chan"),
            P("chan"),
            P(None, "chan", None),
            P(),
            P(),
            P(None, None, "chan"),
            P(None, "chan"),
            P("chan"),
            P(),
            P("chan"),
            P("chan"),
        ),
        out_specs=P(("video", "frame"), "chan", None),
        check_vma=False,
    )
```

```python
import functools

import jax
import jax.numpy as jnp
from jax import lax
from jax.experimental import pallas as pl
from jax.experimental.pallas import tpu as pltpu
from jax.sharding import PartitionSpec as P

MESH = pl.DeviceIdType.MESH
BF = jnp.bfloat16
F32 = jnp.float32
C1 = 320
C2 = 640
GROUPS = 32
W1 = 128
H1 = 24
H2 = 12
W2 = 64
NX = 4
EPS = 1e-6

Q1 = C1 // 4
Q2 = C2 // 4
HALF1 = H1 * W1 // 2
WIN1 = HALF1 + W1
HALF2 = H2 * W2 // 2
POS2 = H2 * W2
DPAD = 768
DPART = DPAD // NX
TILES = HALF2 // 128
CHUNKS = ((0, 640), (640, 512), (1152, 512))
CHUNKS2 = ((0, 384), (384, 256), (640, 128))

SCRATCH = {
    "lat_v": ((Q1, H1 * W1), BF),
    "tw1_v": ((3 * C1, C1), BF),
    "tw2_v": ((3 * C2, C2), BF),
    "cw2_v": ((9 * Q2, C1), BF),
    "sw2_v": ((Q2, C1), BF),
    "zsrc": ((Q1, WIN1), BF),
    "raw1": ((3, 2, Q1, WIN1), BF),
    "hid1": ((2, 3, 2, Q1, WIN1), BF),
    "tmp1": ((C1, 6 * Q1), BF),
    "w1t": ((2, 2 * Q1, 6 * Q1), BF),
    "blk": ((2 * Q1, WIN1), BF),
    "dwt": ((2, DPAD, C1), BF),
    "taps1": ((2, 9 * Q1, HALF2), BF),
    "part": ((C1, HALF2), F32),
    "part_rx": ((C1 // 2, HALF2), F32),
    "red": ((2, 2, C1 // 2, HALF2), BF),
    "nrm": ((C1, POS2 + 256), BF),
    "taps2": ((10 * C1, HALF2), BF),
    "w2t": ((Q2, 10 * C1), BF),
    "raw2": ((2, 3, 2, Q2, POS2), BF),
    "hid2": ((2, 3, 2, Q2, POS2), BF),
    "tmp2": ((C2, 6 * Q2), BF),
    "w4t": ((2, Q2, 6 * Q2), BF),
    "pick1": ((256, 384), BF),
    "pick2": ((3, 256, 256), BF),
    "fin": ((Q2, POS2), BF),
    "par": ((2, 2, 8, 256), F32),
    "par2": ((8, 384), F32),
    "g1_v": ((1, Q1), F32),
    "s1_v": ((1, Q1), F32),
    "g2_v": ((C1,), F32),
    "s2_v": ((C1,), F32),
    "g3_v": ((1, Q2), F32),
    "s3_v": ((1, Q2), F32),
    "tb_v": ((1, Q2), F32),
    "st_tx": ((6, 1, 128), F32),
    "st_rx": ((32, 1, 128), F32),
}
N_SEM = 128


def dot(a, b):
    return lax.dot_general(a, b, (((1,), (0,)), ((), ())), preferred_element_type=F32)


def silu_of_half(w):
    return w + w * jnp.tanh(w)


def to_columns(rows):
    return jnp.concatenate([rows] * (128 // rows.shape[0]), axis=0).T


def one_hots(chan, size):
    lane = lax.broadcasted_iota(jnp.int32, (chan.shape[0], 128), 1) * size
    off = GROUPS * size
    first = (lane <= chan) & (chan < lane + size)
    second = (lane - off <= chan) & (chan < lane - off + size)
    return first, second


def group_row(sums, squares, chan, size):
    first, second = one_hots(chan, size)
    spread = jnp.where(first, sums, 0.0) + jnp.where(second, squares, 0.0)
    return jnp.sum(spread, axis=0, keepdims=True)


def scale_columns(row, count, chan, size, gain, shift):
    first, second = one_hots(chan, size)
    mean = jnp.sum(jnp.where(first, row, 0.0), axis=1, keepdims=True) / count
    square = jnp.sum(jnp.where(second, row, 0.0), axis=1, keepdims=True) / count
    scale = lax.rsqrt(square - mean * mean + EPS) * gain
    return 0.5 * scale, 0.5 * (shift - mean * scale)


def kernel(frames, *refs):
    (lat, tw1, g1, s1, dw, g2, s2, cw2, sw2, tb, tw2, g3, s3, out) = refs[:14]
    names = list(SCRATCH)
    r = dict(zip(names, refs[14 : 14 + len(names)]))
    send_sem, recv_sem, local_sem = refs[14 + len(names) :]
    ny = frames // NX
    f = lax.axis_index("frame")
    c = lax.axis_index("chan")
    x, y = f // ny, lax.rem(f, ny)
    zh, k = c // 2, lax.rem(c, 2)
    oz, ok = 1 - zh, 1 - k
    zp = {"chan": lax.rem(c + 2, 4)}
    kp = {"chan": c + 1 - 2 * k}
    after = {"frame": lax.rem(f + 1, frames)}
    before = {"frame": lax.rem(f + frames - 1, frames)}
    chan_peers = [{"chan": lax.rem(c + d, 4)} for d in range(1, 4)]
    x_peers = [{"frame": lax.rem(x + d, NX) * ny + y} for d in range(1, NX)]
    y_peers = [{"frame": x * ny + lax.rem(y + d, ny)} for d in range(1, ny)]

    xz_peers = [
        {"frame": lax.rem(x + d, NX) * ny + y, "chan": lax.rem(c + e, 4)}
        for d in range(NX)
        for e in (0, 2)
        if d or e
    ]

    barrier = pltpu.get_barrier_semaphore()
    greeted = chan_peers + xz_peers + y_peers + [after, before]
    for peer in greeted:
        pl.semaphore_signal(barrier, inc=1, device_id=peer, device_id_type=MESH)

    loads = {}
    for number, (name, ref, dst) in enumerate(
        (
            ("lat", lat, r["lat_v"]),
            ("dw", dw, r["dwt"].at[zh, pl.ds(0, 9 * Q1)]),
            ("g1", g1, r["g1_v"]),
            ("s1", s1, r["s1_v"]),
            ("g2", g2, r["g2_v"]),
            ("s2", s2, r["s2_v"]),
            ("g3", g3, r["g3_v"]),
            ("s3", s3, r["s3_v"]),
            ("tb", tb, r["tb_v"]),
            ("tw1", tw1, r["tw1_v"]),
            ("cw2", cw2, r["cw2_v"]),
            ("sw2", sw2, r["sw2_v"]),
            ("tw2", tw2, r["tw2_v"]),
        )
    ):
        loads[name] = pltpu.make_async_copy(ref, dst, local_sem.at[number])
        loads[name].start()

    counter = [0]
    sent = []

    def send(src, dst, peer):
        number = counter[0]
        counter[0] += 1
        copy = pltpu.make_async_remote_copy(
            src_ref=src,
            dst_ref=dst,
            send_sem=send_sem.at[number],
            recv_sem=recv_sem.at[number],
            device_id=peer,
            device_id_type=MESH,
        )
        copy.start()
        sent.append(copy)
        return copy

    def lanes(start, size):
        return pl.ds(pl.multiple_of(start, 128), size)

    st_tx, st_rx = r["st_tx"], r["st_rx"]
    stat_slot = [0, 0]

    def stat_send(row, peers):
        tx, rx = stat_slot
        stat_slot[0] += 1
        stat_slot[1] += len(peers)
        st_tx[tx] = row
        return [send(st_tx.at[tx], st_rx.at[rx + i], p) for i, p in enumerate(peers)], tx, rx

    def stat_wait(state):
        copies, tx, rx = state
        total = st_tx[tx]
        for i, copy in enumerate(copies):
            copy.wait_recv()
            total = total + st_rx[rx + i]
        return total

    raw1, raw2 = r["raw1"], r["raw2"]
    lat_v = r["lat_v"]

    par = r["par"]
    loads["lat"].wait()
    zsrc = r["zsrc"]
    raw1[1, zh, :, 0:W1] = lat_v[:, HALF1 - W1 : HALF1]
    raw1[1, zh, :, W1:WIN1] = lat_v[:, lanes(zh * HALF1, HALF1)]
    zsrc[:, 0:W1] = lat_v[:, HALF1 - W1 : HALF1]
    zsrc[:, W1:WIN1] = lat_v[:, lanes(oz * HALF1, HALF1)]
    wide = lat_v[...].astype(F32)
    q1_iota = lax.broadcasted_iota(jnp.int32, (Q1, 1), 0)
    row1 = group_row(
        jnp.sum(wide, axis=1, keepdims=True),
        jnp.sum(wide * wide, axis=1, keepdims=True),
        q1_iota + c * Q1,
        C1 // GROUPS,
    )
    dwt = r["dwt"]
    for name in ("dw", "g1", "s1", "g2", "s2", "g3", "s3", "tb"):
        loads[name].wait()
    par[0, zh, 0:1, 0:Q1] = r["g1_v"][...]
    par[0, zh, 1:2, 0:Q1] = r["s1_v"][...]
    par[0, zh, 2:3, 0:Q2] = r["g3_v"][...]
    par[0, zh, 3:4, 0:Q2] = r["s3_v"][...]
    par[0, zh, 4:5, 0:Q2] = r["tb_v"][...]
    r["par2"][0:1, 0:C1] = r["g2_v"][...].reshape(1, C1)
    r["par2"][1:2, 0:C1] = r["s2_v"][...].reshape(1, C1)
    dwt[zh, 9 * Q1 : DPAD, :] = jnp.zeros((DPAD - 9 * Q1, C1), BF)
    pl.semaphore_wait(barrier, len(greeted))

    state = stat_send(row1, chan_peers)
    pieces = 2
    piece = DPART // pieces
    own_piece = pl.ds(pl.multiple_of(x * DPART + lax.rem(y, 2) * piece, 16), piece)
    dw_z = send(dwt.at[zh, own_piece], dwt.at[zh, own_piece], zp)

    z_copies = [
        send(zsrc.at[:, pl.ds(a, n)], raw1.at[1, zh, :, pl.ds(a, n)], zp) for a, n in CHUNKS
    ]

    def to_frames(raw, z, a, n):
        here = raw.at[1, z, :, pl.ds(a, n)]
        return [
            send(here, raw.at[0, z, :, pl.ds(a, n)], after),
            send(here, raw.at[2, z, :, pl.ds(a, n)], before),
        ]

    y_own = [to_frames(raw1, zh, a, n) for a, n in CHUNKS]
    par_copy = send(par.at[0, zh], par.at[0, zh], zp)

    def prepare(weight, held, width, count, core):
        rows = [
            weight[pl.ds(pl.multiple_of(t * width + z * 2 * count + core * count, 16), count), :]
            for t in range(3)
            for z in range(2)
        ]
        held[...] = jnp.concatenate(rows, axis=0).T

    w1t, w4t, w2t = r["w1t"], r["w4t"], r["w2t"]

    loads["tw1"].wait()
    for slot, core in ((0, k), (1, ok)):
        prepare(r["tw1_v"], r["tmp1"], C1, Q1, core)
        for z in range(2):
            w1t[slot, z * Q1 : (z + 1) * Q1, :] = r["tmp1"][
                pl.ds(pl.multiple_of((2 * z + k) * Q1, 16), Q1), :
            ]

    src = lax.broadcasted_iota(jnp.int32, (256, 128), 0)
    dst = lax.broadcasted_iota(jnp.int32, (256, 128), 1)
    same = (src >= 128) == (dst >= 64)
    src_col = src - jnp.where(src >= 128, 128, 0)
    dst_col = dst - jnp.where(dst >= 64, 64, 0)
    for dx in range(3):
        r["pick1"][:, dx * 128 : (dx + 1) * 128] = jnp.where(
            same & (src_col == 2 * dst_col + dx - 1), 1.0, 0.0
        ).astype(BF)

    state = stat_send(stat_wait(state), x_peers)
    dw_z.wait_recv()
    here = dwt.at[oz, own_piece]
    dw_y = [
        send(here, here, {"frame": x * ny + y + 1 - 2 * lax.rem(y, 2)}) for d in range(1, pieces)
    ]
    dw_x = [send(here, here, p) for p in x_peers]

    src = lax.broadcasted_iota(jnp.int32, (256, 256), 0)
    dst = lax.broadcasted_iota(jnp.int32, (256, 256), 1)
    second = dst >= 128
    lane = dst - jnp.where(second, 128, 0)
    upper = lane >= 64
    col = lane - jnp.where(upper, 64, 0)
    base = jnp.where(second, 128, 64) + jnp.where(upper, 64, 0)
    for dx in range(3):
        want = col + (dx - 1)
        keep = (want >= 0) & (want < W2) & (src == base + want)
        r["pick2"][dx] = jnp.where(keep, 1.0, 0.0).astype(BF)
    loads["cw2"].wait()
    loads["sw2"].wait()
    for t in range(9):
        w2t[:, t * C1 : (t + 1) * C1] = r["cw2_v"][t * Q2 : (t + 1) * Q2, :]
    w2t[:, 9 * C1 : 10 * C1] = r["sw2_v"][...]
    y_fwd = []

    def forward(i):
        z_copies[i].wait_recv()
        y_fwd.append(to_frames(raw1, oz, *CHUNKS[i]))

    forward(0)
    state = stat_send(stat_wait(state), y_peers)
    for d in range(1, pieces):
        dw_y[d - 1].wait_recv()
        start = x * DPART + lax.rem(y + 1, 2) * piece
        there = dwt.at[oz, pl.ds(pl.multiple_of(start, 16), piece)]
        dw_x += [send(there, there, p) for p in x_peers]
    forward(1)
    loads["tw2"].wait()
    for slot, core in ((0, k), (1, ok)):
        prepare(r["tw2_v"], r["tmp2"], C2, Q2, core)
        w4t[slot] = r["tmp2"][pl.ds(pl.multiple_of(c * Q2, 16), Q2), :]
    par_copy.wait_recv()
    par_k = send(par.at[0], par.at[1], kp)
    cols = [to_columns(par[0, z]) for z in range(2)]
    cols2 = to_columns(r["par2"][...])
    bias = jnp.where(zh == 0, cols[0][0:Q2, 4:5], cols[1][0:Q2, 4:5])
    total = stat_wait(state)
    affine1 = [
        scale_columns(
            total,
            float(C1 // GROUPS * H1 * W1 * frames),
            q1_iota + (2 * z + k) * Q1,
            C1 // GROUPS,
            cols[z][0:Q1, 0:1],
            cols[z][0:Q1, 1:2],
        )
        for z in range(2)
    ]
    hid1 = r["hid1"]
    alive = {0: f > 0, 2: f < frames - 1}

    def pick(pair, z):
        return [jnp.where(z == 0, pair[0][i], pair[1][i]) for i in range(2)]

    def hidden(raw, hid, z, affine, a, n, waits):
        span = slice(a, a + n)
        scale, shift = pick(affine, z)
        for tap in (1, 0, 2):
            if tap != 1:
                waits[tap // 2].wait_recv()
            value = silu_of_half(raw[tap, z, :, span].astype(F32) * scale + shift)
            if tap != 1:
                value = jnp.where(alive[tap], value, 0.0)
            hid[0, tap, z, :, span] = value.astype(BF)
        return send(hid.at[0, :, z, :, pl.ds(a, n)], hid.at[1, :, z, :, pl.ds(a, n)], kp)

    blk, taps1 = r["blk"], r["taps1"]
    part, part_rx, red = r["part"], r["part_rx"], r["red"]
    half = C1 // 2
    k1, part_k, red_z, red_k = {}, {}, {}, {}

    def hid_own(i):
        k1[i] = [hidden(raw1, hid1, zh, affine1, *CHUNKS[i], y_own[i])]

    def hid_other(i):
        k1[i].append(hidden(raw1, hid1, oz, affine1, *CHUNKS[i], y_fwd[i]))

    def first_conv(i):
        a, n = CHUNKS[i]
        span = slice(a, a + n)
        for copy in k1[i]:
            copy.wait_recv()
        mixed = sum(
            dot(w1t[slot], hid1[slot, :, :, :, span].reshape(6 * Q1, n)) for slot in range(2)
        ).astype(BF)
        value = raw1[1, :, :, span].reshape(2 * Q1, n).astype(F32) + mixed.astype(F32)
        if i == 0:
            blk[:, 0:W1] = jnp.where(zh == 0, 0.0, value[:, 0:W1]).astype(BF)
            blk[:, W1:n] = value[:, W1:].astype(BF)
        else:
            blk[:, span] = value.astype(BF)
        at = slice(i * 128, (i + 1) * 128)
        for dy in range(3):
            top = (4 * i + dy) * W1
            pair = jnp.concatenate(
                [blk[:, top : top + W1], blk[:, top + 2 * W1 : top + 3 * W1]], axis=1
            )
            got = dot(pair, r["pick1"][...]).astype(BF)
            for dx in range(3):
                t = 3 * dy + dx
                for z in range(2):
                    taps1[z, t * Q1 : (t + 1) * Q1, at] = got[
                        z * Q1 : (z + 1) * Q1, dx * 128 : (dx + 1) * 128
                    ]

    def down(i):
        at = slice(i * 128, (i + 1) * 128)
        part[:, at] = sum(
            lax.dot_general(
                dwt[z, 0 : 9 * Q1, :],
                taps1[z, :, at],
                (((0,), (0,)), ((), ())),
                preferred_element_type=F32,
            )
            for z in range(2)
        )
        part_k[i] = send(
            part.at[pl.ds(pl.multiple_of(ok * half, 16), half), pl.ds(i * 128, 128)],
            part_rx.at[:, pl.ds(i * 128, 128)],
            kp,
        )

    def reduced(i):
        at = slice(i * 128, (i + 1) * 128)
        part_k[i].wait_recv()
        mine = part[pl.ds(pl.multiple_of(k * half, 16), half), at]
        red[k, zh, :, at] = (mine + part_rx[:, at]).astype(BF)
        here = red.at[k, zh, :, pl.ds(i * 128, 128)]
        red_z[i] = send(here, here, zp)
        red_k[i] = [send(here, here, kp)]

    def pass_reduced(i):
        red_z[i].wait_recv()
        here = red.at[k, oz, :, pl.ds(i * 128, 128)]
        red_k[i].append(send(here, here, kp))

    hid_own(0)
    hid_other(0)
    hid_own(1)
    forward(2)
    first_conv(0)
    hid_other(1)
    hid_own(2)
    first_conv(1)
    for copy in dw_x:
        copy.wait_recv()
    down(0)
    down(1)
    hid_other(2)
    reduced(0)
    reduced(1)
    first_conv(2)
    down(2)
    reduced(2)
    for i in range(3):
        pass_reduced(i)
    for i in range(3):
        for copy in red_k[i]:
            copy.wait_recv()

    nrm = r["nrm"]
    nrm[:, 0:128] = jnp.zeros((C1, 128), BF)
    nrm[:, 128 + POS2 :] = jnp.zeros((C1, 128), BF)
    half_iota = lax.broadcasted_iota(jnp.int32, (half, 1), 0)
    for core in range(2):
        sides = [red[core, z] for z in range(2)]
        wide = jnp.concatenate(sides, axis=1).astype(F32)
        chan = half_iota + core * half
        row2 = group_row(
            jnp.sum(wide, axis=1, keepdims=True),
            jnp.sum(wide * wide, axis=1, keepdims=True),
            chan,
            C1 // GROUPS,
        )
        span = slice(core * half, (core + 1) * half)
        scale, shift = scale_columns(
            row2, float(C1 // GROUPS * POS2), chan, C1 // GROUPS, cols2[span, 0:1], cols2[span, 1:2]
        )
        nrm[span, 128 : 128 + POS2] = silu_of_half(wide * scale + shift).astype(BF)

    def second(side, taps):
        for dx in range(3):
            for j in range(TILES + 1):
                window = nrm[:, side * HALF2 + j * 128 : side * HALF2 + j * 128 + 256]
                got = dot(window, r["pick2"][dx]).astype(BF)
                if j < TILES:
                    at = slice(j * 128, (j + 1) * 128)
                    taps[dx * C1 : (dx + 1) * C1, at] = got[:, 0:128]
                    taps[(3 + dx) * C1 : (4 + dx) * C1, at] = got[:, 128:256]
                if j > 0:
                    at = slice((j - 1) * 128, j * 128)
                    taps[(6 + dx) * C1 : (7 + dx) * C1, at] = got[:, 0:128]
        for core in range(2):
            taps[9 * C1 + core * half : 9 * C1 + (core + 1) * half, :] = red[core, side]

    own = raw2.at[0]
    z2 = []

    def to_other(a, n):
        here = own.at[1, zh, :, pl.ds(a, n)]
        z2.append(send(here, here, zp))

    for side in range(2):
        second(side, r["taps2"])
        at = slice(side * HALF2, (side + 1) * HALF2)
        raw2[0, 1, zh, :, at] = (dot(w2t[...], r["taps2"][...]) + bias).astype(BF)
        for a, n in CHUNKS2[:1] if side == 0 else CHUNKS2[1:]:
            to_other(a, n)
    wide = raw2[0, 1, zh].astype(F32)
    q2_iota = lax.broadcasted_iota(jnp.int32, (Q2, 1), 0)
    row3 = group_row(
        jnp.sum(wide, axis=1, keepdims=True),
        jnp.sum(wide * wide, axis=1, keepdims=True),
        q2_iota + c * Q2,
        C2 // GROUPS,
    )
    state = stat_send(row3, y_peers)
    y2_own = to_frames(own, zh, 0, POS2)
    raw_k = {a: [] for a, n in CHUNKS2}

    def share(tap, z, a, n):
        here = pl.ds(a, n)
        raw_k[a].append(send(raw2.at[0, tap, z, :, here], raw2.at[1, tap, z, :, here], kp))

    share(1, zh, 0, POS2)
    par_k.wait_recv()
    cols3 = [cols, [to_columns(par[1, z]) for z in range(2)]]
    y2_fwd = []

    def forward2(i):
        z2[i].wait_recv()
        y2_fwd.append(to_frames(own, oz, *CHUNKS2[i]))
        share(1, oz, *CHUNKS2[i])

    def arrived(i):
        for tap in (0, 2):
            y2_fwd[i][tap // 2].wait_recv()
            share(tap, oz, *CHUNKS2[i])

    forward2(0)
    state = stat_send(stat_wait(state), xz_peers)
    forward2(1)
    forward2(2)
    for tap in (0, 2):
        y2_own[tap // 2].wait_recv()
        share(tap, zh, 0, POS2)
    arrived(0)
    state = stat_send(stat_wait(state), [kp])
    arrived(1)
    arrived(2)
    total = stat_wait(state)
    affine3 = [
        [
            scale_columns(
                total,
                float(C2 // GROUPS * POS2 * frames),
                q2_iota + (2 * z + core) * Q2,
                C2 // GROUPS,
                cols3[slot][z][0:Q2, 2:3],
                cols3[slot][z][0:Q2, 3:4],
            )
            for z in range(2)
        ]
        for slot, core in ((0, k), (1, ok))
    ]
    hid2, fin = r["hid2"], r["fin"]
    stores = []
    for a, n in CHUNKS2:
        at = slice(a, a + n)
        for slot in range(2):
            if slot == 1:
                for copy in raw_k[a]:
                    copy.wait_recv()
            for z in range(2):
                scale, shift = affine3[slot][z]
                for tap in range(3):
                    value = silu_of_half(raw2[slot, tap, z, :, at].astype(F32) * scale + shift)
                    if tap != 1:
                        value = jnp.where(alive[tap], value, 0.0)
                    hid2[slot, tap, z, :, at] = value.astype(BF)
        mixed = sum(
            dot(w4t[slot], hid2[slot, :, :, :, at].reshape(6 * Q2, n)) for slot in range(2)
        ).astype(BF)
        fin[:, at] = (raw2[0, 1, zh, :, at].astype(F32) + mixed.astype(F32)).astype(BF)
        here = pl.ds(a, n)
        stores.append(
            pltpu.make_async_copy(fin.at[:, here], out.at[:, here], local_sem.at[13 + len(stores)])
        )
        stores[-1].start()
    for copy in stores:
        copy.wait()
    for copy in sent:
        copy.wait_send()


def per_device(frames, lat, tw1, g1, s1, dw, g2, s2, cw2, sw2, tb, tw2, g3, s3):
    far = pl.BlockSpec(memory_space=pl.ANY)
    row = lambda v: v.reshape(1, v.shape[0])
    result = pl.pallas_call(
        functools.partial(kernel, frames),
        out_shape=jax.ShapeDtypeStruct((Q2, POS2), BF),
        in_specs=[far] * 13,
        out_specs=far,
        scratch_shapes=[pltpu.VMEM(shape, dtype) for shape, dtype in SCRATCH.values()]
        + [
            pltpu.SemaphoreType.DMA((N_SEM,)),
            pltpu.SemaphoreType.DMA((N_SEM,)),
            pltpu.SemaphoreType.DMA((16,)),
        ],
        compiler_params=pltpu.CompilerParams(
            collective_id=0, has_side_effects=True, vmem_limit_bytes=56 * 2**20
        ),
        name="video_block",
    )(
        lat.reshape(Q1, H1 * W1),
        tw1.reshape(3 * C1, C1),
        row(g1),
        row(s1),
        dw.reshape(9 * Q1, C1),
        g2,
        s2,
        cw2.transpose(0, 2, 1).reshape(9 * Q2, C1),
        sw2.T,
        row(tb),
        tw2.reshape(3 * C2, C2),
        row(g3),
        row(s3),
    )
    return result.reshape(1, Q2, POS2)


def solution(mesh):
    return jax.shard_map(
        functools.partial(per_device, mesh.shape["frame"]),
        mesh=mesh,
        in_specs=(
            P(("video", "frame"), "chan", None),
            P(),
            P("chan"),
            P("chan"),
            P(None, "chan", None),
            P(),
            P(),
            P(None, None, "chan"),
            P(None, "chan"),
            P("chan"),
            P(),
            P("chan"),
            P("chan"),
        ),
        out_specs=P(("video", "frame"), "chan", None),
        check_vma=False,
    )
```

```python
import functools

import jax
import jax.numpy as jnp
from jax import lax
from jax.experimental import pallas as pl
from jax.experimental.pallas import tpu as pltpu
from jax.sharding import PartitionSpec as P

MESH = pl.DeviceIdType.MESH
BF = jnp.bfloat16
F32 = jnp.float32
C1 = 320
C2 = 640
GROUPS = 32
W1 = 128
H1 = 24
H2 = 12
W2 = 64
NX = 4
EPS = 1e-6

Q1 = C1 // 4
Q2 = C2 // 4
HALF1 = H1 * W1 // 2
WIN1 = HALF1 + W1
HALF2 = H2 * W2 // 2
POS2 = H2 * W2
DPAD = 768
DPART = DPAD // NX
TILES = HALF2 // 128
CHUNKS = ((0, 640), (640, 512), (1152, 512))
CHUNKS2 = ((0, 384), (384, 256), (640, 128))

SCRATCH = {
    "lat_v": ((Q1, H1 * W1), BF),
    "tw1_v": ((3 * C1, C1), BF),
    "tw2_v": ((3 * C2, C2), BF),
    "cw2_v": ((9 * Q2, C1), BF),
    "sw2_v": ((Q2, C1), BF),
    "zsrc": ((Q1, WIN1), BF),
    "raw1": ((3, 2, Q1, WIN1), BF),
    "hid1": ((2, 3, 2, Q1, WIN1), BF),
    "tmp1": ((C1, 6 * Q1), BF),
    "w1t": ((2, 2 * Q1, 6 * Q1), BF),
    "blk": ((2 * Q1, WIN1), BF),
    "dwt": ((2, DPAD, C1), BF),
    "taps1": ((2, 9 * Q1, HALF2), BF),
    "part": ((C1, HALF2), F32),
    "part_rx": ((C1 // 2, HALF2), F32),
    "red": ((2, 2, C1 // 2, HALF2), BF),
    "nrm": ((C1, POS2 + 256), BF),
    "taps2": ((10 * C1, HALF2), BF),
    "w2t": ((Q2, 10 * C1), BF),
    "raw2": ((2, 3, 2, Q2, POS2), BF),
    "hid2": ((2, 3, 2, Q2, POS2), BF),
    "tmp2": ((C2, 6 * Q2), BF),
    "w4t": ((2, Q2, 6 * Q2), BF),
    "pick1": ((256, 384), BF),
    "pick2": ((3, 256, 256), BF),
    "fin": ((Q2, POS2), BF),
    "par": ((2, 2, 8, 256), F32),
    "par2": ((8, 384), F32),
    "g1_v": ((1, Q1), F32),
    "s1_v": ((1, Q1), F32),
    "g2_v": ((C1,), F32),
    "s2_v": ((C1,), F32),
    "g3_v": ((1, Q2), F32),
    "s3_v": ((1, Q2), F32),
    "tb_v": ((1, Q2), F32),
    "st_tx": ((6, 1, 128), F32),
    "st_rx": ((32, 1, 128), F32),
}
N_SEM = 128


def dot(a, b):
    return lax.dot_general(a, b, (((1,), (0,)), ((), ())), preferred_element_type=F32)


def silu_of_half(w):
    return w + w * jnp.tanh(w)


def to_columns(rows):
    return jnp.concatenate([rows] * (128 // rows.shape[0]), axis=0).T


def one_hots(chan, size):
    lane = lax.broadcasted_iota(jnp.int32, (chan.shape[0], 128), 1) * size
    off = GROUPS * size
    first = (lane <= chan) & (chan < lane + size)
    second = (lane - off <= chan) & (chan < lane - off + size)
    return first, second


def group_row(sums, squares, chan, size):
    first, second = one_hots(chan, size)
    spread = jnp.where(first, sums, 0.0) + jnp.where(second, squares, 0.0)
    return jnp.sum(spread, axis=0, keepdims=True)


def scale_columns(row, count, chan, size, gain, shift):
    first, second = one_hots(chan, size)
    mean = jnp.sum(jnp.where(first, row, 0.0), axis=1, keepdims=True) / count
    square = jnp.sum(jnp.where(second, row, 0.0), axis=1, keepdims=True) / count
    scale = lax.rsqrt(square - mean * mean + EPS) * gain
    return 0.5 * scale, 0.5 * (shift - mean * scale)


def kernel(frames, *refs):
    (lat, tw1, g1, s1, dw, g2, s2, cw2, sw2, tb, tw2, g3, s3, out) = refs[:14]
    names = list(SCRATCH)
    r = dict(zip(names, refs[14 : 14 + len(names)]))
    send_sem, recv_sem, local_sem = refs[14 + len(names) :]
    ny = frames // NX
    f = lax.axis_index("frame")
    c = lax.axis_index("chan")
    x, y = f // ny, lax.rem(f, ny)
    zh, k = c // 2, lax.rem(c, 2)
    oz, ok = 1 - zh, 1 - k
    zp = {"chan": lax.rem(c + 2, 4)}
    kp = {"chan": c + 1 - 2 * k}
    after = {"frame": lax.rem(f + 1, frames)}
    before = {"frame": lax.rem(f + frames - 1, frames)}
    chan_peers = [{"chan": lax.rem(c + d, 4)} for d in range(1, 4)]
    x_peers = [{"frame": lax.rem(x + d, NX) * ny + y} for d in range(1, NX)]
    y_peers = [{"frame": x * ny + lax.rem(y + d, ny)} for d in range(1, ny)]

    xz_peers = [
        {"frame": lax.rem(x + d, NX) * ny + y, "chan": lax.rem(c + e, 4)}
        for d in range(NX)
        for e in (0, 2)
        if d or e
    ]

    barrier = pltpu.get_barrier_semaphore()
    greeted = chan_peers + xz_peers + y_peers + [after, before]
    for peer in greeted:
        pl.semaphore_signal(barrier, inc=1, device_id=peer, device_id_type=MESH)

    loads = {}
    for number, (name, ref, dst) in enumerate(
        (
            ("lat", lat, r["lat_v"]),
            ("dw", dw, r["dwt"].at[zh, pl.ds(0, 9 * Q1)]),
            ("g1", g1, r["g1_v"]),
            ("s1", s1, r["s1_v"]),
            ("g2", g2, r["g2_v"]),
            ("s2", s2, r["s2_v"]),
            ("g3", g3, r["g3_v"]),
            ("s3", s3, r["s3_v"]),
            ("tb", tb, r["tb_v"]),
            ("tw1", tw1, r["tw1_v"]),
            ("cw2", cw2, r["cw2_v"]),
            ("sw2", sw2, r["sw2_v"]),
            ("tw2", tw2, r["tw2_v"]),
        )
    ):
        loads[name] = pltpu.make_async_copy(ref, dst, local_sem.at[number])
        loads[name].start()

    counter = [0]
    sent = []

    def send(src, dst, peer):
        number = counter[0]
        counter[0] += 1
        copy = pltpu.make_async_remote_copy(
            src_ref=src,
            dst_ref=dst,
            send_sem=send_sem.at[number],
            recv_sem=recv_sem.at[number],
            device_id=peer,
            device_id_type=MESH,
        )
        copy.start()
        sent.append(copy)
        return copy

    def lanes(start, size):
        return pl.ds(pl.multiple_of(start, 128), size)

    st_tx, st_rx = r["st_tx"], r["st_rx"]
    stat_slot = [0, 0]

    def stat_send(row, peers):
        tx, rx = stat_slot
        stat_slot[0] += 1
        stat_slot[1] += len(peers)
        st_tx[tx] = row
        return [send(st_tx.at[tx], st_rx.at[rx + i], p) for i, p in enumerate(peers)], tx, rx

    def stat_wait(state):
        copies, tx, rx = state
        total = st_tx[tx]
        for i, copy in enumerate(copies):
            copy.wait_recv()
            total = total + st_rx[rx + i]
        return total

    raw1, raw2 = r["raw1"], r["raw2"]
    lat_v = r["lat_v"]

    par = r["par"]
    loads["lat"].wait()
    zsrc = r["zsrc"]
    raw1[1, zh, :, 0:W1] = lat_v[:, HALF1 - W1 : HALF1]
    raw1[1, zh, :, W1:WIN1] = lat_v[:, lanes(zh * HALF1, HALF1)]
    zsrc[:, 0:W1] = lat_v[:, HALF1 - W1 : HALF1]
    zsrc[:, W1:WIN1] = lat_v[:, lanes(oz * HALF1, HALF1)]
    wide = lat_v[...].astype(F32)
    q1_iota = lax.broadcasted_iota(jnp.int32, (Q1, 1), 0)
    row1 = group_row(
        jnp.sum(wide, axis=1, keepdims=True),
        jnp.sum(wide * wide, axis=1, keepdims=True),
        q1_iota + c * Q1,
        C1 // GROUPS,
    )
    dwt = r["dwt"]
    for name in ("dw", "g1", "s1", "g2", "s2", "g3", "s3", "tb"):
        loads[name].wait()
    par[0, zh, 0:1, 0:Q1] = r["g1_v"][...]
    par[0, zh, 1:2, 0:Q1] = r["s1_v"][...]
    par[0, zh, 2:3, 0:Q2] = r["g3_v"][...]
    par[0, zh, 3:4, 0:Q2] = r["s3_v"][...]
    par[0, zh, 4:5, 0:Q2] = r["tb_v"][...]
    r["par2"][0:1, 0:C1] = r["g2_v"][...].reshape(1, C1)
    r["par2"][1:2, 0:C1] = r["s2_v"][...].reshape(1, C1)
    dwt[zh, 9 * Q1 : DPAD, :] = jnp.zeros((DPAD - 9 * Q1, C1), BF)
    pl.semaphore_wait(barrier, len(greeted))

    state = stat_send(row1, chan_peers)
    pieces = 2
    piece = DPART // pieces
    own_piece = pl.ds(pl.multiple_of(x * DPART + lax.rem(y, 2) * piece, 16), piece)
    dw_z = send(dwt.at[zh, own_piece], dwt.at[zh, own_piece], zp)

    z_copies = [
        send(zsrc.at[:, pl.ds(a, n)], raw1.at[1, zh, :, pl.ds(a, n)], zp) for a, n in CHUNKS
    ]

    def to_frames(raw, z, a, n):
        here = raw.at[1, z, :, pl.ds(a, n)]
        return [
            send(here, raw.at[0, z, :, pl.ds(a, n)], after),
            send(here, raw.at[2, z, :, pl.ds(a, n)], before),
        ]

    y_own = [to_frames(raw1, zh, a, n) for a, n in CHUNKS]
    par_copy = send(par.at[0, zh], par.at[0, zh], zp)

    def prepare(weight, held, width, count, core):
        rows = [
            weight[pl.ds(pl.multiple_of(t * width + z * 2 * count + core * count, 16), count), :]
            for t in range(3)
            for z in range(2)
        ]
        held[...] = jnp.concatenate(rows, axis=0).T

    w1t, w4t, w2t = r["w1t"], r["w4t"], r["w2t"]

    loads["tw1"].wait()
    for slot, core in ((0, k), (1, ok)):
        prepare(r["tw1_v"], r["tmp1"], C1, Q1, core)
        for z in range(2):
            w1t[slot, z * Q1 : (z + 1) * Q1, :] = r["tmp1"][
                pl.ds(pl.multiple_of((2 * z + k) * Q1, 16), Q1), :
            ]

    src = lax.broadcasted_iota(jnp.int32, (256, 128), 0)
    dst = lax.broadcasted_iota(jnp.int32, (256, 128), 1)
    same = (src >= 128) == (dst >= 64)
    src_col = src - jnp.where(src >= 128, 128, 0)
    dst_col = dst - jnp.where(dst >= 64, 64, 0)
    for dx in range(3):
        r["pick1"][:, dx * 128 : (dx + 1) * 128] = jnp.where(
            same & (src_col == 2 * dst_col + dx - 1), 1.0, 0.0
        ).astype(BF)

    dw_z.wait_recv()
    here = dwt.at[oz, own_piece]
    dw_y = [
        send(here, here, {"frame": x * ny + y + 1 - 2 * lax.rem(y, 2)}) for d in range(1, pieces)
    ]
    dw_x = [send(here, here, p) for p in x_peers]

    state = stat_send(stat_wait(state), x_peers)
    src = lax.broadcasted_iota(jnp.int32, (256, 256), 0)
    dst = lax.broadcasted_iota(jnp.int32, (256, 256), 1)
    second = dst >= 128
    lane = dst - jnp.where(second, 128, 0)
    upper = lane >= 64
    col = lane - jnp.where(upper, 64, 0)
    base = jnp.where(second, 128, 64) + jnp.where(upper, 64, 0)
    for dx in range(3):
        want = col + (dx - 1)
        keep = (want >= 0) & (want < W2) & (src == base + want)
        r["pick2"][dx] = jnp.where(keep, 1.0, 0.0).astype(BF)
    loads["cw2"].wait()
    loads["sw2"].wait()
    for t in range(9):
        w2t[:, t * C1 : (t + 1) * C1] = r["cw2_v"][t * Q2 : (t + 1) * Q2, :]
    w2t[:, 9 * C1 : 10 * C1] = r["sw2_v"][...]
    y_fwd = []

    def forward(i):
        z_copies[i].wait_recv()
        y_fwd.append(to_frames(raw1, oz, *CHUNKS[i]))

    for d in range(1, pieces):
        dw_y[d - 1].wait_recv()
        start = x * DPART + lax.rem(y + 1, 2) * piece
        there = dwt.at[oz, pl.ds(pl.multiple_of(start, 16), piece)]
        dw_x += [send(there, there, p) for p in x_peers]
    forward(0)
    state = stat_send(stat_wait(state), y_peers)
    forward(1)
    loads["tw2"].wait()
    for slot, core in ((0, k), (1, ok)):
        prepare(r["tw2_v"], r["tmp2"], C2, Q2, core)
        w4t[slot] = r["tmp2"][pl.ds(pl.multiple_of(c * Q2, 16), Q2), :]
    par_copy.wait_recv()
    par_k = send(par.at[0], par.at[1], kp)
    cols = [to_columns(par[0, z]) for z in range(2)]
    cols2 = to_columns(r["par2"][...])
    bias = jnp.where(zh == 0, cols[0][0:Q2, 4:5], cols[1][0:Q2, 4:5])
    total = stat_wait(state)
    affine1 = [
        scale_columns(
            total,
            float(C1 // GROUPS * H1 * W1 * frames),
            q1_iota + (2 * z + k) * Q1,
            C1 // GROUPS,
            cols[z][0:Q1, 0:1],
            cols[z][0:Q1, 1:2],
        )
        for z in range(2)
    ]
    hid1 = r["hid1"]
    alive = {0: f > 0, 2: f < frames - 1}

    def pick(pair, z):
        return [jnp.where(z == 0, pair[0][i], pair[1][i]) for i in range(2)]

    def hidden(raw, hid, z, affine, a, n, waits):
        span = slice(a, a + n)
        scale, shift = pick(affine, z)
        for tap in (1, 0, 2):
            if tap != 1:
                waits[tap // 2].wait_recv()
            value = silu_of_half(raw[tap, z, :, span].astype(F32) * scale + shift)
            if tap != 1:
                value = jnp.where(alive[tap], value, 0.0)
            hid[0, tap, z, :, span] = value.astype(BF)
        return send(hid.at[0, :, z, :, pl.ds(a, n)], hid.at[1, :, z, :, pl.ds(a, n)], kp)

    blk, taps1 = r["blk"], r["taps1"]
    part, part_rx, red = r["part"], r["part_rx"], r["red"]
    half = C1 // 2
    k1, part_k, red_z, red_k = {}, {}, {}, {}

    def hid_own(i):
        k1[i] = [hidden(raw1, hid1, zh, affine1, *CHUNKS[i], y_own[i])]

    def hid_other(i):
        k1[i].append(hidden(raw1, hid1, oz, affine1, *CHUNKS[i], y_fwd[i]))

    def first_conv(i):
        a, n = CHUNKS[i]
        span = slice(a, a + n)
        for copy in k1[i]:
            copy.wait_recv()
        mixed = sum(
            dot(w1t[slot], hid1[slot, :, :, :, span].reshape(6 * Q1, n)) for slot in range(2)
        ).astype(BF)
        value = raw1[1, :, :, span].reshape(2 * Q1, n).astype(F32) + mixed.astype(F32)
        if i == 0:
            blk[:, 0:W1] = jnp.where(zh == 0, 0.0, value[:, 0:W1]).astype(BF)
            blk[:, W1:n] = value[:, W1:].astype(BF)
        else:
            blk[:, span] = value.astype(BF)
        at = slice(i * 128, (i + 1) * 128)
        for dy in range(3):
            top = (4 * i + dy) * W1
            pair = jnp.concatenate(
                [blk[:, top : top + W1], blk[:, top + 2 * W1 : top + 3 * W1]], axis=1
            )
            got = dot(pair, r["pick1"][...]).astype(BF)
            for dx in range(3):
                t = 3 * dy + dx
                for z in range(2):
                    taps1[z, t * Q1 : (t + 1) * Q1, at] = got[
                        z * Q1 : (z + 1) * Q1, dx * 128 : (dx + 1) * 128
                    ]

    def down(i):
        at = slice(i * 128, (i + 1) * 128)
        part[:, at] = sum(
            lax.dot_general(
                dwt[z, 0 : 9 * Q1, :],
                taps1[z, :, at],
                (((0,), (0,)), ((), ())),
                preferred_element_type=F32,
            )
            for z in range(2)
        )
        part_k[i] = send(
            part.at[pl.ds(pl.multiple_of(ok * half, 16), half), pl.ds(i * 128, 128)],
            part_rx.at[:, pl.ds(i * 128, 128)],
            kp,
        )

    def reduced(i):
        at = slice(i * 128, (i + 1) * 128)
        part_k[i].wait_recv()
        mine = part[pl.ds(pl.multiple_of(k * half, 16), half), at]
        red[k, zh, :, at] = (mine + part_rx[:, at]).astype(BF)
        here = red.at[k, zh, :, pl.ds(i * 128, 128)]
        red_z[i] = send(here, here, zp)
        red_k[i] = [send(here, here, kp)]

    def pass_reduced(i):
        red_z[i].wait_recv()
        here = red.at[k, oz, :, pl.ds(i * 128, 128)]
        red_k[i].append(send(here, here, kp))

    hid_own(0)
    hid_other(0)
    hid_own(1)
    forward(2)
    first_conv(0)
    hid_other(1)
    hid_own(2)
    first_conv(1)
    for copy in dw_x:
        copy.wait_recv()
    down(0)
    down(1)
    hid_other(2)
    reduced(0)
    reduced(1)
    first_conv(2)
    down(2)
    reduced(2)
    for i in range(3):
        pass_reduced(i)
    for i in range(3):
        for copy in red_k[i]:
            copy.wait_recv()

    nrm = r["nrm"]
    nrm[:, 0:128] = jnp.zeros((C1, 128), BF)
    nrm[:, 128 + POS2 :] = jnp.zeros((C1, 128), BF)
    half_iota = lax.broadcasted_iota(jnp.int32, (half, 1), 0)
    for core in range(2):
        sides = [red[core, z] for z in range(2)]
        wide = jnp.concatenate(sides, axis=1).astype(F32)
        chan = half_iota + core * half
        row2 = group_row(
            jnp.sum(wide, axis=1, keepdims=True),
            jnp.sum(wide * wide, axis=1, keepdims=True),
            chan,
            C1 // GROUPS,
        )
        span = slice(core * half, (core + 1) * half)
        scale, shift = scale_columns(
            row2, float(C1 // GROUPS * POS2), chan, C1 // GROUPS, cols2[span, 0:1], cols2[span, 1:2]
        )
        nrm[span, 128 : 128 + POS2] = silu_of_half(wide * scale + shift).astype(BF)

    def second(side, taps):
        for dx in range(3):
            for j in range(TILES + 1):
                window = nrm[:, side * HALF2 + j * 128 : side * HALF2 + j * 128 + 256]
                got = dot(window, r["pick2"][dx]).astype(BF)
                if j < TILES:
                    at = slice(j * 128, (j + 1) * 128)
                    taps[dx * C1 : (dx + 1) * C1, at] = got[:, 0:128]
                    taps[(3 + dx) * C1 : (4 + dx) * C1, at] = got[:, 128:256]
                if j > 0:
                    at = slice((j - 1) * 128, j * 128)
                    taps[(6 + dx) * C1 : (7 + dx) * C1, at] = got[:, 0:128]
        for core in range(2):
            taps[9 * C1 + core * half : 9 * C1 + (core + 1) * half, :] = red[core, side]

    own = raw2.at[0]
    z2 = []

    def to_other(a, n):
        here = own.at[1, zh, :, pl.ds(a, n)]
        z2.append(send(here, here, zp))

    for side in range(2):
        second(side, r["taps2"])
        at = slice(side * HALF2, (side + 1) * HALF2)
        raw2[0, 1, zh, :, at] = (dot(w2t[...], r["taps2"][...]) + bias).astype(BF)
        for a, n in CHUNKS2[:1] if side == 0 else CHUNKS2[1:]:
            to_other(a, n)
    wide = raw2[0, 1, zh].astype(F32)
    q2_iota = lax.broadcasted_iota(jnp.int32, (Q2, 1), 0)
    row3 = group_row(
        jnp.sum(wide, axis=1, keepdims=True),
        jnp.sum(wide * wide, axis=1, keepdims=True),
        q2_iota + c * Q2,
        C2 // GROUPS,
    )
    state = stat_send(row3, y_peers)
    y2_own = to_frames(own, zh, 0, POS2)
    raw_k = {a: [] for a, n in CHUNKS2}

    def share(tap, z, a, n):
        here = pl.ds(a, n)
        raw_k[a].append(send(raw2.at[0, tap, z, :, here], raw2.at[1, tap, z, :, here], kp))

    share(1, zh, 0, POS2)
    par_k.wait_recv()
    cols3 = [cols, [to_columns(par[1, z]) for z in range(2)]]
    y2_fwd = []

    def forward2(i):
        z2[i].wait_recv()
        y2_fwd.append(to_frames(own, oz, *CHUNKS2[i]))
        share(1, oz, *CHUNKS2[i])

    def arrived(i):
        for tap in (0, 2):
            y2_fwd[i][tap // 2].wait_recv()
            share(tap, oz, *CHUNKS2[i])

    forward2(0)
    state = stat_send(stat_wait(state), xz_peers)
    forward2(1)
    forward2(2)
    for tap in (0, 2):
        y2_own[tap // 2].wait_recv()
        share(tap, zh, 0, POS2)
    arrived(0)
    state = stat_send(stat_wait(state), [kp])
    arrived(1)
    arrived(2)
    total = stat_wait(state)
    affine3 = [
        [
            scale_columns(
                total,
                float(C2 // GROUPS * POS2 * frames),
                q2_iota + (2 * z + core) * Q2,
                C2 // GROUPS,
                cols3[slot][z][0:Q2, 2:3],
                cols3[slot][z][0:Q2, 3:4],
            )
            for z in range(2)
        ]
        for slot, core in ((0, k), (1, ok))
    ]
    hid2, fin = r["hid2"], r["fin"]
    stores = []
    for a, n in CHUNKS2:
        at = slice(a, a + n)
        for slot in range(2):
            if slot == 1:
                for copy in raw_k[a]:
                    copy.wait_recv()
            for z in range(2):
                scale, shift = affine3[slot][z]
                for tap in range(3):
                    value = silu_of_half(raw2[slot, tap, z, :, at].astype(F32) * scale + shift)
                    if tap != 1:
                        value = jnp.where(alive[tap], value, 0.0)
                    hid2[slot, tap, z, :, at] = value.astype(BF)
        mixed = sum(
            dot(w4t[slot], hid2[slot, :, :, :, at].reshape(6 * Q2, n)) for slot in range(2)
        ).astype(BF)
        fin[:, at] = (raw2[0, 1, zh, :, at].astype(F32) + mixed.astype(F32)).astype(BF)
        here = pl.ds(a, n)
        stores.append(
            pltpu.make_async_copy(fin.at[:, here], out.at[:, here], local_sem.at[13 + len(stores)])
        )
        stores[-1].start()
    for copy in stores:
        copy.wait()
    for copy in sent:
        copy.wait_send()


def per_device(frames, lat, tw1, g1, s1, dw, g2, s2, cw2, sw2, tb, tw2, g3, s3):
    far = pl.BlockSpec(memory_space=pl.ANY)
    row = lambda v: v.reshape(1, v.shape[0])
    result = pl.pallas_call(
        functools.partial(kernel, frames),
        out_shape=jax.ShapeDtypeStruct((Q2, POS2), BF),
        in_specs=[far] * 13,
        out_specs=far,
        scratch_shapes=[pltpu.VMEM(shape, dtype) for shape, dtype in SCRATCH.values()]
        + [
            pltpu.SemaphoreType.DMA((N_SEM,)),
            pltpu.SemaphoreType.DMA((N_SEM,)),
            pltpu.SemaphoreType.DMA((16,)),
        ],
        compiler_params=pltpu.CompilerParams(
            collective_id=0, has_side_effects=True, vmem_limit_bytes=56 * 2**20
        ),
        name="video_block",
    )(
        lat.reshape(Q1, H1 * W1),
        tw1.reshape(3 * C1, C1),
        row(g1),
        row(s1),
        dw.reshape(9 * Q1, C1),
        g2,
        s2,
        cw2.transpose(0, 2, 1).reshape(9 * Q2, C1),
        sw2.T,
        row(tb),
        tw2.reshape(3 * C2, C2),
        row(g3),
        row(s3),
    )
    return result.reshape(1, Q2, POS2)


def solution(mesh):
    return jax.shard_map(
        functools.partial(per_device, mesh.shape["frame"]),
        mesh=mesh,
        in_specs=(
            P(("video", "frame"), "chan", None),
            P(),
            P("chan"),
            P("chan"),
            P(None, "chan", None),
            P(),
            P(),
            P(None, None, "chan"),
            P(None, "chan"),
            P("chan"),
            P(),
            P("chan"),
            P("chan"),
        ),
        out_specs=P(("video", "frame"), "chan", None),
        check_vma=False,
    )
```

```python
import functools

import jax
import jax.numpy as jnp
from jax import lax
from jax.experimental import pallas as pl
from jax.experimental.pallas import tpu as pltpu
from jax.sharding import PartitionSpec as P

MESH = pl.DeviceIdType.MESH
BF = jnp.bfloat16
F32 = jnp.float32
C1 = 320
C2 = 640
GROUPS = 32
W1 = 128
H1 = 24
H2 = 12
W2 = 64
NX = 4
EPS = 1e-6

Q1 = C1 // 4
Q2 = C2 // 4
HALF1 = H1 * W1 // 2
WIN1 = HALF1 + W1
HALF2 = H2 * W2 // 2
POS2 = H2 * W2
DPAD = 768
DPART = DPAD // NX
TILES = HALF2 // 128
CHUNKS = ((0, 640), (640, 512), (1152, 512))
CHUNKS2 = ((0, 384), (384, 256), (640, 128))

SCRATCH = {
    "lat_v": ((Q1, H1 * W1), BF),
    "tw1_v": ((3 * C1, C1), BF),
    "tw2_v": ((3 * C2, C2), BF),
    "cw2_v": ((9 * Q2, C1), BF),
    "sw2_v": ((Q2, C1), BF),
    "zsrc": ((Q1, WIN1), BF),
    "raw1": ((3, 2, Q1, WIN1), BF),
    "hid1": ((2, 3, 2, Q1, WIN1), BF),
    "tmp1": ((C1, 6 * Q1), BF),
    "w1t": ((2, 2 * Q1, 6 * Q1), BF),
    "blk": ((2 * Q1, WIN1), BF),
    "dwt": ((2, DPAD, C1), BF),
    "taps1": ((2, 9 * Q1, HALF2), BF),
    "part": ((C1, HALF2), F32),
    "part_rx": ((C1 // 2, HALF2), F32),
    "red": ((2, 2, C1 // 2, HALF2), BF),
    "nrm": ((C1, POS2 + 256), BF),
    "taps2": ((10 * C1, HALF2), BF),
    "w2t": ((Q2, 10 * C1), BF),
    "raw2": ((2, 3, 2, Q2, POS2), BF),
    "hid2": ((2, 3, 2, Q2, POS2), BF),
    "tmp2": ((C2, 6 * Q2), BF),
    "w4t": ((2, Q2, 6 * Q2), BF),
    "pick1": ((256, 384), BF),
    "pick2": ((3, 256, 256), BF),
    "fin": ((Q2, POS2), BF),
    "par": ((2, 2, 8, 256), F32),
    "par2": ((8, 384), F32),
    "g1_v": ((1, Q1), F32),
    "s1_v": ((1, Q1), F32),
    "g2_v": ((C1,), F32),
    "s2_v": ((C1,), F32),
    "g3_v": ((1, Q2), F32),
    "s3_v": ((1, Q2), F32),
    "tb_v": ((1, Q2), F32),
    "st_tx": ((6, 1, 128), F32),
    "st_rx": ((32, 1, 128), F32),
}
N_SEM = 128


def dot(a, b):
    return lax.dot_general(a, b, (((1,), (0,)), ((), ())), preferred_element_type=F32)


def silu_of_half(w):
    return w + w * jnp.tanh(w)


def to_columns(rows):
    return jnp.concatenate([rows] * (128 // rows.shape[0]), axis=0).T


def one_hots(chan, size):
    lane = lax.broadcasted_iota(jnp.int32, (chan.shape[0], 128), 1) * size
    off = GROUPS * size
    first = (lane <= chan) & (chan < lane + size)
    second = (lane - off <= chan) & (chan < lane - off + size)
    return first, second


def group_row(sums, squares, chan, size):
    first, second = one_hots(chan, size)
    spread = jnp.where(first, sums, 0.0) + jnp.where(second, squares, 0.0)
    return jnp.sum(spread, axis=0, keepdims=True)


def scale_columns(row, count, chan, size, gain, shift):
    first, second = one_hots(chan, size)
    mean = jnp.sum(jnp.where(first, row, 0.0), axis=1, keepdims=True) / count
    square = jnp.sum(jnp.where(second, row, 0.0), axis=1, keepdims=True) / count
    scale = lax.rsqrt(square - mean * mean + EPS) * gain
    return 0.5 * scale, 0.5 * (shift - mean * scale)


def kernel(frames, *refs):
    (lat, tw1, g1, s1, dw, g2, s2, cw2, sw2, tb, tw2, g3, s3, out) = refs[:14]
    names = list(SCRATCH)
    r = dict(zip(names, refs[14 : 14 + len(names)]))
    send_sem, recv_sem, local_sem = refs[14 + len(names) :]
    ny = frames // NX
    f = lax.axis_index("frame")
    c = lax.axis_index("chan")
    x, y = f // ny, lax.rem(f, ny)
    zh, k = c // 2, lax.rem(c, 2)
    oz, ok = 1 - zh, 1 - k
    zp = {"chan": lax.rem(c + 2, 4)}
    kp = {"chan": c + 1 - 2 * k}
    after = {"frame": lax.rem(f + 1, frames)}
    before = {"frame": lax.rem(f + frames - 1, frames)}
    chan_peers = [{"chan": lax.rem(c + d, 4)} for d in range(1, 4)]
    x_peers = [{"frame": lax.rem(x + d, NX) * ny + y} for d in range(1, NX)]
    y_peers = [{"frame": x * ny + lax.rem(y + d, ny)} for d in range(1, ny)]

    barrier = pltpu.get_barrier_semaphore()
    greeted = chan_peers + x_peers + y_peers + [after, before]
    for peer in greeted:
        pl.semaphore_signal(barrier, inc=1, device_id=peer, device_id_type=MESH)

    loads = {}
    for number, (name, ref, dst) in enumerate(
        (
            ("lat", lat, r["lat_v"]),
            ("dw", dw, r["dwt"].at[zh, pl.ds(0, 9 * Q1)]),
            ("g1", g1, r["g1_v"]),
            ("s1", s1, r["s1_v"]),
            ("g2", g2, r["g2_v"]),
            ("s2", s2, r["s2_v"]),
            ("g3", g3, r["g3_v"]),
            ("s3", s3, r["s3_v"]),
            ("tb", tb, r["tb_v"]),
            ("tw1", tw1, r["tw1_v"]),
            ("cw2", cw2, r["cw2_v"]),
            ("sw2", sw2, r["sw2_v"]),
            ("tw2", tw2, r["tw2_v"]),
        )
    ):
        loads[name] = pltpu.make_async_copy(ref, dst, local_sem.at[number])
        loads[name].start()

    counter = [0]
    sent = []

    def send(src, dst, peer):
        number = counter[0]
        counter[0] += 1
        copy = pltpu.make_async_remote_copy(
            src_ref=src,
            dst_ref=dst,
            send_sem=send_sem.at[number],
            recv_sem=recv_sem.at[number],
            device_id=peer,
            device_id_type=MESH,
        )
        copy.start()
        sent.append(copy)
        return copy

    def lanes(start, size):
        return pl.ds(pl.multiple_of(start, 128), size)

    st_tx, st_rx = r["st_tx"], r["st_rx"]
    stat_slot = [0, 0]

    def stat_send(row, peers):
        tx, rx = stat_slot
        stat_slot[0] += 1
        stat_slot[1] += len(peers)
        st_tx[tx] = row
        return [send(st_tx.at[tx], st_rx.at[rx + i], p) for i, p in enumerate(peers)], tx, rx

    def stat_wait(state):
        copies, tx, rx = state
        total = st_tx[tx]
        for i, copy in enumerate(copies):
            copy.wait_recv()
            total = total + st_rx[rx + i]
        return total

    raw1, raw2 = r["raw1"], r["raw2"]
    lat_v = r["lat_v"]

    par = r["par"]
    loads["lat"].wait()
    zsrc = r["zsrc"]
    raw1[1, zh, :, 0:W1] = lat_v[:, HALF1 - W1 : HALF1]
    raw1[1, zh, :, W1:WIN1] = lat_v[:, lanes(zh * HALF1, HALF1)]
    zsrc[:, 0:W1] = lat_v[:, HALF1 - W1 : HALF1]
    zsrc[:, W1:WIN1] = lat_v[:, lanes(oz * HALF1, HALF1)]
    wide = lat_v[...].astype(F32)
    q1_iota = lax.broadcasted_iota(jnp.int32, (Q1, 1), 0)
    row1 = group_row(
        jnp.sum(wide, axis=1, keepdims=True),
        jnp.sum(wide * wide, axis=1, keepdims=True),
        q1_iota + c * Q1,
        C1 // GROUPS,
    )
    dwt = r["dwt"]
    for name in ("dw", "g1", "s1", "g2", "s2", "g3", "s3", "tb"):
        loads[name].wait()
    par[0, zh, 0:1, 0:Q1] = r["g1_v"][...]
    par[0, zh, 1:2, 0:Q1] = r["s1_v"][...]
    par[0, zh, 2:3, 0:Q2] = r["g3_v"][...]
    par[0, zh, 3:4, 0:Q2] = r["s3_v"][...]
    par[0, zh, 4:5, 0:Q2] = r["tb_v"][...]
    r["par2"][0:1, 0:C1] = r["g2_v"][...].reshape(1, C1)
    r["par2"][1:2, 0:C1] = r["s2_v"][...].reshape(1, C1)
    dwt[zh, 9 * Q1 : DPAD, :] = jnp.zeros((DPAD - 9 * Q1, C1), BF)
    pl.semaphore_wait(barrier, len(greeted))

    state = stat_send(row1, chan_peers)
    pieces = ny // 2
    piece = DPART // pieces
    own_piece = pl.ds(pl.multiple_of(x * DPART + (y // 2) * piece, 16), piece)
    dw_z = send(dwt.at[zh, own_piece], dwt.at[zh, own_piece], zp)

    z_copies = [
        send(zsrc.at[:, pl.ds(a, n)], raw1.at[1, zh, :, pl.ds(a, n)], zp) for a, n in CHUNKS
    ]

    def to_frames(raw, z, a, n):
        here = raw.at[1, z, :, pl.ds(a, n)]
        return [
            send(here, raw.at[0, z, :, pl.ds(a, n)], after),
            send(here, raw.at[2, z, :, pl.ds(a, n)], before),
        ]

    y_own = [to_frames(raw1, zh, a, n) for a, n in CHUNKS]
    par_copy = send(par.at[0, zh], par.at[0, zh], zp)

    def prepare(weight, held, width, count, core):
        rows = [
            weight[pl.ds(pl.multiple_of(t * width + z * 2 * count + core * count, 16), count), :]
            for t in range(3)
            for z in range(2)
        ]
        held[...] = jnp.concatenate(rows, axis=0).T

    w1t, w4t, w2t = r["w1t"], r["w4t"], r["w2t"]

    loads["tw1"].wait()
    for slot, core in ((0, k), (1, ok)):
        prepare(r["tw1_v"], r["tmp1"], C1, Q1, core)
        for z in range(2):
            w1t[slot, z * Q1 : (z + 1) * Q1, :] = r["tmp1"][
                pl.ds(pl.multiple_of((2 * z + k) * Q1, 16), Q1), :
            ]

    src = lax.broadcasted_iota(jnp.int32, (256, 128), 0)
    dst = lax.broadcasted_iota(jnp.int32, (256, 128), 1)
    same = (src >= 128) == (dst >= 64)
    src_col = src - jnp.where(src >= 128, 128, 0)
    dst_col = dst - jnp.where(dst >= 64, 64, 0)
    for dx in range(3):
        r["pick1"][:, dx * 128 : (dx + 1) * 128] = jnp.where(
            same & (src_col == 2 * dst_col + dx - 1), 1.0, 0.0
        ).astype(BF)

    state = stat_send(stat_wait(state), x_peers)
    dw_z.wait_recv()
    here = dwt.at[oz, own_piece]
    dw_y = [
        send(here, here, {"frame": x * ny + lax.rem(y + 2 * d, ny)}) for d in range(1, pieces)
    ]
    dw_x = [send(here, here, p) for p in x_peers]

    src = lax.broadcasted_iota(jnp.int32, (256, 256), 0)
    dst = lax.broadcasted_iota(jnp.int32, (256, 256), 1)
    second = dst >= 128
    lane = dst - jnp.where(second, 128, 0)
    upper = lane >= 64
    col = lane - jnp.where(upper, 64, 0)
    base = jnp.where(second, 128, 64) + jnp.where(upper, 64, 0)
    for dx in range(3):
        want = col + (dx - 1)
        keep = (want >= 0) & (want < W2) & (src == base + want)
        r["pick2"][dx] = jnp.where(keep, 1.0, 0.0).astype(BF)
    loads["cw2"].wait()
    loads["sw2"].wait()
    for t in range(9):
        w2t[:, t * C1 : (t + 1) * C1] = r["cw2_v"][t * Q2 : (t + 1) * Q2, :]
    w2t[:, 9 * C1 : 10 * C1] = r["sw2_v"][...]
    y_fwd = []

    def forward(i):
        z_copies[i].wait_recv()
        y_fwd.append(to_frames(raw1, oz, *CHUNKS[i]))

    forward(0)
    state = stat_send(stat_wait(state), y_peers)
    for d in range(1, pieces):
        dw_y[d - 1].wait_recv()
        start = x * DPART + lax.rem(y // 2 + pieces - d, pieces) * piece
        there = dwt.at[oz, pl.ds(pl.multiple_of(start, 16), piece)]
        dw_x += [send(there, there, p) for p in x_peers]
    forward(1)
    loads["tw2"].wait()
    for slot, core in ((0, k), (1, ok)):
        prepare(r["tw2_v"], r["tmp2"], C2, Q2, core)
        w4t[slot] = r["tmp2"][pl.ds(pl.multiple_of(c * Q2, 16), Q2), :]
    par_copy.wait_recv()
    par_k = send(par.at[0], par.at[1], kp)
    cols = [to_columns(par[0, z]) for z in range(2)]
    cols2 = to_columns(r["par2"][...])
    bias = jnp.where(zh == 0, cols[0][0:Q2, 4:5], cols[1][0:Q2, 4:5])
    total = stat_wait(state)
    affine1 = [
        scale_columns(
            total,
            float(C1 // GROUPS * H1 * W1 * frames),
            q1_iota + (2 * z + k) * Q1,
            C1 // GROUPS,
            cols[z][0:Q1, 0:1],
            cols[z][0:Q1, 1:2],
        )
        for z in range(2)
    ]
    hid1 = r["hid1"]
    alive = {0: f > 0, 2: f < frames - 1}

    def pick(pair, z):
        return [jnp.where(z == 0, pair[0][i], pair[1][i]) for i in range(2)]

    def hidden(raw, hid, z, affine, a, n, waits):
        span = slice(a, a + n)
        scale, shift = pick(affine, z)
        for tap in (1, 0, 2):
            if tap != 1:
                waits[tap // 2].wait_recv()
            value = silu_of_half(raw[tap, z, :, span].astype(F32) * scale + shift)
            if tap != 1:
                value = jnp.where(alive[tap], value, 0.0)
            hid[0, tap, z, :, span] = value.astype(BF)
        return send(hid.at[0, :, z, :, pl.ds(a, n)], hid.at[1, :, z, :, pl.ds(a, n)], kp)

    blk, taps1 = r["blk"], r["taps1"]
    part, part_rx, red = r["part"], r["part_rx"], r["red"]
    half = C1 // 2
    k1, part_k, red_z, red_k = {}, {}, {}, {}

    def hid_own(i):
        k1[i] = [hidden(raw1, hid1, zh, affine1, *CHUNKS[i], y_own[i])]

    def hid_other(i):
        k1[i].append(hidden(raw1, hid1, oz, affine1, *CHUNKS[i], y_fwd[i]))

    def first_conv(i):
        a, n = CHUNKS[i]
        span = slice(a, a + n)
        for copy in k1[i]:
            copy.wait_recv()
        mixed = sum(
            dot(w1t[slot], hid1[slot, :, :, :, span].reshape(6 * Q1, n)) for slot in range(2)
        ).astype(BF)
        value = raw1[1, :, :, span].reshape(2 * Q1, n).astype(F32) + mixed.astype(F32)
        if i == 0:
            blk[:, 0:W1] = jnp.where(zh == 0, 0.0, value[:, 0:W1]).astype(BF)
            blk[:, W1:n] = value[:, W1:].astype(BF)
        else:
            blk[:, span] = value.astype(BF)
        at = slice(i * 128, (i + 1) * 128)
        for dy in range(3):
            top = (4 * i + dy) * W1
            pair = jnp.concatenate(
                [blk[:, top : top + W1], blk[:, top + 2 * W1 : top + 3 * W1]], axis=1
            )
            got = dot(pair, r["pick1"][...]).astype(BF)
            for dx in range(3):
                t = 3 * dy + dx
                for z in range(2):
                    taps1[z, t * Q1 : (t + 1) * Q1, at] = got[
                        z * Q1 : (z + 1) * Q1, dx * 128 : (dx + 1) * 128
                    ]

    def down(i):
        at = slice(i * 128, (i + 1) * 128)
        part[:, at] = sum(
            lax.dot_general(
                dwt[z, 0 : 9 * Q1, :],
                taps1[z, :, at],
                (((0,), (0,)), ((), ())),
                preferred_element_type=F32,
            )
            for z in range(2)
        )
        part_k[i] = send(
            part.at[pl.ds(pl.multiple_of(ok * half, 16), half), pl.ds(i * 128, 128)],
            part_rx.at[:, pl.ds(i * 128, 128)],
            kp,
        )

    def reduced(i):
        at = slice(i * 128, (i + 1) * 128)
        part_k[i].wait_recv()
        mine = part[pl.ds(pl.multiple_of(k * half, 16), half), at]
        red[k, zh, :, at] = (mine + part_rx[:, at]).astype(BF)
        here = red.at[k, zh, :, pl.ds(i * 128, 128)]
        red_z[i] = send(here, here, zp)
        red_k[i] = [send(here, here, kp)]

    def pass_reduced(i):
        red_z[i].wait_recv()
        here = red.at[k, oz, :, pl.ds(i * 128, 128)]
        red_k[i].append(send(here, here, kp))

    hid_own(0)
    hid_other(0)
    hid_own(1)
    forward(2)
    first_conv(0)
    hid_other(1)
    hid_own(2)
    first_conv(1)
    for copy in dw_x:
        copy.wait_recv()
    down(0)
    down(1)
    hid_other(2)
    reduced(0)
    reduced(1)
    first_conv(2)
    down(2)
    reduced(2)
    for i in range(3):
        pass_reduced(i)
    for i in range(3):
        for copy in red_k[i]:
            copy.wait_recv()

    nrm = r["nrm"]
    nrm[:, 0:128] = jnp.zeros((C1, 128), BF)
    nrm[:, 128 + POS2 :] = jnp.zeros((C1, 128), BF)
    half_iota = lax.broadcasted_iota(jnp.int32, (half, 1), 0)
    for core in range(2):
        sides = [red[core, z] for z in range(2)]
        wide = jnp.concatenate(sides, axis=1).astype(F32)
        chan = half_iota + core * half
        row2 = group_row(
            jnp.sum(wide, axis=1, keepdims=True),
            jnp.sum(wide * wide, axis=1, keepdims=True),
            chan,
            C1 // GROUPS,
        )
        span = slice(core * half, (core + 1) * half)
        scale, shift = scale_columns(
            row2, float(C1 // GROUPS * POS2), chan, C1 // GROUPS, cols2[span, 0:1], cols2[span, 1:2]
        )
        nrm[span, 128 : 128 + POS2] = silu_of_half(wide * scale + shift).astype(BF)

    def second(side, taps):
        for dx in range(3):
            for j in range(TILES + 1):
                window = nrm[:, side * HALF2 + j * 128 : side * HALF2 + j * 128 + 256]
                got = dot(window, r["pick2"][dx]).astype(BF)
                if j < TILES:
                    at = slice(j * 128, (j + 1) * 128)
                    taps[dx * C1 : (dx + 1) * C1, at] = got[:, 0:128]
                    taps[(3 + dx) * C1 : (4 + dx) * C1, at] = got[:, 128:256]
                if j > 0:
                    at = slice((j - 1) * 128, j * 128)
                    taps[(6 + dx) * C1 : (7 + dx) * C1, at] = got[:, 0:128]
        for core in range(2):
            taps[9 * C1 + core * half : 9 * C1 + (core + 1) * half, :] = red[core, side]

    own = raw2.at[0]
    z2 = []

    def to_other(a, n):
        here = own.at[1, zh, :, pl.ds(a, n)]
        z2.append(send(here, here, zp))

    for side in range(2):
        second(side, r["taps2"])
        at = slice(side * HALF2, (side + 1) * HALF2)
        raw2[0, 1, zh, :, at] = (dot(w2t[...], r["taps2"][...]) + bias).astype(BF)
        for a, n in CHUNKS2[:1] if side == 0 else CHUNKS2[1:]:
            to_other(a, n)
    y2_own = to_frames(own, zh, 0, POS2)
    wide = raw2[0, 1, zh].astype(F32)
    q2_iota = lax.broadcasted_iota(jnp.int32, (Q2, 1), 0)
    row3 = group_row(
        jnp.sum(wide, axis=1, keepdims=True),
        jnp.sum(wide * wide, axis=1, keepdims=True),
        q2_iota + c * Q2,
        C2 // GROUPS,
    )
    state = stat_send(row3, x_peers)
    raw_k = {a: [] for a, n in CHUNKS2}

    def share(tap, z, a, n):
        here = pl.ds(a, n)
        raw_k[a].append(send(raw2.at[0, tap, z, :, here], raw2.at[1, tap, z, :, here], kp))

    share(1, zh, 0, POS2)
    par_k.wait_recv()
    cols3 = [cols, [to_columns(par[1, z]) for z in range(2)]]
    y2_fwd = []

    def forward2(i):
        z2[i].wait_recv()
        y2_fwd.append(to_frames(own, oz, *CHUNKS2[i]))
        share(1, oz, *CHUNKS2[i])

    def arrived(i):
        for tap in (0, 2):
            y2_fwd[i][tap // 2].wait_recv()
            share(tap, oz, *CHUNKS2[i])

    state = stat_send(stat_wait(state), y_peers)
    forward2(0)
    for tap in (0, 2):
        y2_own[tap // 2].wait_recv()
        share(tap, zh, 0, POS2)
    state = stat_send(stat_wait(state), chan_peers)
    forward2(1)
    forward2(2)
    for i in range(3):
        arrived(i)
    total = stat_wait(state)
    affine3 = [
        [
            scale_columns(
                total,
                float(C2 // GROUPS * POS2 * frames),
                q2_iota + (2 * z + core) * Q2,
                C2 // GROUPS,
                cols3[slot][z][0:Q2, 2:3],
                cols3[slot][z][0:Q2, 3:4],
            )
            for z in range(2)
        ]
        for slot, core in ((0, k), (1, ok))
    ]
    hid2, fin = r["hid2"], r["fin"]
    stores = []
    for a, n in CHUNKS2:
        at = slice(a, a + n)
        for slot in range(2):
            if slot == 1:
                for copy in raw_k[a]:
                    copy.wait_recv()
            for z in range(2):
                scale, shift = affine3[slot][z]
                for tap in range(3):
                    value = silu_of_half(raw2[slot, tap, z, :, at].astype(F32) * scale + shift)
                    if tap != 1:
                        value = jnp.where(alive[tap], value, 0.0)
                    hid2[slot, tap, z, :, at] = value.astype(BF)
        mixed = sum(
            dot(w4t[slot], hid2[slot, :, :, :, at].reshape(6 * Q2, n)) for slot in range(2)
        ).astype(BF)
        fin[:, at] = (raw2[0, 1, zh, :, at].astype(F32) + mixed.astype(F32)).astype(BF)
        here = pl.ds(a, n)
        stores.append(
            pltpu.make_async_copy(fin.at[:, here], out.at[:, here], local_sem.at[13 + len(stores)])
        )
        stores[-1].start()
    for copy in stores:
        copy.wait()
    for copy in sent:
        copy.wait_send()


def per_device(frames, lat, tw1, g1, s1, dw, g2, s2, cw2, sw2, tb, tw2, g3, s3):
    far = pl.BlockSpec(memory_space=pl.ANY)
    row = lambda v: v.reshape(1, v.shape[0])
    result = pl.pallas_call(
        functools.partial(kernel, frames),
        out_shape=jax.ShapeDtypeStruct((Q2, POS2), BF),
        in_specs=[far] * 13,
        out_specs=far,
        scratch_shapes=[pltpu.VMEM(shape, dtype) for shape, dtype in SCRATCH.values()]
        + [
            pltpu.SemaphoreType.DMA((N_SEM,)),
            pltpu.SemaphoreType.DMA((N_SEM,)),
            pltpu.SemaphoreType.DMA((16,)),
        ],
        compiler_params=pltpu.CompilerParams(
            collective_id=0, has_side_effects=True, vmem_limit_bytes=56 * 2**20
        ),
        name="video_block",
    )(
        lat.reshape(Q1, H1 * W1),
        tw1.reshape(3 * C1, C1),
        row(g1),
        row(s1),
        dw.reshape(9 * Q1, C1),
        g2,
        s2,
        cw2.transpose(0, 2, 1).reshape(9 * Q2, C1),
        sw2.T,
        row(tb),
        tw2.reshape(3 * C2, C2),
        row(g3),
        row(s3),
    )
    return result.reshape(1, Q2, POS2)


def solution(mesh):
    return jax.shard_map(
        functools.partial(per_device, mesh.shape["frame"]),
        mesh=mesh,
        in_specs=(
            P(("video", "frame"), "chan", None),
            P(),
            P("chan"),
            P("chan"),
            P(None, "chan", None),
            P(),
            P(),
            P(None, None, "chan"),
            P(None, "chan"),
            P("chan"),
            P(),
            P("chan"),
            P("chan"),
        ),
        out_specs=P(("video", "frame"), "chan", None),
        check_vma=False,
    )
```

```python
import functools

import jax
import jax.numpy as jnp
from jax import lax
from jax.experimental import pallas as pl
from jax.experimental.pallas import tpu as pltpu
from jax.sharding import PartitionSpec as P

MESH = pl.DeviceIdType.MESH
BF = jnp.bfloat16
F32 = jnp.float32
C1 = 320
C2 = 640
GROUPS = 32
W1 = 128
H1 = 24
H2 = 12
W2 = 64
NX = 4
EPS = 1e-6

Q1 = C1 // 4
Q2 = C2 // 4
HALF1 = H1 * W1 // 2
WIN1 = HALF1 + W1
HALF2 = H2 * W2 // 2
POS2 = H2 * W2
DPAD = 768
DPART = DPAD // NX
TILES = HALF2 // 128
CHUNKS = ((0, 640), (640, 512), (1152, 512))
CHUNKS2 = ((0, 384), (384, 256), (640, 128))

SCRATCH = {
    "lat_v": ((Q1, H1 * W1), BF),
    "tw1_v": ((3 * C1, C1), BF),
    "tw2_v": ((3 * C2, C2), BF),
    "cw2_v": ((9 * Q2, C1), BF),
    "sw2_v": ((Q2, C1), BF),
    "zsrc": ((Q1, WIN1), BF),
    "raw1": ((3, 2, Q1, WIN1), BF),
    "hid1": ((2, 3, 2, Q1, WIN1), BF),
    "tmp1": ((C1, 6 * Q1), BF),
    "w1t": ((2, 2 * Q1, 6 * Q1), BF),
    "blk": ((2 * Q1, WIN1), BF),
    "dwt": ((2, DPAD, C1), BF),
    "taps1": ((2, 9 * Q1, HALF2), BF),
    "part": ((C1, HALF2), F32),
    "part_rx": ((C1 // 2, HALF2), F32),
    "red": ((2, 2, C1 // 2, HALF2), BF),
    "nrm": ((C1, POS2 + 256), BF),
    "taps2": ((10 * C1, HALF2), BF),
    "w2t": ((Q2, 10 * C1), BF),
    "raw2": ((2, 3, 2, Q2, POS2), BF),
    "hid2": ((2, 3, 2, Q2, POS2), BF),
    "tmp2": ((C2, 6 * Q2), BF),
    "w4t": ((2, Q2, 6 * Q2), BF),
    "pick1": ((256, 384), BF),
    "pick2": ((3, 256, 256), BF),
    "fin": ((Q2, POS2), BF),
    "par": ((2, 2, 8, 256), F32),
    "par2": ((8, 384), F32),
    "g1_v": ((1, Q1), F32),
    "s1_v": ((1, Q1), F32),
    "g2_v": ((C1,), F32),
    "s2_v": ((C1,), F32),
    "g3_v": ((1, Q2), F32),
    "s3_v": ((1, Q2), F32),
    "tb_v": ((1, Q2), F32),
    "st_tx": ((6, 1, 128), F32),
    "st_rx": ((32, 1, 128), F32),
}
N_SEM = 128


def dot(a, b):
    return lax.dot_general(a, b, (((1,), (0,)), ((), ())), preferred_element_type=F32)


def silu_of_half(w):
    return w + w * jnp.tanh(w)


def to_columns(rows):
    return jnp.concatenate([rows] * (128 // rows.shape[0]), axis=0).T


def one_hots(chan, size):
    lane = lax.broadcasted_iota(jnp.int32, (chan.shape[0], 128), 1) * size
    off = GROUPS * size
    first = (lane <= chan) & (chan < lane + size)
    second = (lane - off <= chan) & (chan < lane - off + size)
    return first, second


def group_row(sums, squares, chan, size):
    first, second = one_hots(chan, size)
    spread = jnp.where(first, sums, 0.0) + jnp.where(second, squares, 0.0)
    return jnp.sum(spread, axis=0, keepdims=True)


def scale_columns(row, count, chan, size, gain, shift):
    first, second = one_hots(chan, size)
    mean = jnp.sum(jnp.where(first, row, 0.0), axis=1, keepdims=True) / count
    square = jnp.sum(jnp.where(second, row, 0.0), axis=1, keepdims=True) / count
    scale = lax.rsqrt(square - mean * mean + EPS) * gain
    return 0.5 * scale, 0.5 * (shift - mean * scale)


def kernel(frames, *refs):
    (lat, tw1, g1, s1, dw, g2, s2, cw2, sw2, tb, tw2, g3, s3, out) = refs[:14]
    names = list(SCRATCH)
    r = dict(zip(names, refs[14 : 14 + len(names)]))
    send_sem, recv_sem, local_sem = refs[14 + len(names) :]
    ny = frames // NX
    f = lax.axis_index("frame")
    c = lax.axis_index("chan")
    x, y = f // ny, lax.rem(f, ny)
    zh, k = c // 2, lax.rem(c, 2)
    oz, ok = 1 - zh, 1 - k
    zp = {"chan": lax.rem(c + 2, 4)}
    kp = {"chan": c + 1 - 2 * k}
    after = {"frame": lax.rem(f + 1, frames)}
    before = {"frame": lax.rem(f + frames - 1, frames)}
    chan_peers = [{"chan": lax.rem(c + d, 4)} for d in range(1, 4)]
    x_peers = [{"frame": lax.rem(x + d, NX) * ny + y} for d in range(1, NX)]
    y_peers = [{"frame": x * ny + lax.rem(y + d, ny)} for d in range(1, ny)]

    barrier = pltpu.get_barrier_semaphore()
    greeted = chan_peers + x_peers + y_peers + [after, before]
    for peer in greeted:
        pl.semaphore_signal(barrier, inc=1, device_id=peer, device_id_type=MESH)

    loads = {}
    for number, (name, ref, dst) in enumerate(
        (
            ("lat", lat, r["lat_v"]),
            ("dw", dw, r["dwt"].at[zh, pl.ds(0, 9 * Q1)]),
            ("g1", g1, r["g1_v"]),
            ("s1", s1, r["s1_v"]),
            ("g2", g2, r["g2_v"]),
            ("s2", s2, r["s2_v"]),
            ("g3", g3, r["g3_v"]),
            ("s3", s3, r["s3_v"]),
            ("tb", tb, r["tb_v"]),
            ("tw1", tw1, r["tw1_v"]),
            ("cw2", cw2, r["cw2_v"]),
            ("sw2", sw2, r["sw2_v"]),
            ("tw2", tw2, r["tw2_v"]),
        )
    ):
        loads[name] = pltpu.make_async_copy(ref, dst, local_sem.at[number])
        loads[name].start()

    counter = [0]
    sent = []

    def send(src, dst, peer):
        number = counter[0]
        counter[0] += 1
        copy = pltpu.make_async_remote_copy(
            src_ref=src,
            dst_ref=dst,
            send_sem=send_sem.at[number],
            recv_sem=recv_sem.at[number],
            device_id=peer,
            device_id_type=MESH,
        )
        copy.start()
        sent.append(copy)
        return copy

    def lanes(start, size):
        return pl.ds(pl.multiple_of(start, 128), size)

    st_tx, st_rx = r["st_tx"], r["st_rx"]
    stat_slot = [0, 0]

    def stat_send(row, peers):
        tx, rx = stat_slot
        stat_slot[0] += 1
        stat_slot[1] += len(peers)
        st_tx[tx] = row
        return [send(st_tx.at[tx], st_rx.at[rx + i], p) for i, p in enumerate(peers)], tx, rx

    def stat_wait(state):
        copies, tx, rx = state
        total = st_tx[tx]
        for i, copy in enumerate(copies):
            copy.wait_recv()
            total = total + st_rx[rx + i]
        return total

    raw1, raw2 = r["raw1"], r["raw2"]
    lat_v = r["lat_v"]

    par = r["par"]
    loads["lat"].wait()
    zsrc = r["zsrc"]
    raw1[1, zh, :, 0:W1] = lat_v[:, HALF1 - W1 : HALF1]
    raw1[1, zh, :, W1:WIN1] = lat_v[:, lanes(zh * HALF1, HALF1)]
    zsrc[:, 0:W1] = lat_v[:, HALF1 - W1 : HALF1]
    zsrc[:, W1:WIN1] = lat_v[:, lanes(oz * HALF1, HALF1)]
    wide = lat_v[...].astype(F32)
    q1_iota = lax.broadcasted_iota(jnp.int32, (Q1, 1), 0)
    row1 = group_row(
        jnp.sum(wide, axis=1, keepdims=True),
        jnp.sum(wide * wide, axis=1, keepdims=True),
        q1_iota + c * Q1,
        C1 // GROUPS,
    )
    dwt = r["dwt"]
    for name in ("dw", "g1", "s1", "g2", "s2", "g3", "s3", "tb"):
        loads[name].wait()
    par[0, zh, 0:1, 0:Q1] = r["g1_v"][...]
    par[0, zh, 1:2, 0:Q1] = r["s1_v"][...]
    par[0, zh, 2:3, 0:Q2] = r["g3_v"][...]
    par[0, zh, 3:4, 0:Q2] = r["s3_v"][...]
    par[0, zh, 4:5, 0:Q2] = r["tb_v"][...]
    r["par2"][0:1, 0:C1] = r["g2_v"][...].reshape(1, C1)
    r["par2"][1:2, 0:C1] = r["s2_v"][...].reshape(1, C1)
    dwt[zh, 9 * Q1 : DPAD, :] = jnp.zeros((DPAD - 9 * Q1, C1), BF)
    pl.semaphore_wait(barrier, len(greeted))

    state = stat_send(row1, chan_peers)
    pieces = ny // 2
    piece = DPART // pieces
    own_piece = pl.ds(pl.multiple_of(x * DPART + (y // 2) * piece, 16), piece)
    dw_z = send(dwt.at[zh, own_piece], dwt.at[zh, own_piece], zp)

    z_copies = [
        send(zsrc.at[:, pl.ds(a, n)], raw1.at[1, zh, :, pl.ds(a, n)], zp) for a, n in CHUNKS
    ]

    def to_frames(raw, z, a, n):
        here = raw.at[1, z, :, pl.ds(a, n)]
        return [
            send(here, raw.at[0, z, :, pl.ds(a, n)], after),
            send(here, raw.at[2, z, :, pl.ds(a, n)], before),
        ]

    y_own = [to_frames(raw1, zh, a, n) for a, n in CHUNKS]
    par_copy = send(par.at[0, zh], par.at[0, zh], zp)

    def prepare(weight, held, width, count, core):
        rows = [
            weight[pl.ds(pl.multiple_of(t * width + z * 2 * count + core * count, 16), count), :]
            for t in range(3)
            for z in range(2)
        ]
        held[...] = jnp.concatenate(rows, axis=0).T

    w1t, w4t, w2t = r["w1t"], r["w4t"], r["w2t"]

    loads["tw1"].wait()
    for slot, core in ((0, k), (1, ok)):
        prepare(r["tw1_v"], r["tmp1"], C1, Q1, core)
        for z in range(2):
            w1t[slot, z * Q1 : (z + 1) * Q1, :] = r["tmp1"][
                pl.ds(pl.multiple_of((2 * z + k) * Q1, 16), Q1), :
            ]

    src = lax.broadcasted_iota(jnp.int32, (256, 128), 0)
    dst = lax.broadcasted_iota(jnp.int32, (256, 128), 1)
    same = (src >= 128) == (dst >= 64)
    src_col = src - jnp.where(src >= 128, 128, 0)
    dst_col = dst - jnp.where(dst >= 64, 64, 0)
    for dx in range(3):
        r["pick1"][:, dx * 128 : (dx + 1) * 128] = jnp.where(
            same & (src_col == 2 * dst_col + dx - 1), 1.0, 0.0
        ).astype(BF)

    state = stat_send(stat_wait(state), x_peers)
    dw_z.wait_recv()
    here = dwt.at[oz, own_piece]
    dw_y = [
        send(here, here, {"frame": x * ny + lax.rem(y + 2 * d, ny)}) for d in range(1, pieces)
    ]
    dw_x = [send(here, here, p) for p in x_peers]

    src = lax.broadcasted_iota(jnp.int32, (256, 256), 0)
    dst = lax.broadcasted_iota(jnp.int32, (256, 256), 1)
    second = dst >= 128
    lane = dst - jnp.where(second, 128, 0)
    upper = lane >= 64
    col = lane - jnp.where(upper, 64, 0)
    base = jnp.where(second, 128, 64) + jnp.where(upper, 64, 0)
    for dx in range(3):
        want = col + (dx - 1)
        keep = (want >= 0) & (want < W2) & (src == base + want)
        r["pick2"][dx] = jnp.where(keep, 1.0, 0.0).astype(BF)
    loads["cw2"].wait()
    loads["sw2"].wait()
    for t in range(9):
        w2t[:, t * C1 : (t + 1) * C1] = r["cw2_v"][t * Q2 : (t + 1) * Q2, :]
    w2t[:, 9 * C1 : 10 * C1] = r["sw2_v"][...]
    y_fwd = []

    def forward(i):
        z_copies[i].wait_recv()
        y_fwd.append(to_frames(raw1, oz, *CHUNKS[i]))

    forward(0)
    state = stat_send(stat_wait(state), y_peers)
    for d in range(1, pieces):
        dw_y[d - 1].wait_recv()
        start = x * DPART + lax.rem(y // 2 + pieces - d, pieces) * piece
        there = dwt.at[oz, pl.ds(pl.multiple_of(start, 16), piece)]
        dw_x += [send(there, there, p) for p in x_peers]
    forward(1)
    loads["tw2"].wait()
    for slot, core in ((0, k), (1, ok)):
        prepare(r["tw2_v"], r["tmp2"], C2, Q2, core)
        w4t[slot] = r["tmp2"][pl.ds(pl.multiple_of(c * Q2, 16), Q2), :]
    par_copy.wait_recv()
    par_k = send(par.at[0], par.at[1], kp)
    cols = [to_columns(par[0, z]) for z in range(2)]
    cols2 = to_columns(r["par2"][...])
    bias = jnp.where(zh == 0, cols[0][0:Q2, 4:5], cols[1][0:Q2, 4:5])
    total = stat_wait(state)
    affine1 = [
        scale_columns(
            total,
            float(C1 // GROUPS * H1 * W1 * frames),
            q1_iota + (2 * z + k) * Q1,
            C1 // GROUPS,
            cols[z][0:Q1, 0:1],
            cols[z][0:Q1, 1:2],
        )
        for z in range(2)
    ]
    hid1 = r["hid1"]
    alive = {0: f > 0, 2: f < frames - 1}

    def pick(pair, z):
        return [jnp.where(z == 0, pair[0][i], pair[1][i]) for i in range(2)]

    def hidden(raw, hid, z, affine, a, n, waits):
        span = slice(a, a + n)
        scale, shift = pick(affine, z)
        for tap in (1, 0, 2):
            if tap != 1:
                waits[tap // 2].wait_recv()
            value = silu_of_half(raw[tap, z, :, span].astype(F32) * scale + shift)
            if tap != 1:
                value = jnp.where(alive[tap], value, 0.0)
            hid[0, tap, z, :, span] = value.astype(BF)
        return send(hid.at[0, :, z, :, pl.ds(a, n)], hid.at[1, :, z, :, pl.ds(a, n)], kp)

    blk, taps1 = r["blk"], r["taps1"]
    part, part_rx, red = r["part"], r["part_rx"], r["red"]
    half = C1 // 2
    k1, part_k, red_z, red_k = {}, {}, {}, {}

    def hid_own(i):
        k1[i] = [hidden(raw1, hid1, zh, affine1, *CHUNKS[i], y_own[i])]

    def hid_other(i):
        k1[i].append(hidden(raw1, hid1, oz, affine1, *CHUNKS[i], y_fwd[i]))

    def first_conv(i):
        a, n = CHUNKS[i]
        span = slice(a, a + n)
        for copy in k1[i]:
            copy.wait_recv()
        mixed = sum(
            dot(w1t[slot], hid1[slot, :, :, :, span].reshape(6 * Q1, n)) for slot in range(2)
        ).astype(BF)
        value = raw1[1, :, :, span].reshape(2 * Q1, n).astype(F32) + mixed.astype(F32)
        if i == 0:
            blk[:, 0:W1] = jnp.where(zh == 0, 0.0, value[:, 0:W1]).astype(BF)
            blk[:, W1:n] = value[:, W1:].astype(BF)
        else:
            blk[:, span] = value.astype(BF)
        at = slice(i * 128, (i + 1) * 128)
        for dy in range(3):
            top = (4 * i + dy) * W1
            pair = jnp.concatenate(
                [blk[:, top : top + W1], blk[:, top + 2 * W1 : top + 3 * W1]], axis=1
            )
            got = dot(pair, r["pick1"][...]).astype(BF)
            for dx in range(3):
                t = 3 * dy + dx
                for z in range(2):
                    taps1[z, t * Q1 : (t + 1) * Q1, at] = got[
                        z * Q1 : (z + 1) * Q1, dx * 128 : (dx + 1) * 128
                    ]

    def down(i):
        at = slice(i * 128, (i + 1) * 128)
        part[:, at] = sum(
            lax.dot_general(
                dwt[z, 0 : 9 * Q1, :],
                taps1[z, :, at],
                (((0,), (0,)), ((), ())),
                preferred_element_type=F32,
            )
            for z in range(2)
        )
        part_k[i] = send(
            part.at[pl.ds(pl.multiple_of(ok * half, 16), half), pl.ds(i * 128, 128)],
            part_rx.at[:, pl.ds(i * 128, 128)],
            kp,
        )

    def reduced(i):
        at = slice(i * 128, (i + 1) * 128)
        part_k[i].wait_recv()
        mine = part[pl.ds(pl.multiple_of(k * half, 16), half), at]
        red[k, zh, :, at] = (mine + part_rx[:, at]).astype(BF)
        here = red.at[k, zh, :, pl.ds(i * 128, 128)]
        red_z[i] = send(here, here, zp)
        red_k[i] = [send(here, here, kp)]

    def pass_reduced(i):
        red_z[i].wait_recv()
        here = red.at[k, oz, :, pl.ds(i * 128, 128)]
        red_k[i].append(send(here, here, kp))

    hid_own(0)
    hid_other(0)
    hid_own(1)
    forward(2)
    first_conv(0)
    hid_other(1)
    hid_own(2)
    first_conv(1)
    for copy in dw_x:
        copy.wait_recv()
    down(0)
    down(1)
    hid_other(2)
    reduced(0)
    reduced(1)
    first_conv(2)
    down(2)
    reduced(2)
    for i in range(3):
        pass_reduced(i)
    for i in range(3):
        for copy in red_k[i]:
            copy.wait_recv()

    nrm = r["nrm"]
    nrm[:, 0:128] = jnp.zeros((C1, 128), BF)
    nrm[:, 128 + POS2 :] = jnp.zeros((C1, 128), BF)
    half_iota = lax.broadcasted_iota(jnp.int32, (half, 1), 0)
    for core in range(2):
        sides = [red[core, z] for z in range(2)]
        wide = jnp.concatenate(sides, axis=1).astype(F32)
        chan = half_iota + core * half
        row2 = group_row(
            jnp.sum(wide, axis=1, keepdims=True),
            jnp.sum(wide * wide, axis=1, keepdims=True),
            chan,
            C1 // GROUPS,
        )
        span = slice(core * half, (core + 1) * half)
        scale, shift = scale_columns(
            row2, float(C1 // GROUPS * POS2), chan, C1 // GROUPS, cols2[span, 0:1], cols2[span, 1:2]
        )
        nrm[span, 128 : 128 + POS2] = silu_of_half(wide * scale + shift).astype(BF)

    def second(side, taps):
        for dx in range(3):
            for j in range(TILES + 1):
                window = nrm[:, side * HALF2 + j * 128 : side * HALF2 + j * 128 + 256]
                got = dot(window, r["pick2"][dx]).astype(BF)
                if j < TILES:
                    at = slice(j * 128, (j + 1) * 128)
                    taps[dx * C1 : (dx + 1) * C1, at] = got[:, 0:128]
                    taps[(3 + dx) * C1 : (4 + dx) * C1, at] = got[:, 128:256]
                if j > 0:
                    at = slice((j - 1) * 128, j * 128)
                    taps[(6 + dx) * C1 : (7 + dx) * C1, at] = got[:, 0:128]
        for core in range(2):
            taps[9 * C1 + core * half : 9 * C1 + (core + 1) * half, :] = red[core, side]

    own = raw2.at[0]
    z2 = []

    def to_other(a, n):
        here = own.at[1, zh, :, pl.ds(a, n)]
        z2.append(send(here, here, zp))

    raw_k = {a: [] for a, n in CHUNKS2}
    y2_own = []

    def share(tap, z, a, n):
        here = pl.ds(a, n)
        raw_k[a].append(send(raw2.at[0, tap, z, :, here], raw2.at[1, tap, z, :, here], kp))

    for side in range(2):
        second(side, r["taps2"])
        at = slice(side * HALF2, (side + 1) * HALF2)
        raw2[0, 1, zh, :, at] = (dot(w2t[...], r["taps2"][...]) + bias).astype(BF)
        for a, n in CHUNKS2[:1] if side == 0 else CHUNKS2[1:]:
            to_other(a, n)
        y2_own.append(to_frames(own, zh, side * HALF2, HALF2))
        share(1, zh, side * HALF2, HALF2)
    wide = raw2[0, 1, zh].astype(F32)
    q2_iota = lax.broadcasted_iota(jnp.int32, (Q2, 1), 0)
    row3 = group_row(
        jnp.sum(wide, axis=1, keepdims=True),
        jnp.sum(wide * wide, axis=1, keepdims=True),
        q2_iota + c * Q2,
        C2 // GROUPS,
    )
    state = stat_send(row3, x_peers)
    par_k.wait_recv()
    cols3 = [cols, [to_columns(par[1, z]) for z in range(2)]]
    y2_fwd = []

    def forward2(i):
        z2[i].wait_recv()
        y2_fwd.append(to_frames(own, oz, *CHUNKS2[i]))
        share(1, oz, *CHUNKS2[i])

    def arrived(i):
        for tap in (0, 2):
            y2_fwd[i][tap // 2].wait_recv()
            share(tap, oz, *CHUNKS2[i])

    state = stat_send(stat_wait(state), y_peers)
    forward2(0)
    for side in range(2):
        for tap in (0, 2):
            y2_own[side][tap // 2].wait_recv()
            share(tap, zh, side * HALF2, HALF2)
    state = stat_send(stat_wait(state), chan_peers)
    forward2(1)
    forward2(2)
    for i in range(3):
        arrived(i)
    total = stat_wait(state)
    affine3 = [
        [
            scale_columns(
                total,
                float(C2 // GROUPS * POS2 * frames),
                q2_iota + (2 * z + core) * Q2,
                C2 // GROUPS,
                cols3[slot][z][0:Q2, 2:3],
                cols3[slot][z][0:Q2, 3:4],
            )
            for z in range(2)
        ]
        for slot, core in ((0, k), (1, ok))
    ]
    hid2, fin = r["hid2"], r["fin"]
    stores = []
    for a, n in CHUNKS2:
        at = slice(a, a + n)
        for slot in range(2):
            if slot == 1:
                for copy in raw_k[a]:
                    copy.wait_recv()
            for z in range(2):
                scale, shift = affine3[slot][z]
                for tap in range(3):
                    value = silu_of_half(raw2[slot, tap, z, :, at].astype(F32) * scale + shift)
                    if tap != 1:
                        value = jnp.where(alive[tap], value, 0.0)
                    hid2[slot, tap, z, :, at] = value.astype(BF)
        mixed = sum(
            dot(w4t[slot], hid2[slot, :, :, :, at].reshape(6 * Q2, n)) for slot in range(2)
        ).astype(BF)
        fin[:, at] = (raw2[0, 1, zh, :, at].astype(F32) + mixed.astype(F32)).astype(BF)
        here = pl.ds(a, n)
        stores.append(
            pltpu.make_async_copy(fin.at[:, here], out.at[:, here], local_sem.at[13 + len(stores)])
        )
        stores[-1].start()
    for copy in stores:
        copy.wait()
    for copy in sent:
        copy.wait_send()


def per_device(frames, lat, tw1, g1, s1, dw, g2, s2, cw2, sw2, tb, tw2, g3, s3):
    far = pl.BlockSpec(memory_space=pl.ANY)
    row = lambda v: v.reshape(1, v.shape[0])
    result = pl.pallas_call(
        functools.partial(kernel, frames),
        out_shape=jax.ShapeDtypeStruct((Q2, POS2), BF),
        in_specs=[far] * 13,
        out_specs=far,
        scratch_shapes=[pltpu.VMEM(shape, dtype) for shape, dtype in SCRATCH.values()]
        + [
            pltpu.SemaphoreType.DMA((N_SEM,)),
            pltpu.SemaphoreType.DMA((N_SEM,)),
            pltpu.SemaphoreType.DMA((16,)),
        ],
        compiler_params=pltpu.CompilerParams(
            collective_id=0, has_side_effects=True, vmem_limit_bytes=56 * 2**20
        ),
        name="video_block",
    )(
        lat.reshape(Q1, H1 * W1),
        tw1.reshape(3 * C1, C1),
        row(g1),
        row(s1),
        dw.reshape(9 * Q1, C1),
        g2,
        s2,
        cw2.transpose(0, 2, 1).reshape(9 * Q2, C1),
        sw2.T,
        row(tb),
        tw2.reshape(3 * C2, C2),
        row(g3),
        row(s3),
    )
    return result.reshape(1, Q2, POS2)


def solution(mesh):
    return jax.shard_map(
        functools.partial(per_device, mesh.shape["frame"]),
        mesh=mesh,
        in_specs=(
            P(("video", "frame"), "chan", None),
            P(),
            P("chan"),
            P("chan"),
            P(None, "chan", None),
            P(),
            P(),
            P(None, None, "chan"),
            P(None, "chan"),
            P("chan"),
            P(),
            P("chan"),
            P("chan"),
        ),
        out_specs=P(("video", "frame"), "chan", None),
        check_vma=False,
    )
```
